768 devices in a mesh: lat: 96 (over x, z, core), lon: 8 (over y).
Axes of the slice: x: 4, y: 8, z: 12, core: 2. Of those that a mesh axis runs over, the one named last changes fastest.
Arguments:
- departures: float32 [196608, 128], P(('lat', 'lon')), may hold values from -6 to 6
- obs_weight: float32 [196608, 128], P(('lat', 'lon')), may hold values from 0.2 to 4
- obs_columns: int32 [196608], P(('lat', 'lon')), may hold values from 0 to 127
- obs_owner: int32 [196608, 1], P(('lat', 'lon')), may hold values from 0 to 7; in each aligned block of 256 rows (0 to 255, 256 to 511, ...) at most 64 rows name the same one
- obs_counts: int32 [768], P(('lat', 'lon')), may hold values from 128 to 256
- background_std: float32 [768, 128, 128], P('lat', 'lon'), may hold values from 0.5 to 2
- diffusion: float32 [768, 128], P('lat', 'lon'), may hold values from 0.15 to 0.45
- level_factor: float32 [128, 128], replicated, may hold values from -0.5 to 0.5
- model_mixing: float32 [128, 128], replicated, may hold values from -0.5 to 0.5
Outputs:
- solution: float32 [768, 128, 128], P('lat', 'lon')
- residual: float32 [768, 128, 128], P('lat', 'lon')
The draws below stay inside these ranges and needn't reach their ends.
Inputs may be any that keep to these rules, and one draw needn't show every extreme that they name: `obs_owner`: among the 256 rows of one shard no tile is named by more than 64 rows.
All inputs are finite; a program needn't handle non-finite values.
Results may differ from the reference program's by a relative error of at most 0.025.
Values sent between devices are 32-bit elements; how exact they have to be, the bound alone decides.
No kernel may reach another device: no remote copies, remote signals or barrier semaphores. Data moves between devices by JAX's collectives and lax.ppermute only.
A program may use at most 32 MiB of HBM per device.

```python
import math
import jax
import jax.numpy as jnp
import numpy as np
from jax import lax

L = 128
CLAT = 8
CLON = 16
NOBS = 256
STEPS = 3
ITERS = 2
CAP = 64
NLAT = 768
NLON = 128
TILES = 768
NOBS_ALL = 196608
N_LON = 8


def draw_obs_counts(key, part):
    key = jax.random.fold_in(key, 11)
    first_key, second_key = jax.random.split(key)
    counts = jax.random.randint(first_key, (TILES,), NOBS // 2, NOBS + 1)
    where_full = jax.random.randint(second_key, (), 0, TILES)
    return counts.at[where_full].set(NOBS).astype(jnp.int32)


def set_ends(values, key, smallest, high):
    shape = values.shape
    place = [jax.random.randint(jax.random.fold_in(key, axis), (), 0, shape[axis]) for axis in range(len(shape))]
    values = values.at[tuple(place)].set(smallest)
    longest = shape.index(max(shape))
    place[longest] = (place[longest] + 1) % shape[longest]
    return values.at[tuple(place)].set(high)


def steps_of(stream_key, extent, shards, smallest, largest):
    def one(dim, blocks):
        draws = jax.random.uniform(jax.random.fold_in(jax.random.fold_in(stream_key, 6), dim), (blocks,), jnp.float32, smallest / len(shards), largest / len(shards))
        return jnp.repeat(jnp.exp(draws), extent[dim] // blocks).reshape((-1,) + (1,) * (len(extent) - dim - 1))

    level = one(*shards[0])
    for cut in shards[1:]:
        level = level * one(*cut)
    return level


def assign_block(key, own, number, rows, number_of, top, most, slope):
    ranking = jax.random.permutation(key, number_of)
    crowded, ordinary = shares(number_of, rows * top, most, slope, True), shares(number_of, rows * top, most, slope, False)
    places = jnp.arange(number_of)

    def named(tallies, offset_by):
        used = int((tallies > 0).sum())
        fixed = max(1, used // 4)
        moved = fixed + (places - fixed + offset_by * (used - fixed)) % max(1, number_of - fixed)
        return jnp.zeros((number_of,), jnp.int32).at[ranking[jnp.where(places < fixed, places, moved)]].set(jnp.asarray(tallies, jnp.int32))

    tallies = jnp.where(number % 4 == 0, named(crowded, number // 4), named(ordinary, number - number // 4 - 1))
    mixed = jax.random.permutation(jax.random.fold_in(own, 3), number_of)
    source_of, receiver = mixed[0:number_of // 2 * 2:2], mixed[1:number_of // 2 * 2:2]
    margin = jnp.minimum(tallies[source_of] - 1, most - tallies[receiver]) // 2
    margin = jnp.where((source_of == ranking[0]) | (receiver == ranking[0]) | (tallies[receiver] == 0), 0, jnp.maximum(margin, 0))
    moved = jax.random.randint(jax.random.fold_in(own, 4), (number_of // 2,), 0, 1 << 20) % (margin + 1)
    tallies = tallies.at[source_of].add(-moved).at[receiver].add(moved)
    items = jnp.searchsorted(jnp.cumsum(tallies), jnp.arange(rows * top), side="right").astype(jnp.int32)
    grid = items.reshape(top, rows).T
    grid = grid[jax.random.permutation(jax.random.fold_in(own, 1), rows)]
    offset_by = jax.random.randint(jax.random.fold_in(own, 2), (rows, 1), 0, top)
    return jnp.take_along_axis(grid, (jnp.arange(top)[None, :] + offset_by) % top, axis=1)


def shares(count, total, bound, skew, full):
    loads = [(1 << 20) // math.isqrt(rank ** skew) + 1 for rank in range(1, count + 1)]
    largest = bound if full else min(bound, max(-(-total // count), total * loads[0] // sum(loads)))
    least = 1 if total - largest >= count - 1 else 0
    holding, spare = [largest] + [least] * (count - 1), total - largest - least * (count - 1)
    while spare > 0:
        movable = [i for i in range(1, count) if holding[i] < largest] or [i for i in range(1, count) if holding[i] < bound]
        whole, left = sum([loads[i] for i in movable]), spare
        for i in movable:
            extra = min(bound - holding[i], max(1, left * loads[i] // whole), spare)
            holding[i] = holding[i] + extra
            spare = spare - extra
    return np.array(holding)


def normal_values(rng, dims, spread, most, cuts=(), kind=jnp.bfloat16):
    result = spread * jax.random.normal(rng, dims, jnp.float32)
    if cuts:
        result = result * steps_of(rng, dims, cuts, -0.22, 0.18)
    return jnp.clip(result, -most, most).astype(kind)


def setup_inputs(seed: int = 0) -> dict:
    seeds = jax.random.split(jax.random.key(seed), 10)
    departures = normal_values(seeds[0], (NOBS_ALL, L), 1.0, 6.0, ((0, 768),), jnp.float32)
    obs_weight = jnp.clip(jnp.exp(math.log(4.0) - 2.9957323 * jax.random.uniform(seeds[1], (NOBS_ALL, L), jnp.float32) ** steps_of(seeds[1], (NOBS_ALL, L), ((0, 768),), -0.2, 0.2)), 0.2, 4.0)
    obs_columns = set_ends(jax.random.randint(seeds[2], (NOBS_ALL,), 0, CLAT * CLON), jax.random.fold_in(seeds[2], 1), 0, (CLAT * CLON) - 1).astype(jnp.int32)
    obs_owner_keys = jax.random.split(jax.random.fold_in(seeds[3], 1), NOBS_ALL // NOBS)
    obs_owner_turns = jax.random.permutation(jax.random.fold_in(seeds[3], 3), NOBS_ALL // NOBS)
    obs_owner = jax.vmap(lambda own, number: assign_block(jax.random.fold_in(seeds[3], 2), own, number, NOBS, N_LON, 1, CAP, 2))(obs_owner_keys, obs_owner_turns).reshape((NOBS_ALL, 1))
    obs_counts = draw_obs_counts(jax.random.fold_in(seeds[9], 71), 0)
    background_std = jnp.clip(jnp.exp(math.log(2.0) - 1.3862944 * jax.random.uniform(seeds[5], (NLAT, NLON, L), jnp.float32) ** steps_of(seeds[5], (NLAT, NLON, L), ((0, 96), (1, 8)), -0.2, 0.2)), 0.5, 2.0)
    diffusion = jnp.clip(jnp.exp(math.log(0.45) - 1.0986122 * jax.random.uniform(seeds[6], (NLAT, NLON), jnp.float32) ** steps_of(seeds[6], (NLAT, NLON), ((0, 96), (1, 8)), -0.2, 0.2)), 0.15, 0.45)
    level_factor = normal_values(seeds[7], (L, L), L ** -0.5, 0.5, (), jnp.float32)
    model_mixing = normal_values(seeds[8], (L, L), L ** -0.5, 0.5, (), jnp.float32)
    return dict(departures=departures, obs_weight=obs_weight, obs_columns=obs_columns, obs_owner=obs_owner, obs_counts=obs_counts, background_std=background_std, diffusion=diffusion, level_factor=level_factor, model_mixing=model_mixing)


HIGH = lax.Precision.HIGHEST


def level_mix(field, matrix):
    return jnp.einsum("abl,lm->abm", field, matrix, precision=HIGH)


def level_mix_t(field, matrix):
    return jnp.einsum("abl,ml->abm", field, matrix, precision=HIGH)


def smooth(field, diffusion):
    scaled = diffusion[:, :, None] * field
    padded = jnp.pad(scaled, ((1, 1), (0, 0), (0, 0)))
    padded = jnp.concatenate([padded[:, -1:], padded, padded[:, :1]], axis=1)
    centre = padded[1:-1, 1:-1]
    laplace = padded[:-2, 1:-1] + padded[2:, 1:-1] + padded[1:-1, :-2] + padded[1:-1, 2:] - 4.0 * centre
    return field + diffusion[:, :, None] * laplace


def forward(control, background_std, diffusion, level_factor, model_mixing):
    current = background_std * (control + 0.5 * level_mix(control, level_factor))
    states = []
    for section in range(STEPS):
        smoothed = smooth(current, diffusion)
        current = smoothed + 0.5 * level_mix(smoothed, model_mixing)
        states.append(current)
    return states


def backward(forcings, background_std, diffusion, level_factor, model_mixing):
    adjoint = forcings[STEPS - 1]
    for section in range(STEPS - 1, -1, -1):
        adjoint = smooth(adjoint + 0.5 * level_mix_t(adjoint, model_mixing), diffusion)
        if section > 0:
            adjoint = adjoint + forcings[section - 1]
    scaled = background_std * adjoint
    return scaled + 0.5 * level_mix_t(scaled, level_factor)


def reference(departures, obs_weight, obs_columns, obs_owner, obs_counts, background_std, diffusion, level_factor, model_mixing):
    total = obs_columns.shape[0]
    obs_index = jnp.arange(total, dtype=jnp.int32)
    shard_index = obs_index // NOBS
    slot_index = obs_index % NOBS
    is_used = (slot_index < obs_counts[shard_index]).astype(jnp.float32)
    obs_time = slot_index % STEPS
    grid_row = (shard_index // N_LON) * CLAT + obs_columns // CLON
    grid_col = obs_owner[:, 0] * CLON + obs_columns % CLON
    row_index = obs_time * (NLAT * NLON) + grid_row * NLON + grid_col
    weights = obs_weight * is_used[:, None]
    levels = background_std.shape[2]

    def spread_forcing(values):
        forcing_rows = jnp.zeros((STEPS * NLAT * NLON, levels), jnp.float32).at[row_index].add(values)
        forcing_rows = forcing_rows.reshape(STEPS, NLAT, NLON, levels)
        return [forcing_rows[section] for section in range(STEPS)]

    def hessian(vector):
        states = forward(vector, background_std, diffusion, level_factor, model_mixing)
        stacked = jnp.stack(states, axis=0).reshape(STEPS * NLAT * NLON, levels)
        sampled = stacked[row_index]
        forcings = spread_forcing(weights * sampled)
        return vector + backward(forcings, background_std, diffusion, level_factor, model_mixing)

    right_side = backward(spread_forcing(weights * departures), background_std, diffusion, level_factor, model_mixing)
    solution = jnp.zeros_like(right_side)
    residual = right_side
    direction = right_side
    norm_now = jnp.sum(residual * residual)
    for section in range(ITERS):
        hess_dir = hessian(direction)
        step_size = norm_now / jnp.sum(direction * hess_dir)
        solution = solution + step_size * direction
        residual = residual - step_size * hess_dir
        if section + 1 < ITERS:
            norm_next = jnp.sum(residual * residual)
            direction = residual + (norm_next / norm_now) * direction
            norm_now = norm_next
    return solution, residual
```

```python
import functools
import jax
import jax.numpy as jnp
from jax import lax
from jax.experimental import pallas as pl
from jax.experimental.pallas import tpu as pltpu
from jax.sharding import PartitionSpec as P

F32 = jnp.float32
BF16 = jnp.bfloat16
L = 128
ROWS = 8
COLS = 16
CELLS = ROWS * COLS
STEPS = 3
SLOTS = 256
CAP = 64
WIDE = 3 * COLS
HALO = 2 * STEPS
BUCKET = 2 * CAP + 8
TILE_ROWS = 2 * STEPS * CELLS + CELLS + COLS
SIDE = 13

PARAMS = pltpu.CompilerParams(vmem_limit_bytes=40 * 1024 * 1024)


def call(kernel, name, outs, scratch=(), smem=()):
    def run(*args):
        specs = [
            pl.BlockSpec(memory_space=pltpu.SMEM if i in smem else pltpu.VMEM) for i in range(len(args))
        ]
        return pl.pallas_call(
            kernel,
            name=name,
            out_shape=outs,
            in_specs=specs,
            out_specs=jax.tree.map(lambda _: pl.BlockSpec(memory_space=pltpu.VMEM), outs),
            scratch_shapes=scratch,
            compiler_params=PARAMS,
        )(*args)

    return run


def shape(*dims, dtype=F32):
    return jax.ShapeDtypeStruct(dims, dtype)


def halves(x):
    high = x.astype(BF16)
    return high, (x - high.astype(F32)).astype(BF16)


def dot(a, b):
    return jnp.dot(a, b, preferred_element_type=F32)


def matrices_kernel(factor_ref, mixing_ref, out_ref):
    for i, ref in enumerate((mixing_ref, factor_ref)):
        for j in range(2):
            m = 0.5 * ref[...]
            high, low = halves(m.T if j else m)
            row = jnp.concatenate([high, low], axis=1)
            out_ref[2 * i + j] = jnp.concatenate([row, row], axis=0)


MIX, MIX_T, FACTOR, FACTOR_T = range(4)


def bucket_kernel(departures_ref, weight_ref, columns_ref, owner_ref, counts_ref, parity_ref, out_ref):
    sub = lax.broadcasted_iota(jnp.int32, (SLOTS, SLOTS), 0)
    lane = lax.broadcasted_iota(jnp.int32, (SLOTS, SLOTS), 1)
    owner_row = owner_ref[...].astype(F32)
    owner_col = jnp.sum(jnp.where(sub == lane, owner_row, 0.0), axis=1, keepdims=True)
    same = owner_row == owner_col
    rank_row = jnp.sum(jnp.where(same & (sub < lane), 1.0, 0.0), axis=0, keepdims=True)
    rank_col = jnp.sum(jnp.where(same & (lane < sub), 1.0, 0.0), axis=1, keepdims=True)
    place = (owner_row * CAP + rank_row).astype(jnp.int32)
    pick = lax.broadcasted_iota(jnp.int32, (8 * CAP, SLOTS), 0) == place
    pick = jnp.where(pick, 1.0, 0.0).astype(BF16)
    slot = lax.broadcasted_iota(jnp.int32, (SLOTS, L), 0)
    weights = jnp.where(slot < counts_ref[0], weight_ref[...], 0.0)
    parts = halves(weights * departures_ref[...]) + halves(weights)
    moved = dot(pick, jnp.concatenate(parts, axis=1))
    forcing = moved[:, :L] + moved[:, L : 2 * L]
    weights = moved[:, 2 * L : 3 * L] + moved[:, 3 * L :]
    number = lax.broadcasted_iota(jnp.int32, (1, SLOTS), 1)
    time = (number - STEPS * ((number * 171) >> 9)).astype(F32)
    tile = lax.broadcasted_iota(jnp.int32, (8, SLOTS), 0).astype(F32)
    here = tile == owner_row
    marks = jnp.concatenate(
        [jnp.where(here, time, 0.0), jnp.where(here, columns_ref[...].astype(F32), 0.0)], axis=0
    )
    target = rank_col + (CAP * parity_ref[0]).astype(F32)
    spread = jnp.where(lax.broadcasted_iota(jnp.int32, (SLOTS, L), 1).astype(F32) == target, 1.0, 0.0)
    codes = dot(marks.astype(BF16), spread.astype(BF16))
    codes = CELLS * codes[:8] + codes[8:]
    for d in range(8):
        out_ref[d, :CAP] = forcing[d * CAP : (d + 1) * CAP]
        out_ref[d, CAP : 2 * CAP] = weights[d * CAP : (d + 1) * CAP]
        out_ref[d, 2 * CAP :] = jnp.broadcast_to(codes[d : d + 1], (8, L))


def tile_kernel(received_ref, std_ref, diffusion_ref, out_ref):
    ones, data = [], []
    cell = lax.broadcasted_iota(jnp.int32, (STEPS * CELLS, L), 0)
    for j in range(4):
        pair = (2 * j, 2 * j + 1)
        codes = sum(received_ref[s, 2 * CAP : 2 * CAP + 1] for s in pair).astype(jnp.int32)
        ones.append(jnp.where(cell == codes, 1.0, 0.0).astype(BF16))
        for s in pair:
            parts = halves(received_ref[s, :CAP]) + halves(received_ref[s, CAP : 2 * CAP])
            data.append(jnp.concatenate(parts, axis=1))
    total = dot(jnp.concatenate(ones, axis=1), jnp.concatenate(data, axis=0))
    size = STEPS * CELLS
    out_ref[:size] = total[:, :L] + total[:, L : 2 * L]
    out_ref[size : 2 * size] = total[:, 2 * L : 3 * L] + total[:, 3 * L :]
    out_ref[2 * size : 2 * size + CELLS] = std_ref[...]
    sub = lax.broadcasted_iota(jnp.int32, (COLS, L), 0)
    lane = lax.broadcasted_iota(jnp.int32, (COLS, L), 1)
    turned = jnp.zeros((COLS, L), F32)
    for r in range(ROWS):
        row = diffusion_ref[r : r + 1]
        column = jnp.sum(jnp.where(sub == lane, row, 0.0), axis=1, keepdims=True)
        turned = turned + jnp.where(lane == r, column, 0.0)
    out_ref[2 * size + CELLS :] = turned


def wide(refs, start):
    return jnp.concatenate([ref[start : start + COLS] for ref in refs], axis=0)


def forcing_row(refs, t, r):
    return wide(refs, t * CELLS + r * COLS)


def weight_row(refs, t, r):
    return wide(refs, (STEPS + t) * CELLS + r * COLS)


def std_row(refs, r):
    return wide(refs, 2 * STEPS * CELLS + r * COLS)


def turned_row(refs):
    return wide(refs, 2 * STEPS * CELLS + CELLS)


def side_index(kind, t, k):
    return 6 * kind + (0, 3, 5)[2 - t] + k


def sides_kernel(left_ref, own_ref, right_ref, low_ref, high_ref):
    refs = (left_ref, own_ref, right_ref)
    for kind, row in enumerate((forcing_row, weight_row)):
        for t in range(STEPS):
            for k in range(t + 1):
                at = side_index(kind, t, k) * WIDE
                low_ref[at : at + WIDE] = row(refs, t, k)
                high_ref[at : at + WIDE] = row(refs, t, ROWS - 1 - t + k)
    last = (SIDE - 1) * WIDE
    low_ref[last:] = turned_row(refs)
    high_ref[last:] = turned_row(refs)


def side_or_own(refs, below_ref, above_ref, kind, t, r):
    if 0 <= r < ROWS:
        return (forcing_row, weight_row)[kind](refs, t, r)
    ref, k = (below_ref, r + t + 1) if r < 0 else (above_ref, r - ROWS)
    at = side_index(kind, t, k) * WIDE
    return ref[at : at + WIDE]


def fill_diffusion(refs, below_ref, above_ref, d_ref, first, stop):
    last = (SIDE - 1) * WIDE
    own, below, above = turned_row(refs), below_ref[last:], above_ref[last:]
    for r in range(first, stop):
        source = below if r < 0 else above if r >= ROWS else own
        column = source[:, r % ROWS : r % ROWS + 1]
        at = (r + HALO) * WIDE
        d_ref[at : at + WIDE] = jnp.broadcast_to(column, (WIDE, L))


def at(r):
    return pl.ds((r + HALO) * WIDE, WIDE)


def smooth_rows(first, stop, get, d_ref, put):
    held = []
    for r in range(first, stop):
        value, d = get(r), d_ref[at(r)]
        held.append((value, d, d * value))
        if len(held) == 3:
            value, d, u = held[1]
            laplace = held[0][2] + held[2][2] + pltpu.roll(u, 1, 0) + pltpu.roll(u, WIDE - 1, 0) - 4.0 * u
            put(r - 1, value + d * laplace)
            held.pop(0)


class Field:
    def __init__(self, v_ref, x_ref, y_ref, m_ref):
        self.v_ref, self.x_ref, self.y_ref, self.m_ref = v_ref, x_ref, y_ref, m_ref

    def put(self, r, value):
        self.v_ref[at(r)] = value
        high, low = halves(value)
        self.x_ref[at(r), :L] = high
        self.x_ref[at(r), L:] = low

    def mix(self, first, stop, which):
        rows = pl.ds((first + HALO) * WIDE, (stop - first) * WIDE)
        self.y_ref[rows] = dot(self.x_ref[rows], self.m_ref[which])

    def get(self, r):
        return self.v_ref[at(r)] + self.y_ref[at(r), :L] + self.y_ref[at(r), L:]


def adjoint(field, d_ref, forcing, std):
    for t in range(STEPS - 1, -1, -1):
        field.mix(-t - 1, ROWS + t + 1, MIX_T)
        if t > 0:
            put = lambda r, value, t=t: field.put(r, value + forcing(t - 1, r))
        else:
            put = lambda r, value: field.put(r, std(r) * value)
        smooth_rows(-t - 1, ROWS + t + 1, field.get, d_ref, put)
    field.mix(0, ROWS, FACTOR_T)


def right_side_kernel(
    left_ref, own_ref, right_ref, below_ref, above_ref, m_ref, b_ref, y_ref, low_ref, high_ref,
    v_ref, x_ref, p_ref, d_ref,
):
    refs = (left_ref, own_ref, right_ref)
    fill_diffusion(refs, below_ref, above_ref, d_ref, -STEPS, ROWS + STEPS)
    field = Field(v_ref, x_ref, p_ref, m_ref)
    forcing = lambda t, r: side_or_own(refs, below_ref, above_ref, 0, t, r)
    std = lambda r: std_row(refs, r)
    for r in range(-STEPS, ROWS + STEPS):
        field.put(r, forcing(STEPS - 1, r))
    adjoint(field, d_ref, forcing, std)
    for r in range(ROWS):
        value = field.get(r)
        b_ref[r] = value
        field.put(r, value)
    send_states(field, std, y_ref, low_ref, high_ref, slice(None))


def send_states(field, std, y_ref, low_ref, high_ref, columns):
    field.mix(0, ROWS, FACTOR)
    for r in range(ROWS):
        state = (std(r) * field.get(r))[columns]
        y_ref[r] = state
        if r < HALO:
            low_ref[r] = state
        if r >= ROWS - HALO:
            high_ref[r - (ROWS - HALO)] = state


def image(field, d_ref, weights, std, start, tops):
    smooth_rows(-HALO, ROWS + HALO, start, d_ref, field.put)
    for t in range(STEPS):
        first, stop = -HALO + t + 1, ROWS + HALO - t - 1
        field.mix(first, stop, MIX)
        if t == STEPS - 1:
            for r in range(first, stop):
                field.put(r, kept(field.get(r), weights, t, r, tops))
            break

        def get(r, t=t):
            value = field.get(r)
            if -t - 1 <= r < ROWS + t + 1:
                tops[t][at(r)] = kept(value, weights, t, r, tops)
            return value

        smooth_rows(first, stop, get, d_ref, field.put)
    adjoint(field, d_ref, lambda t, r: tops[t][at(r)], std)


def kept(value, weights, t, r, tops):
    forced = weights(t, r) * value
    if tops[2] is not None and 0 <= r < ROWS:
        own = slice(COLS, 2 * COLS)
        tops[2].append(forced[own] * value[own])
    return forced


INNER = slice(COLS // 2, WIDE - COLS // 2)
OWN = slice(COLS, 2 * COLS)


def first_image_kernel(
    left_ref, own_ref, right_ref, below_ref, above_ref, m_ref, b_ref, y_ref, south_ref, north_ref,
    q_ref, z_ref, low_ref, high_ref,
    v_ref, x_ref, p_ref, d_ref, g0_ref, g1_ref,
):
    refs = (left_ref, own_ref, right_ref)
    fill_diffusion(refs, below_ref, above_ref, d_ref, -HALO, ROWS + HALO)
    field = Field(v_ref, x_ref, p_ref, m_ref)
    weights = lambda t, r: side_or_own(refs, below_ref, above_ref, 1, t, r)
    std = lambda r: std_row(refs, r)

    def start(r):
        if r < 0:
            return south_ref[r + HALO]
        return north_ref[r - ROWS] if r >= ROWS else y_ref[r]

    image(field, d_ref, weights, std, start, (g0_ref, g1_ref, None))
    for r in range(ROWS):
        value = b_ref[r] + field.get(r)
        q_ref[r] = value[INNER]
        field.put(r, value)
    send_states(field, std, z_ref, low_ref, high_ref, INNER)


def second_image_kernel(
    left_ref, own_ref, right_ref, below_ref, above_ref, m_ref, b_ref, q_ref, y_ref, south_ref, north_ref,
    u_ref, sums_ref,
    v_ref, x_ref, p_ref, d_ref, g0_ref, g1_ref,
):
    refs = (left_ref, own_ref, right_ref)
    fill_diffusion(refs, below_ref, above_ref, d_ref, -HALO, ROWS + HALO)
    field = Field(v_ref, x_ref, p_ref, m_ref)
    weights = lambda t, r: side_or_own(refs, below_ref, above_ref, 1, t, r)
    std = lambda r: std_row(refs, r)
    edge = jnp.zeros((COLS // 2, L), F32)

    def start(r):
        state = south_ref[r + HALO] if r < 0 else north_ref[r - ROWS] if r >= ROWS else y_ref[r]
        return jnp.concatenate([edge, state, edge], axis=0)

    image(field, d_ref, weights, std, start, (g0_ref, g1_ref, None))
    sums = [jnp.zeros((COLS, L), F32) for _ in range(4)]
    middle = slice(COLS // 2, COLS // 2 + COLS)
    for r in range(ROWS):
        b, q = b_ref[r, OWN], q_ref[r, middle]
        u = q + field.get(r)[OWN]
        u_ref[r * COLS : (r + 1) * COLS] = u
        for i, term in enumerate((b * b, b * q, q * q, q * u)):
            sums[i] = sums[i] + term
    lane = lax.broadcasted_iota(jnp.int32, (1, L), 1)
    row = jnp.zeros((1, L), F32)
    for i, term in enumerate(sums):
        total = jnp.sum(jnp.sum(term, axis=0, keepdims=True), axis=1, keepdims=True)
        row = row + jnp.where(lane == i, total, 0.0)
    sums_ref[...] = jnp.broadcast_to(row, sums_ref.shape)


def add_kernel(parts_ref, out_ref):
    out_ref[...] = jnp.broadcast_to(jnp.sum(parts_ref[...], axis=0, keepdims=True), out_ref.shape)


def finish_kernel(parts_ref, b_ref, q_ref, u_ref, solution_ref, residual_ref):
    total = jnp.sum(parts_ref[...], axis=0, keepdims=True)
    bb, bq, qq, qu = (total[:, i : i + 1] for i in range(4))
    first = bb / bq
    norm = first * first * qq - bb
    gain = 1.0 + norm / bb
    curve = gain * gain * bq - 2.0 * first * gain * qq + first * first * qu
    second = norm / curve
    along_b = first + second * gain
    along_q = first * second
    middle = slice(COLS // 2, COLS // 2 + COLS)
    for r in range(ROWS):
        rows = slice(r * COLS, (r + 1) * COLS)
        b, q = b_ref[r, OWN], q_ref[r, middle]
        solution_ref[rows] = along_b * b - along_q * q
        residual_ref[rows] = b - along_b * q + along_q * u_ref[rows]


def exchange(to_before, to_after, axis, wrap):
    size = lax.axis_size(axis)
    up = [(i, (i + 1) % size) for i in range(size if wrap else size - 1)]
    down = [(j, i) for i, j in up]
    return lax.ppermute(to_after, axis, up), lax.ppermute(to_before, axis, down)


def shards(
    departures, obs_weight, obs_columns, obs_owner, obs_counts, background_std, diffusion, level_factor, model_mixing
):
    parity = (lax.axis_index("lon") % 2).astype(jnp.int32).reshape(1)
    mats = call(matrices_kernel, "matrices", shape(4, 2 * L, 2 * L, dtype=BF16))(level_factor, model_mixing)
    buckets = call(bucket_kernel, "bucket", shape(8, BUCKET, L), smem=(4, 5))(
        departures, obs_weight, obs_columns.reshape(1, SLOTS), obs_owner.reshape(1, SLOTS), obs_counts, parity
    )
    received = lax.all_to_all(buckets, "lon", 0, 0)
    own = call(tile_kernel, "tile", shape(TILE_ROWS, L))(
        received, background_std.reshape(CELLS, L), jnp.pad(diffusion, ((0, 0), (0, L - COLS)))
    )
    left, right = exchange(own, own, "lon", True)
    refs = (left, own, right)
    side = shape(SIDE * WIDE, L)
    low, high = call(sides_kernel, "sides", (side, side))(*refs)
    below, above = exchange(low, high, "lat", False)
    tall = (ROWS + 2 * HALO) * WIDE
    scratch = [
        pltpu.VMEM((tall, L), F32),
        pltpu.VMEM((tall, 2 * L), BF16),
        pltpu.VMEM((tall, 2 * L), F32),
        pltpu.VMEM((tall, L), F32),
    ]
    tops = [pltpu.VMEM((tall, L), F32)] * 2
    send = shape(HALO, WIDE, L)
    b, y, low, high = call(
        right_side_kernel, "right_side", (shape(ROWS, WIDE, L), shape(ROWS, WIDE, L), send, send), scratch
    )(*refs, below, above, mats)
    south, north = exchange(low, high, "lat", False)
    inner = 2 * COLS
    send = shape(HALO, inner, L)
    q, z, low, high = call(
        first_image_kernel, "first_image", (shape(ROWS, inner, L), shape(ROWS, inner, L), send, send), scratch + tops
    )(*refs, below, above, mats, b, y, south, north)
    south, north = exchange(low, high, "lat", False)
    lat = lax.axis_size("lat")
    u, sums = call(second_image_kernel, "second_image", (shape(CELLS, L), shape(lat, L)), scratch + tops)(
        *refs, below, above, mats, b, q, z, south, north
    )
    sums = lax.all_to_all(sums, "lat", 0, 0, tiled=True)
    sums = call(add_kernel, "add", shape(8, L))(sums)
    sums = lax.all_to_all(sums, "lon", 0, 0, tiled=True)
    out = shape(CELLS, L)
    solution, residual = call(finish_kernel, "finish", (out, out))(sums, b, q, u)
    return solution.reshape(ROWS, COLS, L), residual.reshape(ROWS, COLS, L)


def solution(mesh):
    placed = (
        P(("lat", "lon"), None),
        P(("lat", "lon"), None),
        P(("lat", "lon")),
        P(("lat", "lon"), None),
        P(("lat", "lon")),
        P("lat", "lon", None),
        P("lat", "lon"),
        P(),
        P(),
    )
    return jax.shard_map(
        shards,
        mesh=mesh,
        in_specs=placed,
        out_specs=(P("lat", "lon", None), P("lat", "lon", None)),
        check_vma=False,
    )
```

```python
import jax
import jax.numpy as jnp
from jax import lax
from jax.experimental import pallas as pl
from jax.experimental.pallas import tpu as pltpu
from jax.sharding import PartitionSpec as P

F32 = jnp.float32
BF16 = jnp.bfloat16
L = 128
ROWS = 8
COLS = 16
CELLS = ROWS * COLS
STEPS = 3
SLOTS = 256
CAP = 64
WIDE = 3 * COLS
INNER = 2 * COLS
EDGE = COLS // 2
BUCKET = 2 * CAP + 8
REACH = 3 * STEPS

MIB = 1024 * 1024


def call(kernel, name, outs, scratch=(), smem=(), hbm=(), vmem=40):
    def run(*args):
        spaces = [pltpu.SMEM if i in smem else pltpu.HBM if i in hbm else pltpu.VMEM for i in range(len(args))]
        specs = [pl.BlockSpec(memory_space=space) for space in spaces]
        return pl.pallas_call(
            kernel,
            name=name,
            out_shape=outs,
            in_specs=specs,
            out_specs=jax.tree.map(lambda _: pl.BlockSpec(memory_space=pltpu.VMEM), outs),
            scratch_shapes=scratch,
            compiler_params=pltpu.CompilerParams(vmem_limit_bytes=vmem * MIB),
        )(*args)

    return run


def shape(*dims, dtype=F32):
    return jax.ShapeDtypeStruct(dims, dtype)


def halves(x):
    high = x.astype(BF16)
    return high, (x - high.astype(F32)).astype(BF16)


def dot(a, b):
    return jnp.dot(a, b, preferred_element_type=F32)


def matrices_kernel(factor_ref, mixing_ref, out_ref):
    for i, ref in enumerate((mixing_ref, factor_ref)):
        for j in range(2):
            m = 0.5 * ref[...]
            high, low = halves(m.T if j else m)
            row = jnp.concatenate([high, low], axis=1)
            out_ref[2 * i + j] = jnp.concatenate([row, row], axis=0)


MIX, MIX_T, FACTOR, FACTOR_T = range(4)


def bucket_kernel(
    departures_hbm, weight_hbm, columns_ref, owner_ref, counts_ref, parity_ref, out_ref, departures_ref, weight_ref, sems
):
    copies = [
        pltpu.make_async_copy(departures_hbm, departures_ref, sems.at[0]),
        pltpu.make_async_copy(weight_hbm, weight_ref, sems.at[1]),
    ]
    for copy in copies:
        copy.start()
    sub = lax.broadcasted_iota(jnp.int32, (SLOTS, SLOTS), 0)
    lane = lax.broadcasted_iota(jnp.int32, (SLOTS, SLOTS), 1)
    owner_row = owner_ref[...].astype(F32)
    owner_col = jnp.sum(jnp.where(sub == lane, owner_row, 0.0), axis=1, keepdims=True)
    same = owner_row == owner_col
    rank_row = jnp.sum(jnp.where(same & (sub < lane), 1.0, 0.0), axis=0, keepdims=True)
    rank_col = jnp.sum(jnp.where(same & (lane < sub), 1.0, 0.0), axis=1, keepdims=True)
    place = (owner_row * CAP + rank_row).astype(jnp.int32)
    pick = lax.broadcasted_iota(jnp.int32, (8 * CAP, SLOTS), 0) == place
    pick = jnp.where(pick, 1.0, 0.0).astype(BF16)
    slot = lax.broadcasted_iota(jnp.int32, (SLOTS, L), 0)
    for copy in copies:
        copy.wait()
    weights = jnp.where(slot < counts_ref[0], weight_ref[...], 0.0)
    parts = halves(weights * departures_ref[...]) + halves(weights)
    moved = dot(pick, jnp.concatenate(parts, axis=1))
    forcing = moved[:, :L] + moved[:, L : 2 * L]
    weights = moved[:, 2 * L : 3 * L] + moved[:, 3 * L :]
    number = lax.broadcasted_iota(jnp.int32, (1, SLOTS), 1)
    time = (number - STEPS * ((number * 171) >> 9)).astype(F32)
    tile = lax.broadcasted_iota(jnp.int32, (8, SLOTS), 0).astype(F32)
    here = tile == owner_row
    marks = jnp.concatenate(
        [jnp.where(here, time, 0.0), jnp.where(here, columns_ref[...].astype(F32), 0.0)], axis=0
    )
    target = rank_col + (CAP * parity_ref[0]).astype(F32)
    spread = jnp.where(lax.broadcasted_iota(jnp.int32, (SLOTS, L), 1).astype(F32) == target, 1.0, 0.0)
    codes = dot(marks.astype(BF16), spread.astype(BF16))
    codes = CELLS * codes[:8] + codes[8:]
    for d in range(8):
        out_ref[d, :CAP] = forcing[d * CAP : (d + 1) * CAP]
        out_ref[d, CAP : 2 * CAP] = weights[d * CAP : (d + 1) * CAP]
        out_ref[d, 2 * CAP :] = jnp.broadcast_to(codes[d : d + 1], (8, L))


def fixed_kernel(std_ref, diffusion_ref, out_ref):
    out_ref[:CELLS] = std_ref[...]
    sub = lax.broadcasted_iota(jnp.int32, (COLS, COLS), 0)
    lane = lax.broadcasted_iota(jnp.int32, (COLS, COLS), 1)
    place = lax.broadcasted_iota(jnp.int32, (COLS, L), 1)
    turned = jnp.zeros((COLS, L), F32)
    for r in range(ROWS):
        row = diffusion_ref[r : r + 1]
        column = jnp.sum(jnp.where(sub == lane, row, 0.0), axis=1, keepdims=True)
        turned = turned + jnp.where(place == r, column, 0.0)
    out_ref[CELLS:] = turned


SIZE = STEPS * CELLS
PACKED = SIZE + STEPS * ROWS * EDGE


def tile_kernel(received_ref, fixed_left_ref, fixed_right_ref, own_ref, to_left_ref, to_right_ref):
    ones, data = [], []
    cell = lax.broadcasted_iota(jnp.int32, (SIZE, L), 0)
    for j in range(4):
        pair = (2 * j, 2 * j + 1)
        codes = sum(received_ref[s, 2 * CAP : 2 * CAP + 1] for s in pair).astype(jnp.int32)
        ones.append(jnp.where(cell == codes, 1.0, 0.0).astype(BF16))
        for s in pair:
            parts = halves(received_ref[s, :CAP]) + halves(received_ref[s, CAP : 2 * CAP])
            data.append(jnp.concatenate(parts, axis=1))
    total = dot(jnp.concatenate(ones, axis=1), jnp.concatenate(data, axis=0))
    forcing = total[:, :L] + total[:, L : 2 * L]
    weights = total[:, 2 * L : 3 * L] + total[:, 3 * L :]
    for ref in (own_ref, to_left_ref, to_right_ref):
        ref[:SIZE] = forcing
    own_ref[SIZE:] = weights
    for k in range(STEPS * ROWS):
        to = pl.ds(SIZE + k * EDGE, EDGE)
        to_left_ref[to] = weights[k * COLS : k * COLS + EDGE]
        to_right_ref[to] = weights[k * COLS + EDGE : (k + 1) * COLS]
    for r in range(ROWS):
        first = (STEPS - 1) * CELLS + r * COLS
        to_left_ref[PACKED + r : PACKED + r + 1] = weights[first + EDGE : first + EDGE + 1]
        to_right_ref[PACKED + r : PACKED + r + 1] = weights[first + EDGE - 1 : first + EDGE]


def wide(refs, start):
    return jnp.concatenate([ref[start : start + COLS] for ref in refs], axis=0)


class Tile:
    def __init__(self, left_ref, own_ref, right_ref, fixed_left_ref, fixed_ref, fixed_right_ref):
        self.left, self.own, self.right = left_ref, own_ref, right_ref
        self.fixed = (fixed_left_ref, fixed_ref, fixed_right_ref)

    def forcing(self, t, r):
        return wide((self.left, self.own, self.right), t * CELLS + r * COLS)

    def inner_weights(self, t, r):
        start = SIZE + t * CELLS + r * COLS
        packed = pl.ds(SIZE + (t * ROWS + r) * EDGE, EDGE)
        return [self.left[packed], self.own[start : start + COLS], self.right[packed]]

    def weights(self, t, r):
        inner = self.inner_weights(t, r)
        if t < STEPS - 1:
            edges = [jnp.zeros((EDGE, L), F32)] * 2
        else:
            edges = [jnp.broadcast_to(ref[PACKED + r : PACKED + r + 1], (EDGE, L)) for ref in (self.left, self.right)]
        return jnp.concatenate([edges[0], *inner, edges[1]], axis=0)

    def std(self, r):
        return wide(self.fixed, r * COLS)

    def turned(self):
        return wide(self.fixed, CELLS)


def inside(row):
    return row[EDGE : EDGE + INNER]


def padded(row):
    edge = jnp.zeros((EDGE, L), F32)
    return jnp.concatenate([edge, row, edge], axis=0)


def places(rows):
    found, total = {}, 0
    for kind, h, width in rows:
        found[kind, h] = (total, width)
        total += width
    return found, total


FIRST, FIRST_ROWS = places(
    [(("f", t), h, WIDE) for t in range(STEPS) for h in range(1, t + 3)]
    + [("std", h, WIDE) for h in range(1, STEPS + 1)]
    + [("diffusion", 1, WIDE)]
)
SECOND, SECOND_ROWS = places(
    [("state", h, WIDE if h <= STEPS else INNER) for h in range(1, REACH + 1)]
    + [("b", h, INNER) for h in range(1, STEPS + 1)]
    + [(("w", t), h, INNER) for t in range(STEPS) for h in range(1, t + 5)]
)
THIRD, THIRD_ROWS = places([(("g", t), h, INNER) for t in range(STEPS) for h in range(1, t + 2)])


def send(low_ref, high_ref, found, kind, h, row):
    start, width = found[kind, h]
    for ref, r in ((low_ref, h - 1), (high_ref, ROWS - h)):
        ref[start : start + width] = row(r)


def taken(sides, found, kind, r):
    below_ref, above_ref = sides
    ref, h = (below_ref, -r) if r < 0 else (above_ref, r - ROWS + 1)
    start, width = found[kind, h]
    return ref[start : start + width]


def sides_kernel(*refs):
    tile, (low_ref, high_ref) = Tile(*refs[:6]), refs[6:]
    for kind, h in FIRST:
        if kind == "std":
            row = tile.std
        elif kind == "diffusion":
            row = lambda r: tile.turned()
        else:
            row = lambda r, t=kind[1]: tile.forcing(t, r)
        send(low_ref, high_ref, FIRST, kind, h, row)


def own(r):
    return 0 <= r < ROWS


class Field:
    def __init__(self, width, reach, v_ref, x_ref, y_ref, d_ref, m_ref):
        self.width, self.reach = width, reach
        self.v_ref, self.x_ref, self.y_ref, self.d_ref, self.m_ref = v_ref, x_ref, y_ref, d_ref, m_ref

    def at(self, r):
        return pl.ds((r + self.reach) * self.width, self.width)

    def put(self, r, value):
        self.v_ref[self.at(r)] = value
        high, low = halves(value)
        self.x_ref[self.at(r), :L] = high
        self.x_ref[self.at(r), L:] = low

    def mix(self, first, stop, which):
        rows = pl.ds((first + self.reach) * self.width, (stop - first) * self.width)
        self.y_ref[rows] = dot(self.x_ref[rows], self.m_ref[which])

    def get(self, r):
        return self.v_ref[self.at(r)] + self.y_ref[self.at(r), :L] + self.y_ref[self.at(r), L:]

    def fill_diffusion(self, tile, sides, reach):
        values = {0: tile.turned(), -1: taken(sides, FIRST, "diffusion", -1), 1: taken(sides, FIRST, "diffusion", ROWS)}
        skip = (WIDE - self.width) // 2
        for r in range(-reach, ROWS + reach):
            column = values[r // ROWS][skip : skip + self.width, r % ROWS : r % ROWS + 1]
            self.d_ref[self.at(r)] = jnp.broadcast_to(column, (self.width, L))

    def smooth(self, first, stop, get, put, scaled=False):
        held = []
        for r in range(first, stop):
            value = get(r)
            if scaled and r in (first, stop - 1):
                held.append((value, None, value))
            else:
                d = self.d_ref[self.at(r)]
                held.append((value, d, d * value))
            if len(held) == 3:
                value, d, u = held[1]
                around = held[0][2] + held[2][2] + pltpu.roll(u, 1, 0) + pltpu.roll(u, self.width - 1, 0)
                put(r - 1, value + d * (around - 4.0 * u))
                held.pop(0)

    def forward(self, h, start, seen, scaled=False):
        self.smooth(-h, ROWS + h, start, self.put, scaled)
        for t in range(STEPS):
            first, stop = -h + t + 1, ROWS + h - t - 1
            self.mix(first, stop, MIX)

            def get(r, t=t):
                value = self.get(r)
                seen(t, r, value)
                return value

            if t < STEPS - 1:
                self.smooth(first, stop, get, self.put)
            else:
                for r in range(first, stop):
                    get(r)

    def adjoint(self, h, forcing, std):
        for t in range(STEPS - 1, -1, -1):
            first, stop = -h - t - 1, ROWS + h + t + 1
            self.mix(first, stop, MIX_T)
            if t > 0:
                put = lambda r, value, t=t: self.put(r, value + forcing(t - 1, r))
            else:
                put = lambda r, value: self.put(r, std(r) * value)
            self.smooth(first, stop, self.get, put)
        self.mix(-h, ROWS + h, FACTOR_T)


def scratch(width, reach):
    tall = (ROWS + 2 * reach) * width
    return [
        pltpu.VMEM((tall, L), F32),
        pltpu.VMEM((tall, 2 * L), BF16),
        pltpu.VMEM((tall, 2 * L), F32),
        pltpu.VMEM((tall, L), F32),
    ]


def std_rows(tile, sides):
    return lambda r: tile.std(r) if own(r) else taken(sides, FIRST, "std", r)


def right_side_kernel(*refs):
    tile, sides, m_ref = Tile(*refs[:6]), refs[6:8], refs[8]
    b_ref, y_ref, low_ref, high_ref = refs[9:13]
    field = Field(WIDE, STEPS + 1, *refs[13:17], m_ref)
    field.fill_diffusion(tile, sides, STEPS + 1)
    forcing = lambda t, r: tile.forcing(t, r) if own(r) else taken(sides, FIRST, ("f", t), r)
    std = std_rows(tile, sides)
    for r in range(-STEPS - 1, ROWS + STEPS + 1):
        field.put(r, forcing(STEPS - 1, r))
    field.adjoint(1, forcing, std)
    for r in range(-1, ROWS + 1):
        value = field.get(r)
        field.put(r, value)
        if own(r):
            b_ref[r] = value
    field.mix(-1, ROWS + 1, FACTOR)
    for r in range(-1, ROWS + 1):
        state = std(r) * field.get(r)
        if own(r):
            y_ref[r] = state
        else:
            state = field.d_ref[field.at(r)] * state
        for ref, h in ((low_ref, r + 1), (high_ref, ROWS - r)):
            if 1 <= h <= REACH and own(r) == (h < REACH):
                start, width = SECOND["state", h]
                ref[start : start + width] = state if width == WIDE else inside(state)
    for kind, h in SECOND:
        if kind == "b":
            send(low_ref, high_ref, SECOND, kind, h, lambda r: inside(b_ref[r]))
        elif kind != "state":
            row = lambda r, t=kind[1]: jnp.concatenate(tile.inner_weights(t, r), axis=0)
            send(low_ref, high_ref, SECOND, kind, h, row)


MIDDLE = slice(COLS, 2 * COLS)


def first_image_kernel(*refs):
    tile, sides, m_ref = Tile(*refs[:6]), refs[6:8], refs[8]
    b_ref, y_ref = refs[9:11]
    more = refs[11:13]
    q_ref, g_ref, low_ref, high_ref, sums_ref = refs[13:18]
    field = Field(WIDE, REACH, *refs[18:22], m_ref)
    tops = refs[22:24]
    field.fill_diffusion(tile, sides, REACH - 1)
    std = std_rows(tile, sides)

    def weights(t, r):
        return tile.weights(t, r) if own(r) else padded(taken(more, SECOND, ("w", t), r))

    def start(r):
        if own(r):
            return y_ref[r]
        row = taken(more, SECOND, "state", r)
        return row if row.shape[0] == WIDE else padded(row)

    def force(t, r, value):
        if -t - 4 <= r < ROWS + t + 4:
            if t < STEPS - 1:
                tops[t][field.at(r)] = weights(t, r) * value
            else:
                field.put(r, weights(t, r) * value)

    field.forward(REACH, start, force, scaled=True)
    field.adjoint(STEPS, lambda t, r: tops[t][field.at(r)], std)
    sums = [jnp.zeros((COLS, L), F32) for _ in range(4)]
    for r in range(-STEPS, ROWS + STEPS):
        b = b_ref[r] if own(r) else padded(taken(more, SECOND, "b", r))
        q = b + field.get(r)
        field.put(r, q)
        if own(r):
            b, q = b[MIDDLE], q[MIDDLE]
            q_ref[r] = q
            for i, term in enumerate((b * b, b * q, q * q, q * q)):
                sums[i] = sums[i] + term
    field.mix(-STEPS, ROWS + STEPS, FACTOR)

    def keep(t, r, value):
        if own(r):
            forced = tile.weights(t, r) * value
            sums[3] = sums[3] + forced[MIDDLE] * value[MIDDLE]
            forced = inside(forced)
            g_ref[t, r] = forced
            for ref, h in ((low_ref, r + 1), (high_ref, ROWS - r)):
                if h <= t + 1:
                    begin, width = THIRD[("g", t), h]
                    ref[begin : begin + width] = forced

    field.forward(STEPS, lambda r: std(r) * field.get(r), keep)
    lane = lax.broadcasted_iota(jnp.int32, (1, L), 1)
    row = jnp.zeros((1, L), F32)
    for i, term in enumerate(sums):
        total = jnp.sum(jnp.sum(term, axis=0, keepdims=True), axis=1, keepdims=True)
        row = row + jnp.where(lane == i, total, 0.0)
    sums_ref[...] = jnp.broadcast_to(row, sums_ref.shape)


def second_image_kernel(*refs):
    tile, sides, m_ref = Tile(*refs[:6]), refs[6:8], refs[8]
    q_ref, g_ref = refs[9:11]
    more = refs[11:13]
    u_ref = refs[13]
    field = Field(INNER, STEPS, *refs[14:18], m_ref)
    field.fill_diffusion(tile, sides, STEPS)
    forcing = lambda t, r: g_ref[t, r] if own(r) else taken(more, THIRD, ("g", t), r)
    for r in range(-STEPS, ROWS + STEPS):
        field.put(r, forcing(STEPS - 1, r))
    field.adjoint(0, forcing, lambda r: inside(tile.std(r)))
    for r in range(ROWS):
        u_ref[r] = q_ref[r] + field.get(r)[EDGE : EDGE + COLS]


def add_kernel(parts_ref, out_ref):
    out_ref[...] = jnp.broadcast_to(jnp.sum(parts_ref[...], axis=0, keepdims=True), out_ref.shape)


def finish_kernel(parts_ref, b_ref, q_ref, u_ref, solution_ref, residual_ref):
    total = jnp.sum(parts_ref[...], axis=0, keepdims=True)
    bb, bq, qq, qu = (total[:, i : i + 1] for i in range(4))
    first = bb / bq
    norm = first * first * qq - bb
    gain = 1.0 + norm / bb
    curve = gain * gain * bq - 2.0 * first * gain * qq + first * first * qu
    second = norm / curve
    along_b = first + second * gain
    along_q = first * second
    for r in range(ROWS):
        b, q = b_ref[r, MIDDLE], q_ref[r]
        solution_ref[r] = along_b * b - along_q * q
        residual_ref[r] = b - along_b * q + along_q * u_ref[r]


def exchange(to_before, to_after, axis, wrap):
    size = lax.axis_size(axis)
    up = [(i, (i + 1) % size) for i in range(size if wrap else size - 1)]
    down = [(j, i) for i, j in up]
    return lax.ppermute(to_after, axis, up), lax.ppermute(to_before, axis, down)


def shards(
    departures, obs_weight, obs_columns, obs_owner, obs_counts, background_std, diffusion, level_factor, model_mixing
):
    parity = (lax.axis_index("lon") % 2).astype(jnp.int32).reshape(1)
    slots = pltpu.VMEM((SLOTS, L), F32)
    buckets = call(
        bucket_kernel,
        "bucket",
        shape(8, BUCKET, L),
        [slots, slots, pltpu.SemaphoreType.DMA((2,))],
        smem=(4, 5),
        hbm=(0, 1),
        vmem=60,
    )(departures, obs_weight, obs_columns.reshape(1, SLOTS), obs_owner.reshape(1, SLOTS), obs_counts, parity)
    received = lax.all_to_all(buckets, "lon", 0, 0)
    mats = call(matrices_kernel, "matrices", shape(4, 2 * L, 2 * L, dtype=BF16))(level_factor, model_mixing)
    fixed = call(fixed_kernel, "fixed", shape(CELLS + COLS, L))(background_std.reshape(CELLS, L), diffusion)
    fixed_left, fixed_right = exchange(fixed, fixed, "lon", True)
    beside = shape(PACKED + ROWS, L)
    tile, to_left, to_right = call(tile_kernel, "tile", (shape(2 * SIZE, L), beside, beside))(
        received, fixed_left, fixed_right
    )
    left, right = exchange(to_left, to_right, "lon", True)
    refs = (left, tile, right, fixed_left, fixed, fixed_right)
    side = shape(FIRST_ROWS, L)
    below, above = exchange(*call(sides_kernel, "sides", (side, side))(*refs), "lat", False)
    refs = (*refs, below, above, mats)
    field, side = shape(ROWS, WIDE, L), shape(SECOND_ROWS, L)
    b, y, low, high = call(right_side_kernel, "right_side", (field, field, side, side), scratch(WIDE, STEPS + 1))(*refs)
    south, north = exchange(low, high, "lat", False)
    lat = lax.axis_size("lat")
    small, side = shape(ROWS, COLS, L), shape(THIRD_ROWS, L)
    space = scratch(WIDE, REACH)
    q, g, low, high, sums = call(
        first_image_kernel,
        "first_image",
        (small, shape(STEPS, ROWS, INNER, L), side, side, shape(lat, L)),
        space + [space[0]] * 2,
    )(*refs, b, y, south, north)
    sums = lax.all_to_all(sums, "lat", 0, 0, tiled=True)
    south, north = exchange(low, high, "lat", False)
    u = call(second_image_kernel, "second_image", small, scratch(INNER, STEPS))(*refs, q, g, south, north)
    sums = call(add_kernel, "add", shape(8, L))(sums)
    sums = lax.all_to_all(sums, "lon", 0, 0, tiled=True)
    return call(finish_kernel, "finish", (small, small))(sums, b, q, u)


def solution(mesh):
    placed = (
        P(("lat", "lon"), None),
        P(("lat", "lon"), None),
        P(("lat", "lon")),
        P(("lat", "lon"), None),
        P(("lat", "lon")),
        P("lat", "lon", None),
        P("lat", "lon"),
        P(),
        P(),
    )
    return jax.shard_map(
        shards,
        mesh=mesh,
        in_specs=placed,
        out_specs=(P("lat", "lon", None), P("lat", "lon", None)),
        check_vma=False,
    )
```

```python
import jax
import jax.numpy as jnp
from jax import lax
from jax.experimental import pallas as pl
from jax.experimental.pallas import tpu as pltpu
from jax.sharding import PartitionSpec as P

F32 = jnp.float32
BF16 = jnp.bfloat16
L = 128
ROWS = 8
COLS = 16
CELLS = ROWS * COLS
STEPS = 3
SLOTS = 256
CAP = 64
WIDE = 3 * COLS
INNER = 2 * COLS
EDGE = COLS // 2
BUCKET = 2 * CAP + 8
REACH = 3 * STEPS

MIB = 1024 * 1024


def call(kernel, name, outs, scratch=(), smem=(), hbm=(), vmem=40):
    def run(*args):
        spaces = [pltpu.SMEM if i in smem else pltpu.HBM if i in hbm else pltpu.VMEM for i in range(len(args))]
        specs = [pl.BlockSpec(memory_space=space) for space in spaces]
        return pl.pallas_call(
            kernel,
            name=name,
            out_shape=outs,
            in_specs=specs,
            out_specs=jax.tree.map(lambda _: pl.BlockSpec(memory_space=pltpu.VMEM), outs),
            scratch_shapes=scratch,
            compiler_params=pltpu.CompilerParams(vmem_limit_bytes=vmem * MIB),
        )(*args)

    return run


def shape(*dims, dtype=F32):
    return jax.ShapeDtypeStruct(dims, dtype)


def halves(x):
    high = x.astype(BF16)
    return high, (x - high.astype(F32)).astype(BF16)


def dot(a, b):
    return jnp.dot(a, b, preferred_element_type=F32)


def matrices_kernel(factor_ref, mixing_ref, out_ref):
    for i, ref in enumerate((mixing_ref, factor_ref)):
        for j in range(2):
            m = 0.5 * ref[...]
            high, low = halves(m.T if j else m)
            row = jnp.concatenate([high, low], axis=1)
            out_ref[2 * i + j] = jnp.concatenate([row, row], axis=0)


MIX, MIX_T, FACTOR, FACTOR_T = range(4)


def bucket_kernel(
    departures_hbm, weight_hbm, columns_ref, owner_ref, counts_ref, parity_ref, out_ref, departures_ref, weight_ref, sems
):
    copies = [
        pltpu.make_async_copy(departures_hbm, departures_ref, sems.at[0]),
        pltpu.make_async_copy(weight_hbm, weight_ref, sems.at[1]),
    ]
    for copy in copies:
        copy.start()
    sub = lax.broadcasted_iota(jnp.int32, (SLOTS, SLOTS), 0)
    lane = lax.broadcasted_iota(jnp.int32, (SLOTS, SLOTS), 1)
    owner_row = owner_ref[...].astype(F32)
    owner_col = jnp.sum(jnp.where(sub == lane, owner_row, 0.0), axis=1, keepdims=True)
    same = owner_row == owner_col
    rank_row = jnp.sum(jnp.where(same & (sub < lane), 1.0, 0.0), axis=0, keepdims=True)
    rank_col = jnp.sum(jnp.where(same & (lane < sub), 1.0, 0.0), axis=1, keepdims=True)
    place = (owner_row * CAP + rank_row).astype(jnp.int32)
    pick = lax.broadcasted_iota(jnp.int32, (8 * CAP, SLOTS), 0) == place
    pick = jnp.where(pick, 1.0, 0.0).astype(BF16)
    slot = lax.broadcasted_iota(jnp.int32, (SLOTS, L), 0)
    for copy in copies:
        copy.wait()
    weights = jnp.where(slot < counts_ref[0], weight_ref[...], 0.0)
    parts = halves(weights * departures_ref[...]) + halves(weights)
    moved = dot(pick, jnp.concatenate(parts, axis=1))
    forcing = moved[:, :L] + moved[:, L : 2 * L]
    weights = moved[:, 2 * L : 3 * L] + moved[:, 3 * L :]
    number = lax.broadcasted_iota(jnp.int32, (1, SLOTS), 1)
    time = (number - STEPS * ((number * 171) >> 9)).astype(F32)
    tile = lax.broadcasted_iota(jnp.int32, (8, SLOTS), 0).astype(F32)
    here = tile == owner_row
    marks = jnp.concatenate(
        [jnp.where(here, time, 0.0), jnp.where(here, columns_ref[...].astype(F32), 0.0)], axis=0
    )
    target = rank_col + (CAP * parity_ref[0]).astype(F32)
    spread = jnp.where(lax.broadcasted_iota(jnp.int32, (SLOTS, L), 1).astype(F32) == target, 1.0, 0.0)
    codes = dot(marks.astype(BF16), spread.astype(BF16))
    codes = CELLS * codes[:8] + codes[8:]
    for d in range(8):
        out_ref[d, :CAP] = forcing[d * CAP : (d + 1) * CAP]
        out_ref[d, CAP : 2 * CAP] = weights[d * CAP : (d + 1) * CAP]
        out_ref[d, 2 * CAP :] = jnp.broadcast_to(codes[d : d + 1], (8, L))


def fixed_kernel(std_ref, diffusion_ref, out_ref):
    out_ref[:CELLS] = std_ref[...]
    sub = lax.broadcasted_iota(jnp.int32, (COLS, COLS), 0)
    lane = lax.broadcasted_iota(jnp.int32, (COLS, COLS), 1)
    place = lax.broadcasted_iota(jnp.int32, (COLS, L), 1)
    turned = jnp.zeros((COLS, L), F32)
    for r in range(ROWS):
        row = diffusion_ref[r : r + 1]
        column = jnp.sum(jnp.where(sub == lane, row, 0.0), axis=1, keepdims=True)
        turned = turned + jnp.where(place == r, column, 0.0)
    out_ref[CELLS:] = turned


SIZE = STEPS * CELLS
PACKED = SIZE + STEPS * ROWS * EDGE


def tile_kernel(received_ref, fixed_left_ref, fixed_right_ref, own_ref, to_left_ref, to_right_ref):
    ones, data = [], []
    cell = lax.broadcasted_iota(jnp.int32, (SIZE, L), 0)
    for j in range(4):
        pair = (2 * j, 2 * j + 1)
        codes = sum(received_ref[s, 2 * CAP : 2 * CAP + 1] for s in pair).astype(jnp.int32)
        ones.append(jnp.where(cell == codes, 1.0, 0.0).astype(BF16))
        for s in pair:
            parts = halves(received_ref[s, :CAP]) + halves(received_ref[s, CAP : 2 * CAP])
            data.append(jnp.concatenate(parts, axis=1))
    total = dot(jnp.concatenate(ones, axis=1), jnp.concatenate(data, axis=0))
    forcing = total[:, :L] + total[:, L : 2 * L]
    weights = total[:, 2 * L : 3 * L] + total[:, 3 * L :]
    for ref in (own_ref, to_left_ref, to_right_ref):
        ref[:SIZE] = forcing
    own_ref[SIZE:] = weights
    for k in range(STEPS * ROWS):
        to = pl.ds(SIZE + k * EDGE, EDGE)
        to_left_ref[to] = weights[k * COLS : k * COLS + EDGE]
        to_right_ref[to] = weights[k * COLS + EDGE : (k + 1) * COLS]
    for r in range(ROWS):
        first = (STEPS - 1) * CELLS + r * COLS
        to_left_ref[PACKED + r : PACKED + r + 1] = weights[first + EDGE : first + EDGE + 1]
        to_right_ref[PACKED + r : PACKED + r + 1] = weights[first + EDGE - 1 : first + EDGE]


def wide(refs, start):
    return jnp.concatenate([ref[start : start + COLS] for ref in refs], axis=0)


class Tile:
    def __init__(self, left_ref, own_ref, right_ref, fixed_left_ref, fixed_ref, fixed_right_ref):
        self.left, self.own, self.right = left_ref, own_ref, right_ref
        self.fixed = (fixed_left_ref, fixed_ref, fixed_right_ref)

    def forcing(self, t, r):
        return wide((self.left, self.own, self.right), t * CELLS + r * COLS)

    def inner_weights(self, t, r):
        start = SIZE + t * CELLS + r * COLS
        packed = pl.ds(SIZE + (t * ROWS + r) * EDGE, EDGE)
        return [self.left[packed], self.own[start : start + COLS], self.right[packed]]

    def weights(self, t, r):
        inner = self.inner_weights(t, r)
        if t < STEPS - 1:
            edges = [jnp.zeros((EDGE, L), F32)] * 2
        else:
            edges = [jnp.broadcast_to(ref[PACKED + r : PACKED + r + 1], (EDGE, L)) for ref in (self.left, self.right)]
        return jnp.concatenate([edges[0], *inner, edges[1]], axis=0)

    def std(self, r):
        return wide(self.fixed, r * COLS)

    def turned(self):
        return wide(self.fixed, CELLS)


def inside(row):
    return row[EDGE : EDGE + INNER]


def padded(row):
    if row.shape[0] == WIDE:
        return row
    edge = jnp.zeros((EDGE, L), F32)
    return jnp.concatenate([edge, row, edge], axis=0)


def places(rows):
    found, total = {}, 0
    for kind, h, width in rows:
        found[kind, h] = (total, width)
        total += width
    return found, total


FIRST, FIRST_ROWS = places(
    [(("f", t), h, WIDE if h < t + 2 else INNER) for t in range(STEPS) for h in range(1, t + 3)]
    + [("std", h, INNER) for h in range(1, STEPS + 1)]
    + [("diffusion", 1, WIDE)]
)
SECOND, SECOND_ROWS = places(
    [("state", h, WIDE if h <= STEPS else INNER) for h in range(1, REACH + 1)]
    + [("b", h, INNER) for h in range(1, STEPS + 1)]
)
WEIGHTS, WEIGHTS_ROWS = places([(("w", t), h, INNER) for t in range(STEPS) for h in range(1, t + 5)])
THIRD, THIRD_ROWS = places([(("g", t), h, INNER) for t in range(STEPS) for h in range(1, t + 2)])


def send(low_ref, high_ref, found, kind, h, row):
    start, width = found[kind, h]
    for ref, r in ((low_ref, h - 1), (high_ref, ROWS - h)):
        value = row(r)
        ref[start : start + width] = inside(value) if width < value.shape[0] else value


def taken(sides, found, kind, r):
    below_ref, above_ref = sides
    ref, h = (below_ref, -r) if r < 0 else (above_ref, r - ROWS + 1)
    start, width = found[kind, h]
    return ref[start : start + width]


def sides_kernel(*refs):
    tile, (low_ref, high_ref) = Tile(*refs[:6]), refs[6:]
    for kind, h in FIRST:
        if kind == "std":
            row = tile.std
        elif kind == "diffusion":
            row = lambda r: tile.turned()
        else:
            row = lambda r, t=kind[1]: tile.forcing(t, r)
        send(low_ref, high_ref, FIRST, kind, h, row)


def weights_kernel(*refs):
    tile, (low_ref, high_ref) = Tile(*refs[:6]), refs[6:]
    for kind, h in WEIGHTS:
        send(low_ref, high_ref, WEIGHTS, kind, h, lambda r: jnp.concatenate(tile.inner_weights(kind[1], r), axis=0))


def own(r):
    return 0 <= r < ROWS


class Field:
    def __init__(self, width, reach, v_ref, x_ref, y_ref, d_ref, m_ref):
        self.width, self.reach = width, reach
        self.v_ref, self.x_ref, self.y_ref, self.d_ref, self.m_ref = v_ref, x_ref, y_ref, d_ref, m_ref

    def at(self, r):
        return pl.ds((r + self.reach) * self.width, self.width)

    def put(self, r, value):
        self.v_ref[self.at(r)] = value
        high, low = halves(value)
        self.x_ref[self.at(r), :L] = high
        self.x_ref[self.at(r), L:] = low

    def mix(self, first, stop, which):
        rows = pl.ds((first + self.reach) * self.width, (stop - first) * self.width)
        self.y_ref[rows] = dot(self.x_ref[rows], self.m_ref[which])

    def get(self, r):
        return self.v_ref[self.at(r)] + self.y_ref[self.at(r), :L] + self.y_ref[self.at(r), L:]

    def fill_diffusion(self, tile, sides, reach):
        values = {0: tile.turned(), -1: taken(sides, FIRST, "diffusion", -1), 1: taken(sides, FIRST, "diffusion", ROWS)}
        skip = (WIDE - self.width) // 2
        for r in range(-reach, ROWS + reach):
            column = values[r // ROWS][skip : skip + self.width, r % ROWS : r % ROWS + 1]
            self.d_ref[self.at(r)] = jnp.broadcast_to(column, (self.width, L))

    def smooth(self, first, stop, get, put, scaled=False):
        held = []
        for r in range(first, stop):
            value = get(r)
            if scaled and r in (first, stop - 1):
                held.append((value, None, value))
            else:
                d = self.d_ref[self.at(r)]
                held.append((value, d, d * value))
            if len(held) == 3:
                value, d, u = held[1]
                around = held[0][2] + held[2][2] + pltpu.roll(u, 1, 0) + pltpu.roll(u, self.width - 1, 0)
                put(r - 1, value + d * (around - 4.0 * u))
                held.pop(0)

    def forward(self, h, start, seen, scaled=False):
        self.smooth(-h, ROWS + h, start, self.put, scaled)
        for t in range(STEPS):
            first, stop = -h + t + 1, ROWS + h - t - 1
            self.mix(first, stop, MIX)

            def get(r, t=t):
                value = self.get(r)
                seen(t, r, value)
                return value

            if t < STEPS - 1:
                self.smooth(first, stop, get, self.put)
            else:
                for r in range(first, stop):
                    get(r)

    def adjoint(self, h, forcing, std):
        for t in range(STEPS - 1, -1, -1):
            first, stop = -h - t - 1, ROWS + h + t + 1
            self.mix(first, stop, MIX_T)
            if t > 0:
                put = lambda r, value, t=t: self.put(r, value + forcing(t - 1, r))
            else:
                put = lambda r, value: self.put(r, std(r) * value)
            self.smooth(first, stop, self.get, put)
        self.mix(-h, ROWS + h, FACTOR_T)


def scratch(width, reach):
    tall = (ROWS + 2 * reach) * width
    return [
        pltpu.VMEM((tall, L), F32),
        pltpu.VMEM((tall, 2 * L), BF16),
        pltpu.VMEM((tall, 2 * L), F32),
        pltpu.VMEM((tall, L), F32),
    ]


def std_rows(tile, sides):
    return lambda r: tile.std(r) if own(r) else padded(taken(sides, FIRST, "std", r))


def right_side_kernel(*refs):
    tile, sides, m_ref = Tile(*refs[:6]), refs[6:8], refs[8]
    b_ref, y_ref, low_ref, high_ref = refs[9:13]
    field = Field(WIDE, STEPS + 1, *refs[13:17], m_ref)
    field.fill_diffusion(tile, sides, STEPS + 1)
    forcing = lambda t, r: tile.forcing(t, r) if own(r) else padded(taken(sides, FIRST, ("f", t), r))
    std = std_rows(tile, sides)
    for r in range(-STEPS - 1, ROWS + STEPS + 1):
        field.put(r, forcing(STEPS - 1, r))
    field.adjoint(1, forcing, std)
    for r in range(-1, ROWS + 1):
        value = field.get(r)
        field.put(r, value)
        if own(r):
            b_ref[r] = value
    field.mix(-1, ROWS + 1, FACTOR)
    for r in range(-1, ROWS + 1):
        state = std(r) * field.get(r)
        if own(r):
            y_ref[r] = state
        else:
            state = field.d_ref[field.at(r)] * state
        for ref, h in ((low_ref, r + 1), (high_ref, ROWS - r)):
            if 1 <= h <= REACH and own(r) == (h < REACH):
                start, width = SECOND["state", h]
                ref[start : start + width] = state if width == WIDE else inside(state)
    for h in range(1, STEPS + 1):
        send(low_ref, high_ref, SECOND, "b", h, lambda r: b_ref[r])


MIDDLE = slice(COLS, 2 * COLS)


def first_image_kernel(*refs):
    tile, sides, m_ref = Tile(*refs[:6]), refs[6:8], refs[8]
    b_ref, y_ref = refs[9:11]
    more, forced = refs[11:13], refs[13:15]
    q_ref, g_ref, low_ref, high_ref, sums_ref = refs[15:20]
    field = Field(WIDE, REACH, *refs[20:24], m_ref)
    tops = refs[24:26]
    field.fill_diffusion(tile, sides, REACH - 1)
    std = std_rows(tile, sides)

    def weights(t, r):
        return tile.weights(t, r) if own(r) else padded(taken(forced, WEIGHTS, ("w", t), r))

    def start(r):
        if own(r):
            return y_ref[r]
        return padded(taken(more, SECOND, "state", r))

    def force(t, r, value):
        if -t - 4 <= r < ROWS + t + 4:
            if t < STEPS - 1:
                tops[t][field.at(r)] = weights(t, r) * value
            else:
                field.put(r, weights(t, r) * value)

    field.forward(REACH, start, force, scaled=True)
    field.adjoint(STEPS, lambda t, r: tops[t][field.at(r)], std)
    sums = [jnp.zeros((COLS, L), F32) for _ in range(4)]
    for r in range(-STEPS, ROWS + STEPS):
        b = b_ref[r] if own(r) else padded(taken(more, SECOND, "b", r))
        q = b + field.get(r)
        field.put(r, q)
        if own(r):
            b, q = b[MIDDLE], q[MIDDLE]
            q_ref[r] = q
            for i, term in enumerate((b * b, b * q, q * q, q * q)):
                sums[i] = sums[i] + term
    field.mix(-STEPS, ROWS + STEPS, FACTOR)

    def keep(t, r, value):
        if own(r):
            forced = tile.weights(t, r) * value
            sums[3] = sums[3] + forced[MIDDLE] * value[MIDDLE]
            forced = inside(forced)
            g_ref[t, r] = forced
            for ref, h in ((low_ref, r + 1), (high_ref, ROWS - r)):
                if h <= t + 1:
                    begin, width = THIRD[("g", t), h]
                    ref[begin : begin + width] = forced

    field.forward(STEPS, lambda r: std(r) * field.get(r), keep)
    lane = lax.broadcasted_iota(jnp.int32, (1, L), 1)
    row = jnp.zeros((1, L), F32)
    for i, term in enumerate(sums):
        total = jnp.sum(jnp.sum(term, axis=0, keepdims=True), axis=1, keepdims=True)
        row = row + jnp.where(lane == i, total, 0.0)
    sums_ref[...] = jnp.broadcast_to(row, sums_ref.shape)


def second_image_kernel(*refs):
    tile, sides, m_ref = Tile(*refs[:6]), refs[6:8], refs[8]
    q_ref, g_ref = refs[9:11]
    more = refs[11:13]
    u_ref = refs[13]
    field = Field(INNER, STEPS, *refs[14:18], m_ref)
    field.fill_diffusion(tile, sides, STEPS)
    forcing = lambda t, r: g_ref[t, r] if own(r) else taken(more, THIRD, ("g", t), r)
    for r in range(-STEPS, ROWS + STEPS):
        field.put(r, forcing(STEPS - 1, r))
    field.adjoint(0, forcing, lambda r: inside(tile.std(r)))
    for r in range(ROWS):
        u_ref[r] = q_ref[r] + field.get(r)[EDGE : EDGE + COLS]


def levels(lat, lon):
    quarter = lat // 4
    near = [[i * quarter + k for k in range(quarter)] for i in range(4)]
    far = [[(i * quarter + k) * lon + j for i in range(4) for j in range(lon)] for k in range(quarter)]
    return near, far


def add_kernel(parts_ref, out_ref):
    out_ref[...] = jnp.broadcast_to(jnp.sum(parts_ref[...], axis=0, keepdims=True), out_ref.shape)


def finish_kernel(parts_ref, b_ref, q_ref, u_ref, solution_ref, residual_ref):
    total = jnp.sum(parts_ref[...], axis=0, keepdims=True)
    bb, bq, qq, qu = (total[:, i : i + 1] for i in range(4))
    first = bb / bq
    norm = first * first * qq - bb
    gain = 1.0 + norm / bb
    curve = gain * gain * bq - 2.0 * first * gain * qq + first * first * qu
    second = norm / curve
    along_b = first + second * gain
    along_q = first * second
    for r in range(ROWS):
        b, q = b_ref[r, MIDDLE], q_ref[r]
        solution_ref[r] = along_b * b - along_q * q
        residual_ref[r] = b - along_b * q + along_q * u_ref[r]


def exchange(to_before, to_after, axis, wrap):
    size = lax.axis_size(axis)
    up = [(i, (i + 1) % size) for i in range(size if wrap else size - 1)]
    down = [(j, i) for i, j in up]
    return lax.ppermute(to_after, axis, up), lax.ppermute(to_before, axis, down)


def shards(
    departures, obs_weight, obs_columns, obs_owner, obs_counts, background_std, diffusion, level_factor, model_mixing
):
    parity = (lax.axis_index("lon") % 2).astype(jnp.int32).reshape(1)
    slots = pltpu.VMEM((SLOTS, L), F32)
    buckets = call(
        bucket_kernel,
        "bucket",
        shape(8, BUCKET, L),
        [slots, slots, pltpu.SemaphoreType.DMA((2,))],
        smem=(4, 5),
        hbm=(0, 1),
        vmem=60,
    )(departures, obs_weight, obs_columns.reshape(1, SLOTS), obs_owner.reshape(1, SLOTS), obs_counts, parity)
    received = lax.all_to_all(buckets, "lon", 0, 0)
    mats = call(matrices_kernel, "matrices", shape(4, 2 * L, 2 * L, dtype=BF16))(level_factor, model_mixing)
    fixed = call(fixed_kernel, "fixed", shape(CELLS + COLS, L))(background_std.reshape(CELLS, L), diffusion)
    fixed_left, fixed_right = exchange(fixed, fixed, "lon", True)
    beside = shape(PACKED + ROWS, L)
    tile, to_left, to_right = call(tile_kernel, "tile", (shape(2 * SIZE, L), beside, beside))(
        received, fixed_left, fixed_right
    )
    left, right = exchange(to_left, to_right, "lon", True)
    refs = (left, tile, right, fixed_left, fixed, fixed_right)
    side = shape(FIRST_ROWS, L)
    below, above = exchange(*call(sides_kernel, "sides", (side, side))(*refs), "lat", False)
    side = shape(WEIGHTS_ROWS, L)
    weights = exchange(*call(weights_kernel, "weights", (side, side))(*refs), "lat", False)
    refs = (*refs, below, above, mats)
    field, side = shape(ROWS, WIDE, L), shape(SECOND_ROWS, L)
    b, y, low, high = call(right_side_kernel, "right_side", (field, field, side, side), scratch(WIDE, STEPS + 1))(*refs)
    south, north = exchange(low, high, "lat", False)
    lat, lon = lax.axis_size("lat"), lax.axis_size("lon")
    near, far = levels(lat, lon)
    small, side = shape(ROWS, COLS, L), shape(THIRD_ROWS, L)
    space = scratch(WIDE, REACH)
    q, g, low, high, sums = call(
        first_image_kernel,
        "first_image",
        (small, shape(STEPS, ROWS, INNER, L), side, side, shape(4 * lon, L)),
        space + [space[0]] * 2,
    )(*refs, b, y, south, north, *weights)
    sums = lax.all_to_all(sums, ("lat", "lon"), 0, 0, axis_index_groups=far, tiled=True)
    south, north = exchange(low, high, "lat", False)
    u = call(second_image_kernel, "second_image", small, scratch(INNER, STEPS))(*refs, q, g, south, north)
    sums = call(add_kernel, "add", shape(lat // 4, L))(sums)
    sums = lax.all_to_all(sums, "lat", 0, 0, axis_index_groups=near, tiled=True)
    return call(finish_kernel, "finish", (small, small))(sums, b, q, u)


def solution(mesh):
    placed = (
        P(("lat", "lon"), None),
        P(("lat", "lon"), None),
        P(("lat", "lon")),
        P(("lat", "lon"), None),
        P(("lat", "lon")),
        P("lat", "lon", None),
        P("lat", "lon"),
        P(),
        P(),
    )
    return jax.shard_map(
        shards,
        mesh=mesh,
        in_specs=placed,
        out_specs=(P("lat", "lon", None), P("lat", "lon", None)),
        check_vma=False,
    )
```

```python
import jax
import jax.numpy as jnp
from jax import lax
from jax.experimental import pallas as pl
from jax.experimental.pallas import tpu as pltpu
from jax.sharding import PartitionSpec as P

F32 = jnp.float32
BF16 = jnp.bfloat16
L = 128
ROWS = 8
COLS = 16
CELLS = ROWS * COLS
STEPS = 3
SLOTS = 256
CAP = 64
WIDE = 3 * COLS
INNER = 2 * COLS
EDGE = COLS // 2
BUCKET = 2 * CAP + 8
REACH = 3 * STEPS

MIB = 1024 * 1024


def call(kernel, name, outs, scratch=(), smem=(), hbm=(), vmem=40):
    def run(*args):
        spaces = [pltpu.SMEM if i in smem else pltpu.HBM if i in hbm else pltpu.VMEM for i in range(len(args))]
        specs = [pl.BlockSpec(memory_space=space) for space in spaces]
        return pl.pallas_call(
            kernel,
            name=name,
            out_shape=outs,
            in_specs=specs,
            out_specs=jax.tree.map(lambda _: pl.BlockSpec(memory_space=pltpu.VMEM), outs),
            scratch_shapes=scratch,
            compiler_params=pltpu.CompilerParams(vmem_limit_bytes=vmem * MIB),
        )(*args)

    return run


def shape(*dims, dtype=F32):
    return jax.ShapeDtypeStruct(dims, dtype)


def halves(x):
    high = x.astype(BF16)
    return high, (x - high.astype(F32)).astype(BF16)


def dot(a, b):
    return jnp.dot(a, b, preferred_element_type=F32)


def matrices_kernel(factor_ref, mixing_ref, out_ref):
    for i, ref in enumerate((mixing_ref, factor_ref)):
        for j in range(2):
            m = 0.5 * ref[...]
            high, low = halves(m.T if j else m)
            row = jnp.concatenate([high, low], axis=1)
            out_ref[2 * i + j] = jnp.concatenate([row, row], axis=0)


MIX, MIX_T, FACTOR, FACTOR_T = range(4)


def bucket_kernel(
    departures_hbm, weight_hbm, columns_ref, owner_ref, counts_ref, parity_ref, out_ref, departures_ref, weight_ref, sems
):
    copies = [
        pltpu.make_async_copy(departures_hbm, departures_ref, sems.at[0]),
        pltpu.make_async_copy(weight_hbm, weight_ref, sems.at[1]),
    ]
    for copy in copies:
        copy.start()
    sub = lax.broadcasted_iota(jnp.int32, (SLOTS, SLOTS), 0)
    lane = lax.broadcasted_iota(jnp.int32, (SLOTS, SLOTS), 1)
    owner_row = owner_ref[...].astype(F32)
    owner_col = jnp.sum(jnp.where(sub == lane, owner_row, 0.0), axis=1, keepdims=True)
    same = owner_row == owner_col
    rank_row = jnp.sum(jnp.where(same & (sub < lane), 1.0, 0.0), axis=0, keepdims=True)
    rank_col = jnp.sum(jnp.where(same & (lane < sub), 1.0, 0.0), axis=1, keepdims=True)
    place = (owner_row * CAP + rank_row).astype(jnp.int32)
    pick = lax.broadcasted_iota(jnp.int32, (8 * CAP, SLOTS), 0) == place
    pick = jnp.where(pick, 1.0, 0.0).astype(BF16)
    slot = lax.broadcasted_iota(jnp.int32, (SLOTS, L), 0)
    for copy in copies:
        copy.wait()
    weights = jnp.where(slot < counts_ref[0], weight_ref[...], 0.0)
    parts = halves(weights * departures_ref[...]) + halves(weights)
    moved = dot(pick, jnp.concatenate(parts, axis=1))
    forcing = moved[:, :L] + moved[:, L : 2 * L]
    weights = moved[:, 2 * L : 3 * L] + moved[:, 3 * L :]
    number = lax.broadcasted_iota(jnp.int32, (1, SLOTS), 1)
    time = (number - STEPS * ((number * 171) >> 9)).astype(F32)
    tile = lax.broadcasted_iota(jnp.int32, (8, SLOTS), 0).astype(F32)
    here = tile == owner_row
    marks = jnp.concatenate(
        [jnp.where(here, time, 0.0), jnp.where(here, columns_ref[...].astype(F32), 0.0)], axis=0
    )
    target = rank_col + (CAP * parity_ref[0]).astype(F32)
    spread = jnp.where(lax.broadcasted_iota(jnp.int32, (SLOTS, L), 1).astype(F32) == target, 1.0, 0.0)
    codes = dot(marks.astype(BF16), spread.astype(BF16))
    codes = CELLS * codes[:8] + codes[8:]
    for d in range(8):
        out_ref[d, :CAP] = forcing[d * CAP : (d + 1) * CAP]
        out_ref[d, CAP : 2 * CAP] = weights[d * CAP : (d + 1) * CAP]
        out_ref[d, 2 * CAP :] = jnp.broadcast_to(codes[d : d + 1], (8, L))


def fixed_kernel(std_ref, diffusion_ref, out_ref):
    out_ref[:CELLS] = std_ref[...]
    sub = lax.broadcasted_iota(jnp.int32, (COLS, COLS), 0)
    lane = lax.broadcasted_iota(jnp.int32, (COLS, COLS), 1)
    place = lax.broadcasted_iota(jnp.int32, (COLS, L), 1)
    turned = jnp.zeros((COLS, L), F32)
    for r in range(ROWS):
        row = diffusion_ref[r : r + 1]
        column = jnp.sum(jnp.where(sub == lane, row, 0.0), axis=1, keepdims=True)
        turned = turned + jnp.where(place == r, column, 0.0)
    out_ref[CELLS:] = turned


SIZE = STEPS * CELLS
PACKED = SIZE + STEPS * ROWS * EDGE


def tile_kernel(received_ref, fixed_left_ref, fixed_right_ref, own_ref, to_left_ref, to_right_ref):
    ones, data = [], []
    cell = lax.broadcasted_iota(jnp.int32, (SIZE, L), 0)
    for j in range(4):
        pair = (2 * j, 2 * j + 1)
        codes = sum(received_ref[s, 2 * CAP : 2 * CAP + 1] for s in pair).astype(jnp.int32)
        ones.append(jnp.where(cell == codes, 1.0, 0.0).astype(BF16))
        for s in pair:
            parts = halves(received_ref[s, :CAP]) + halves(received_ref[s, CAP : 2 * CAP])
            data.append(jnp.concatenate(parts, axis=1))
    total = dot(jnp.concatenate(ones, axis=1), jnp.concatenate(data, axis=0))
    forcing = total[:, :L] + total[:, L : 2 * L]
    weights = total[:, 2 * L : 3 * L] + total[:, 3 * L :]
    for ref in (own_ref, to_left_ref, to_right_ref):
        ref[:SIZE] = forcing
    own_ref[SIZE:] = weights
    for k in range(STEPS * ROWS):
        to = pl.ds(SIZE + k * EDGE, EDGE)
        to_left_ref[to] = weights[k * COLS : k * COLS + EDGE]
        to_right_ref[to] = weights[k * COLS + EDGE : (k + 1) * COLS]
    for r in range(ROWS):
        first = (STEPS - 1) * CELLS + r * COLS
        to_left_ref[PACKED + r : PACKED + r + 1] = weights[first + EDGE : first + EDGE + 1]
        to_right_ref[PACKED + r : PACKED + r + 1] = weights[first + EDGE - 1 : first + EDGE]


def wide(refs, start):
    return jnp.concatenate([ref[start : start + COLS] for ref in refs], axis=0)


class Tile:
    def __init__(self, left_ref, own_ref, right_ref, fixed_left_ref, fixed_ref, fixed_right_ref):
        self.left, self.own, self.right = left_ref, own_ref, right_ref
        self.fixed = (fixed_left_ref, fixed_ref, fixed_right_ref)

    def forcing(self, t, r):
        return wide((self.left, self.own, self.right), t * CELLS + r * COLS)

    def inner_weights(self, t, r):
        start = SIZE + t * CELLS + r * COLS
        packed = pl.ds(SIZE + (t * ROWS + r) * EDGE, EDGE)
        return [self.left[packed], self.own[start : start + COLS], self.right[packed]]

    def weights(self, t, r):
        inner = self.inner_weights(t, r)
        if t < STEPS - 1:
            edges = [jnp.zeros((EDGE, L), F32)] * 2
        else:
            edges = [jnp.broadcast_to(ref[PACKED + r : PACKED + r + 1], (EDGE, L)) for ref in (self.left, self.right)]
        return jnp.concatenate([edges[0], *inner, edges[1]], axis=0)

    def std(self, r):
        return wide(self.fixed, r * COLS)

    def turned(self):
        return wide(self.fixed, CELLS)


def inside(row):
    return row[EDGE : EDGE + INNER]


def padded(row):
    if row.shape[0] == WIDE:
        return row
    edge = jnp.zeros((EDGE, L), F32)
    return jnp.concatenate([edge, row, edge], axis=0)


def places(rows):
    found, total = {}, 0
    for kind, h, width in rows:
        found[kind, h] = (total, width)
        total += width
    return found, total


FIRST, FIRST_ROWS = places(
    [(("f", t), h, WIDE if h < t + 2 else INNER) for t in range(STEPS) for h in range(1, t + 3)]
    + [("std", h, INNER) for h in range(1, STEPS + 1)]
    + [("diffusion", 1, WIDE)]
)
SECOND, SECOND_ROWS = places(
    [("state", h, WIDE if h <= STEPS else INNER) for h in range(1, REACH + 1)]
    + [("b", h, INNER) for h in range(1, STEPS + 1)]
)
WEIGHTS, WEIGHTS_ROWS = places([(("w", t), h, INNER) for t in range(STEPS) for h in range(1, t + 5)])
THIRD, THIRD_ROWS = places([(("g", t), h, INNER) for t in range(STEPS) for h in range(1, t + 2)])


def send(low_ref, high_ref, found, kind, h, row):
    start, width = found[kind, h]
    for ref, r in ((low_ref, h - 1), (high_ref, ROWS - h)):
        value = row(r)
        ref[start : start + width] = inside(value) if width < value.shape[0] else value


def taken(sides, found, kind, r):
    below_ref, above_ref = sides
    ref, h = (below_ref, -r) if r < 0 else (above_ref, r - ROWS + 1)
    start, width = found[kind, h]
    return ref[start : start + width]


def sides_kernel(*refs):
    tile, (low_ref, high_ref) = Tile(*refs[:6]), refs[6:]
    for kind, h in FIRST:
        if kind == "std":
            row = tile.std
        elif kind == "diffusion":
            row = lambda r: tile.turned()
        else:
            row = lambda r, t=kind[1]: tile.forcing(t, r)
        send(low_ref, high_ref, FIRST, kind, h, row)


def weights_kernel(*refs):
    tile, (low_ref, high_ref) = Tile(*refs[:6]), refs[6:]
    for kind, h in WEIGHTS:
        send(low_ref, high_ref, WEIGHTS, kind, h, lambda r: jnp.concatenate(tile.inner_weights(kind[1], r), axis=0))


def own(r):
    return 0 <= r < ROWS


class Field:
    def __init__(self, width, reach, v_ref, x_ref, y_ref, d_ref, m_ref):
        self.width, self.reach = width, reach
        self.v_ref, self.x_ref, self.y_ref, self.d_ref, self.m_ref = v_ref, x_ref, y_ref, d_ref, m_ref

    def at(self, r):
        return pl.ds((r + self.reach) * self.width, self.width)

    def put(self, r, value):
        self.v_ref[self.at(r)] = value
        high, low = halves(value)
        self.x_ref[self.at(r), :L] = high
        self.x_ref[self.at(r), L:] = low

    def mix(self, first, stop, which):
        rows = pl.ds((first + self.reach) * self.width, (stop - first) * self.width)
        self.y_ref[rows] = dot(self.x_ref[rows], self.m_ref[which])

    def get(self, r):
        return self.v_ref[self.at(r)] + self.y_ref[self.at(r), :L] + self.y_ref[self.at(r), L:]

    def fill_diffusion(self, tile, sides, reach):
        values = {0: tile.turned(), -1: taken(sides, FIRST, "diffusion", -1), 1: taken(sides, FIRST, "diffusion", ROWS)}
        skip = (WIDE - self.width) // 2
        for r in range(-reach, ROWS + reach):
            column = values[r // ROWS][skip : skip + self.width, r % ROWS : r % ROWS + 1]
            self.d_ref[self.at(r)] = jnp.broadcast_to(column, (self.width, L))

    def smooth(self, first, stop, get, put, scaled=False):
        held = []
        for r in range(first, stop):
            value = get(r)
            if scaled and r in (first, stop - 1):
                held.append((value, None, value))
            else:
                d = self.d_ref[self.at(r)]
                held.append((value, d, d * value))
            if len(held) == 3:
                value, d, u = held[1]
                around = held[0][2] + held[2][2] + pltpu.roll(u, 1, 0) + pltpu.roll(u, self.width - 1, 0)
                put(r - 1, value + d * (around - 4.0 * u))
                held.pop(0)

    def forward(self, h, start, seen, scaled=False):
        self.smooth(-h, ROWS + h, start, self.put, scaled)
        for t in range(STEPS):
            first, stop = -h + t + 1, ROWS + h - t - 1
            self.mix(first, stop, MIX)

            def get(r, t=t):
                value = self.get(r)
                seen(t, r, value)
                return value

            if t < STEPS - 1:
                self.smooth(first, stop, get, self.put)
            else:
                for r in range(first, stop):
                    get(r)

    def adjoint(self, h, forcing, std):
        for t in range(STEPS - 1, -1, -1):
            first, stop = -h - t - 1, ROWS + h + t + 1
            self.mix(first, stop, MIX_T)
            if t > 0:
                put = lambda r, value, t=t: self.put(r, value + forcing(t - 1, r))
            else:
                put = lambda r, value: self.put(r, std(r) * value)
            self.smooth(first, stop, self.get, put)
        self.mix(-h, ROWS + h, FACTOR_T)


def scratch(width, reach):
    tall = (ROWS + 2 * reach) * width
    return [
        pltpu.VMEM((tall, L), F32),
        pltpu.VMEM((tall, 2 * L), BF16),
        pltpu.VMEM((tall, 2 * L), F32),
        pltpu.VMEM((tall, L), F32),
    ]


def std_rows(tile, sides):
    return lambda r: tile.std(r) if own(r) else padded(taken(sides, FIRST, "std", r))


def right_side_kernel(*refs):
    tile, sides, m_ref = Tile(*refs[:6]), refs[6:8], refs[8]
    b_ref, y_ref, low_ref, high_ref = refs[9:13]
    field = Field(WIDE, STEPS + 1, *refs[13:17], m_ref)
    field.fill_diffusion(tile, sides, STEPS + 1)
    forcing = lambda t, r: tile.forcing(t, r) if own(r) else padded(taken(sides, FIRST, ("f", t), r))
    std = std_rows(tile, sides)
    for r in range(-STEPS - 1, ROWS + STEPS + 1):
        field.put(r, forcing(STEPS - 1, r))
    field.adjoint(1, forcing, std)
    for r in range(-1, ROWS + 1):
        value = field.get(r)
        field.put(r, value)
        if own(r):
            b_ref[r] = value
    field.mix(-1, ROWS + 1, FACTOR)
    for r in range(-1, ROWS + 1):
        state = std(r) * field.get(r)
        if own(r):
            y_ref[r] = state
        else:
            state = field.d_ref[field.at(r)] * state
        for ref, h in ((low_ref, r + 1), (high_ref, ROWS - r)):
            if 1 <= h <= REACH and own(r) == (h < REACH):
                start, width = SECOND["state", h]
                ref[start : start + width] = state if width == WIDE else inside(state)
    for h in range(1, STEPS + 1):
        send(low_ref, high_ref, SECOND, "b", h, lambda r: b_ref[r])


MIDDLE = slice(COLS, 2 * COLS)


def first_image_kernel(*refs):
    tile, sides, m_ref = Tile(*refs[:6]), refs[6:8], refs[8]
    b_ref, y_ref = refs[9:11]
    more, forced = refs[11:13], refs[13:15]
    q_ref, g_ref, low_ref, high_ref, sums_ref = refs[15:20]
    field = Field(WIDE, REACH, *refs[20:24], m_ref)
    tops = refs[24:26]
    field.fill_diffusion(tile, sides, REACH - 1)
    std = std_rows(tile, sides)

    def weights(t, r):
        return tile.weights(t, r) if own(r) else padded(taken(forced, WEIGHTS, ("w", t), r))

    def start(r):
        if own(r):
            return y_ref[r]
        return padded(taken(more, SECOND, "state", r))

    def force(t, r, value):
        if -t - 4 <= r < ROWS + t + 4:
            if t < STEPS - 1:
                tops[t][field.at(r)] = weights(t, r) * value
            else:
                field.put(r, weights(t, r) * value)

    field.forward(REACH, start, force, scaled=True)
    field.adjoint(STEPS, lambda t, r: tops[t][field.at(r)], std)
    sums = [jnp.zeros((COLS, L), F32) for _ in range(4)]
    for r in range(-STEPS, ROWS + STEPS):
        b = b_ref[r] if own(r) else padded(taken(more, SECOND, "b", r))
        q = b + field.get(r)
        field.put(r, q)
        if own(r):
            b, q = b[MIDDLE], q[MIDDLE]
            q_ref[r] = q
            for i, term in enumerate((b * b, b * q, q * q, q * q)):
                sums[i] = sums[i] + term
    field.mix(-STEPS, ROWS + STEPS, FACTOR)

    def keep(t, r, value):
        if own(r):
            forced = tile.weights(t, r) * value
            sums[3] = sums[3] + forced[MIDDLE] * value[MIDDLE]
            forced = inside(forced)
            g_ref[t, r] = forced
            for ref, h in ((low_ref, r + 1), (high_ref, ROWS - r)):
                if h <= t + 1:
                    begin, width = THIRD[("g", t), h]
                    ref[begin : begin + width] = forced

    field.forward(STEPS, lambda r: std(r) * field.get(r), keep)
    lane = lax.broadcasted_iota(jnp.int32, (1, L), 1)
    row = jnp.zeros((1, L), F32)
    for i, term in enumerate(sums):
        total = jnp.sum(jnp.sum(term, axis=0, keepdims=True), axis=1, keepdims=True)
        row = row + jnp.where(lane == i, total, 0.0)
    sums_ref[...] = jnp.broadcast_to(row, sums_ref.shape)


def second_image_kernel(*refs):
    tile, sides, m_ref = Tile(*refs[:6]), refs[6:8], refs[8]
    q_ref, g_ref = refs[9:11]
    more = refs[11:13]
    u_ref = refs[13]
    field = Field(INNER, STEPS, *refs[14:18], m_ref)
    field.fill_diffusion(tile, sides, STEPS)
    forcing = lambda t, r: g_ref[t, r] if own(r) else taken(more, THIRD, ("g", t), r)
    for r in range(-STEPS, ROWS + STEPS):
        field.put(r, forcing(STEPS - 1, r))
    field.adjoint(0, forcing, lambda r: inside(tile.std(r)))
    for r in range(ROWS):
        u_ref[r] = q_ref[r] + field.get(r)[EDGE : EDGE + COLS]


def levels(lat, lon):
    quarter = lat // 4
    near = [[i * quarter + k for k in range(quarter)] for i in range(4)]
    far = [[(i * quarter + k) * lon + j for i in range(4) for j in range(lon)] for k in range(quarter)]
    return near, far


def add_kernel(parts_ref, out_ref):
    out_ref[...] = jnp.broadcast_to(0.25 * jnp.sum(parts_ref[...], axis=0, keepdims=True), out_ref.shape)


def finish_kernel(parts_ref, b_ref, q_ref, u_ref, solution_ref, residual_ref):
    total = jnp.sum(parts_ref[...], axis=0, keepdims=True)
    bb, bq, qq, qu = (total[:, i : i + 1] for i in range(4))
    first = bb / bq
    norm = first * first * qq - bb
    gain = 1.0 + norm / bb
    curve = gain * gain * bq - 2.0 * first * gain * qq + first * first * qu
    second = norm / curve
    along_b = first + second * gain
    along_q = first * second
    for r in range(ROWS):
        b, q = b_ref[r, MIDDLE], q_ref[r]
        solution_ref[r] = along_b * b - along_q * q
        residual_ref[r] = b - along_b * q + along_q * u_ref[r]


def exchange(to_before, to_after, axis, wrap):
    size = lax.axis_size(axis)
    up = [(i, (i + 1) % size) for i in range(size if wrap else size - 1)]
    down = [(j, i) for i, j in up]
    return lax.ppermute(to_after, axis, up), lax.ppermute(to_before, axis, down)


def shards(
    departures, obs_weight, obs_columns, obs_owner, obs_counts, background_std, diffusion, level_factor, model_mixing
):
    parity = (lax.axis_index("lon") % 2).astype(jnp.int32).reshape(1)
    slots = pltpu.VMEM((SLOTS, L), F32)
    buckets = call(
        bucket_kernel,
        "bucket",
        shape(8, BUCKET, L),
        [slots, slots, pltpu.SemaphoreType.DMA((2,))],
        smem=(4, 5),
        hbm=(0, 1),
        vmem=60,
    )(departures, obs_weight, obs_columns.reshape(1, SLOTS), obs_owner.reshape(1, SLOTS), obs_counts, parity)
    received = lax.all_to_all(buckets, "lon", 0, 0)
    mats = call(matrices_kernel, "matrices", shape(4, 2 * L, 2 * L, dtype=BF16))(level_factor, model_mixing)
    fixed = call(fixed_kernel, "fixed", shape(CELLS + COLS, L))(background_std.reshape(CELLS, L), diffusion)
    fixed_left, fixed_right = exchange(fixed, fixed, "lon", True)
    beside = shape(PACKED + ROWS, L)
    tile, to_left, to_right = call(tile_kernel, "tile", (shape(2 * SIZE, L), beside, beside))(
        received, fixed_left, fixed_right
    )
    left, right = exchange(to_left, to_right, "lon", True)
    refs = (left, tile, right, fixed_left, fixed, fixed_right)
    side = shape(FIRST_ROWS, L)
    below, above = exchange(*call(sides_kernel, "sides", (side, side))(*refs), "lat", False)
    side = shape(WEIGHTS_ROWS, L)
    weights = exchange(*call(weights_kernel, "weights", (side, side))(*refs), "lat", False)
    refs = (*refs, below, above, mats)
    field, side = shape(ROWS, WIDE, L), shape(SECOND_ROWS, L)
    b, y, low, high = call(right_side_kernel, "right_side", (field, field, side, side), scratch(WIDE, STEPS + 1))(*refs)
    south, north = exchange(low, high, "lat", False)
    lat, lon = lax.axis_size("lat"), lax.axis_size("lon")
    near, far = levels(lat, lon)
    small, side = shape(ROWS, COLS, L), shape(THIRD_ROWS, L)
    space = scratch(WIDE, REACH)
    q, g, low, high, sums = call(
        first_image_kernel,
        "first_image",
        (small, shape(STEPS, ROWS, INNER, L), side, side, shape(lat, L)),
        space + [space[0]] * 2,
    )(*refs, b, y, south, north, *weights)
    sums = lax.all_to_all(sums, "lat", 0, 0, axis_index_groups=near, tiled=True)
    south, north = exchange(low, high, "lat", False)
    u = call(second_image_kernel, "second_image", small, scratch(INNER, STEPS))(*refs, q, g, south, north)
    sums = call(add_kernel, "add", shape(4 * lon, L))(sums)
    sums = lax.all_to_all(sums, ("lat", "lon"), 0, 0, axis_index_groups=far, tiled=True)
    return call(finish_kernel, "finish", (small, small))(sums, b, q, u)


def solution(mesh):
    placed = (
        P(("lat", "lon"), None),
        P(("lat", "lon"), None),
        P(("lat", "lon")),
        P(("lat", "lon"), None),
        P(("lat", "lon")),
        P("lat", "lon", None),
        P("lat", "lon"),
        P(),
        P(),
    )
    return jax.shard_map(
        shards,
        mesh=mesh,
        in_specs=placed,
        out_specs=(P("lat", "lon", None), P("lat", "lon", None)),
        check_vma=False,
    )
```

```python
import jax
import jax.numpy as jnp
from jax import lax
from jax.experimental import pallas as pl
from jax.experimental.pallas import tpu as pltpu
from jax.sharding import PartitionSpec as P

F32 = jnp.float32
BF16 = jnp.bfloat16
L = 128
ROWS = 8
COLS = 16
CELLS = ROWS * COLS
STEPS = 3
SLOTS = 256
CAP = 64
WIDE = 3 * COLS
INNER = 2 * COLS
EDGE = COLS // 2
BUCKET = 2 * CAP + 8
REACH = 3 * STEPS

MIB = 1024 * 1024


def call(kernel, name, outs, scratch=(), smem=(), hbm=(), vmem=40):
    def run(*args):
        spaces = [pltpu.SMEM if i in smem else pltpu.HBM if i in hbm else pltpu.VMEM for i in range(len(args))]
        specs = [pl.BlockSpec(memory_space=space) for space in spaces]
        return pl.pallas_call(
            kernel,
            name=name,
            out_shape=outs,
            in_specs=specs,
            out_specs=jax.tree.map(lambda _: pl.BlockSpec(memory_space=pltpu.VMEM), outs),
            scratch_shapes=scratch,
            compiler_params=pltpu.CompilerParams(vmem_limit_bytes=vmem * MIB),
        )(*args)

    return run


def shape(*dims, dtype=F32):
    return jax.ShapeDtypeStruct(dims, dtype)


def halves(x):
    high = x.astype(BF16)
    return high, (x - high.astype(F32)).astype(BF16)


def dot(a, b):
    return jnp.dot(a, b, preferred_element_type=F32)


def matrices_kernel(factor_ref, mixing_ref, out_ref):
    for i, ref in enumerate((mixing_ref, factor_ref)):
        for j in range(2):
            m = 0.5 * ref[...]
            high, low = halves(m.T if j else m)
            row = jnp.concatenate([high, low], axis=1)
            out_ref[2 * i + j] = jnp.concatenate([row, row], axis=0)


MIX, MIX_T, FACTOR, FACTOR_T = range(4)


def bucket_kernel(
    departures_hbm, weight_hbm, columns_ref, owner_ref, counts_ref, parity_ref, out_ref, departures_ref, weight_ref, sems
):
    copies = [
        pltpu.make_async_copy(departures_hbm, departures_ref, sems.at[0]),
        pltpu.make_async_copy(weight_hbm, weight_ref, sems.at[1]),
    ]
    for copy in copies:
        copy.start()
    sub = lax.broadcasted_iota(jnp.int32, (SLOTS, SLOTS), 0)
    lane = lax.broadcasted_iota(jnp.int32, (SLOTS, SLOTS), 1)
    owner_row = owner_ref[...].astype(F32)
    owner_col = jnp.sum(jnp.where(sub == lane, owner_row, 0.0), axis=1, keepdims=True)
    same = owner_row == owner_col
    rank_row = jnp.sum(jnp.where(same & (sub < lane), 1.0, 0.0), axis=0, keepdims=True)
    rank_col = jnp.sum(jnp.where(same & (lane < sub), 1.0, 0.0), axis=1, keepdims=True)
    place = (owner_row * CAP + rank_row).astype(jnp.int32)
    pick = lax.broadcasted_iota(jnp.int32, (8 * CAP, SLOTS), 0) == place
    pick = jnp.where(pick, 1.0, 0.0).astype(BF16)
    slot = lax.broadcasted_iota(jnp.int32, (SLOTS, L), 0)
    for copy in copies:
        copy.wait()
    weights = jnp.where(slot < counts_ref[0], weight_ref[...], 0.0)
    parts = halves(weights * departures_ref[...]) + halves(weights)
    moved = dot(pick, jnp.concatenate(parts, axis=1))
    forcing = moved[:, :L] + moved[:, L : 2 * L]
    weights = moved[:, 2 * L : 3 * L] + moved[:, 3 * L :]
    number = lax.broadcasted_iota(jnp.int32, (1, SLOTS), 1)
    time = (number - STEPS * ((number * 171) >> 9)).astype(F32)
    tile = lax.broadcasted_iota(jnp.int32, (8, SLOTS), 0).astype(F32)
    here = tile == owner_row
    marks = jnp.concatenate(
        [jnp.where(here, time, 0.0), jnp.where(here, columns_ref[...].astype(F32), 0.0)], axis=0
    )
    target = rank_col + (CAP * parity_ref[0]).astype(F32)
    spread = jnp.where(lax.broadcasted_iota(jnp.int32, (SLOTS, L), 1).astype(F32) == target, 1.0, 0.0)
    codes = dot(marks.astype(BF16), spread.astype(BF16))
    codes = CELLS * codes[:8] + codes[8:]
    for d in range(8):
        out_ref[d, :CAP] = forcing[d * CAP : (d + 1) * CAP]
        out_ref[d, CAP : 2 * CAP] = weights[d * CAP : (d + 1) * CAP]
        out_ref[d, 2 * CAP :] = jnp.broadcast_to(codes[d : d + 1], (8, L))


def fixed_kernel(std_ref, diffusion_ref, out_ref):
    out_ref[:CELLS] = std_ref[...]
    sub = lax.broadcasted_iota(jnp.int32, (COLS, COLS), 0)
    lane = lax.broadcasted_iota(jnp.int32, (COLS, COLS), 1)
    place = lax.broadcasted_iota(jnp.int32, (COLS, L), 1)
    turned = jnp.zeros((COLS, L), F32)
    for r in range(ROWS):
        row = diffusion_ref[r : r + 1]
        column = jnp.sum(jnp.where(sub == lane, row, 0.0), axis=1, keepdims=True)
        turned = turned + jnp.where(place == r, column, 0.0)
    out_ref[CELLS:] = turned


SIZE = STEPS * CELLS
PACKED = SIZE + STEPS * ROWS * EDGE


def tile_kernel(received_ref, fixed_left_ref, fixed_right_ref, own_ref, to_left_ref, to_right_ref):
    ones, data = [], []
    cell = lax.broadcasted_iota(jnp.int32, (SIZE, L), 0)
    for j in range(4):
        pair = (2 * j, 2 * j + 1)
        codes = sum(received_ref[s, 2 * CAP : 2 * CAP + 1] for s in pair).astype(jnp.int32)
        ones.append(jnp.where(cell == codes, 1.0, 0.0).astype(BF16))
        for s in pair:
            parts = halves(received_ref[s, :CAP]) + halves(received_ref[s, CAP : 2 * CAP])
            data.append(jnp.concatenate(parts, axis=1))
    total = dot(jnp.concatenate(ones, axis=1), jnp.concatenate(data, axis=0))
    forcing = total[:, :L] + total[:, L : 2 * L]
    weights = total[:, 2 * L : 3 * L] + total[:, 3 * L :]
    for ref in (own_ref, to_left_ref, to_right_ref):
        ref[:SIZE] = forcing
    own_ref[SIZE:] = weights
    for k in range(STEPS * ROWS):
        to = pl.ds(SIZE + k * EDGE, EDGE)
        to_left_ref[to] = weights[k * COLS : k * COLS + EDGE]
        to_right_ref[to] = weights[k * COLS + EDGE : (k + 1) * COLS]
    for r in range(ROWS):
        first = (STEPS - 1) * CELLS + r * COLS
        to_left_ref[PACKED + r : PACKED + r + 1] = weights[first + EDGE : first + EDGE + 1]
        to_right_ref[PACKED + r : PACKED + r + 1] = weights[first + EDGE - 1 : first + EDGE]


def wide(refs, start):
    return jnp.concatenate([ref[start : start + COLS] for ref in refs], axis=0)


class Tile:
    def __init__(self, left_ref, own_ref, right_ref, fixed_left_ref, fixed_ref, fixed_right_ref):
        self.left, self.own, self.right = left_ref, own_ref, right_ref
        self.fixed = (fixed_left_ref, fixed_ref, fixed_right_ref)

    def forcing(self, t, r):
        return wide((self.left, self.own, self.right), t * CELLS + r * COLS)

    def inner_weights(self, t, r):
        start = SIZE + t * CELLS + r * COLS
        packed = pl.ds(SIZE + (t * ROWS + r) * EDGE, EDGE)
        return [self.left[packed], self.own[start : start + COLS], self.right[packed]]

    def weights(self, t, r):
        inner = self.inner_weights(t, r)
        if t < STEPS - 1:
            edges = [jnp.zeros((EDGE, L), F32)] * 2
        else:
            edges = [jnp.broadcast_to(ref[PACKED + r : PACKED + r + 1], (EDGE, L)) for ref in (self.left, self.right)]
        return jnp.concatenate([edges[0], *inner, edges[1]], axis=0)

    def std(self, r):
        return wide(self.fixed, r * COLS)

    def turned(self):
        return wide(self.fixed, CELLS)


def inside(row):
    return row[EDGE : EDGE + INNER]


def padded(row):
    if row.shape[0] == WIDE:
        return row
    edge = jnp.zeros((EDGE, L), F32)
    return jnp.concatenate([edge, row, edge], axis=0)


def places(rows):
    found, total = {}, 0
    for kind, h, width in rows:
        found[kind, h] = (total, width)
        total += width
    return found, total


FIRST, FIRST_ROWS = places(
    [(("f", t), h, WIDE if h < t + 2 else INNER) for t in range(STEPS) for h in range(1, t + 3)]
    + [("std", h, INNER) for h in range(1, STEPS + 1)]
    + [("diffusion", 1, WIDE)]
)
SECOND, SECOND_ROWS = places(
    [("state", h, WIDE if h <= STEPS else INNER) for h in range(1, REACH + 1)]
    + [("b", h, INNER) for h in range(1, STEPS + 1)]
)
WEIGHTS, WEIGHTS_ROWS = places([(("w", t), h, INNER) for t in range(STEPS) for h in range(1, t + 5)])
THIRD, THIRD_ROWS = places([(("g", t), h, INNER) for t in range(STEPS) for h in range(1, t + 2)])


class Sides:
    def __init__(self, parity_ref, core_ref, chip_ref, found):
        self.even = parity_ref[0] == 0
        self.core_ref, self.chip_ref, self.found = core_ref, chip_ref, found

    def send(self, kind, h, row):
        start, width = self.found[kind, h]
        values = [row(r) for r in (h - 1, ROWS - h)]
        low, high = [inside(v) if width < v.shape[0] else v for v in values]
        self.core_ref[start : start + width] = jnp.where(self.even, high, low)
        self.chip_ref[start : start + width] = jnp.where(self.even, low, high)

    def taken(self, kind, r):
        start, width = self.found[kind, -r if r < 0 else r - ROWS + 1]
        core, chip = self.core_ref[start : start + width], self.chip_ref[start : start + width]
        return jnp.where(self.even, chip, core) if r < 0 else jnp.where(self.even, core, chip)


def sides_kernel(*refs):
    tile, sides = Tile(*refs[1:7]), Sides(refs[0], *refs[7:], FIRST)
    for kind, h in FIRST:
        if kind == "std":
            row = tile.std
        elif kind == "diffusion":
            row = lambda r: tile.turned()
        else:
            row = lambda r: tile.forcing(kind[1], r)
        sides.send(kind, h, row)


def weights_kernel(*refs):
    tile, sides = Tile(*refs[1:7]), Sides(refs[0], *refs[7:], WEIGHTS)
    for kind, h in WEIGHTS:
        sides.send(kind, h, lambda r: jnp.concatenate(tile.inner_weights(kind[1], r), axis=0))


def own(r):
    return 0 <= r < ROWS


class Field:
    def __init__(self, width, reach, v_ref, x_ref, y_ref, d_ref, m_ref):
        self.width, self.reach = width, reach
        self.v_ref, self.x_ref, self.y_ref, self.d_ref, self.m_ref = v_ref, x_ref, y_ref, d_ref, m_ref

    def at(self, r):
        return pl.ds((r + self.reach) * self.width, self.width)

    def put(self, r, value):
        self.v_ref[self.at(r)] = value
        high, low = halves(value)
        self.x_ref[self.at(r), :L] = high
        self.x_ref[self.at(r), L:] = low

    def mix(self, first, stop, which):
        rows = pl.ds((first + self.reach) * self.width, (stop - first) * self.width)
        self.y_ref[rows] = dot(self.x_ref[rows], self.m_ref[which])

    def get(self, r):
        return self.v_ref[self.at(r)] + self.y_ref[self.at(r), :L] + self.y_ref[self.at(r), L:]

    def fill_diffusion(self, tile, sides, reach):
        values = {0: tile.turned(), -1: sides.taken("diffusion", -1), 1: sides.taken("diffusion", ROWS)}
        skip = (WIDE - self.width) // 2
        for r in range(-reach, ROWS + reach):
            column = values[r // ROWS][skip : skip + self.width, r % ROWS : r % ROWS + 1]
            self.d_ref[self.at(r)] = jnp.broadcast_to(column, (self.width, L))

    def smooth(self, first, stop, get, put, scaled=False):
        held = []
        for r in range(first, stop):
            value = get(r)
            if scaled and r in (first, stop - 1):
                held.append((value, None, value))
            else:
                d = self.d_ref[self.at(r)]
                held.append((value, d, d * value))
            if len(held) == 3:
                value, d, u = held[1]
                around = held[0][2] + held[2][2] + pltpu.roll(u, 1, 0) + pltpu.roll(u, self.width - 1, 0)
                put(r - 1, value + d * (around - 4.0 * u))
                held.pop(0)

    def forward(self, h, start, seen, scaled=False):
        self.smooth(-h, ROWS + h, start, self.put, scaled)
        for t in range(STEPS):
            first, stop = -h + t + 1, ROWS + h - t - 1
            self.mix(first, stop, MIX)

            def get(r, t=t):
                value = self.get(r)
                seen(t, r, value)
                return value

            if t < STEPS - 1:
                self.smooth(first, stop, get, self.put)
            else:
                for r in range(first, stop):
                    get(r)

    def adjoint(self, h, forcing, std):
        for t in range(STEPS - 1, -1, -1):
            first, stop = -h - t - 1, ROWS + h + t + 1
            self.mix(first, stop, MIX_T)
            if t > 0:
                put = lambda r, value, t=t: self.put(r, value + forcing(t - 1, r))
            else:
                put = lambda r, value: self.put(r, std(r) * value)
            self.smooth(first, stop, self.get, put)
        self.mix(-h, ROWS + h, FACTOR_T)


def scratch(width, reach):
    tall = (ROWS + 2 * reach) * width
    return [
        pltpu.VMEM((tall, L), F32),
        pltpu.VMEM((tall, 2 * L), BF16),
        pltpu.VMEM((tall, 2 * L), F32),
        pltpu.VMEM((tall, L), F32),
    ]


def std_rows(tile, sides):
    return lambda r: tile.std(r) if own(r) else padded(sides.taken("std", r))


def right_side_kernel(parity_ref, *refs):
    tile, sides, m_ref = Tile(*refs[:6]), Sides(parity_ref, *refs[6:8], FIRST), refs[8]
    b_ref, y_ref = refs[9:11]
    out = Sides(parity_ref, *refs[11:13], SECOND)
    field = Field(WIDE, STEPS + 1, *refs[13:17], m_ref)
    field.fill_diffusion(tile, sides, STEPS + 1)
    forcing = lambda t, r: tile.forcing(t, r) if own(r) else padded(sides.taken(("f", t), r))
    std = std_rows(tile, sides)
    for r in range(-STEPS - 1, ROWS + STEPS + 1):
        field.put(r, forcing(STEPS - 1, r))
    field.adjoint(1, forcing, std)
    for r in range(-1, ROWS + 1):
        value = field.get(r)
        field.put(r, value)
        if own(r):
            b_ref[r] = value
    field.mix(-1, ROWS + 1, FACTOR)
    beyond = {}
    for r in range(-1, ROWS + 1):
        state = std(r) * field.get(r)
        if own(r):
            y_ref[r] = state
        else:
            beyond[r] = field.d_ref[field.at(r)] * state
    for kind, h in SECOND:
        out.send(kind, h, lambda r: b_ref[r] if kind == "b" else y_ref[r] if own(r) else beyond[r])


MIDDLE = slice(COLS, 2 * COLS)


def first_image_kernel(parity_ref, *refs):
    tile, sides, m_ref = Tile(*refs[:6]), Sides(parity_ref, *refs[6:8], FIRST), refs[8]
    b_ref, y_ref = refs[9:11]
    more, forced = Sides(parity_ref, *refs[11:13], SECOND), Sides(parity_ref, *refs[13:15], WEIGHTS)
    q_ref, g_ref = refs[15:17]
    out, sums_ref = Sides(parity_ref, *refs[17:19], THIRD), refs[19]
    field = Field(WIDE, REACH, *refs[20:24], m_ref)
    tops = refs[24:26]
    field.fill_diffusion(tile, sides, REACH - 1)
    std = std_rows(tile, sides)

    def weights(t, r):
        return tile.weights(t, r) if own(r) else padded(forced.taken(("w", t), r))

    def start(r):
        if own(r):
            return y_ref[r]
        return padded(more.taken("state", r))

    def force(t, r, value):
        if -t - 4 <= r < ROWS + t + 4:
            if t < STEPS - 1:
                tops[t][field.at(r)] = weights(t, r) * value
            else:
                field.put(r, weights(t, r) * value)

    field.forward(REACH, start, force, scaled=True)
    field.adjoint(STEPS, lambda t, r: tops[t][field.at(r)], std)
    sums = [jnp.zeros((COLS, L), F32) for _ in range(4)]
    for r in range(-STEPS, ROWS + STEPS):
        b = b_ref[r] if own(r) else padded(more.taken("b", r))
        q = b + field.get(r)
        field.put(r, q)
        if own(r):
            b, q = b[MIDDLE], q[MIDDLE]
            q_ref[r] = q
            for i, term in enumerate((b * b, b * q, q * q, q * q)):
                sums[i] = sums[i] + term
    field.mix(-STEPS, ROWS + STEPS, FACTOR)

    def keep(t, r, value):
        if own(r):
            forcing = tile.weights(t, r) * value
            sums[3] = sums[3] + forcing[MIDDLE] * value[MIDDLE]
            g_ref[t, r] = inside(forcing)

    field.forward(STEPS, lambda r: std(r) * field.get(r), keep)
    for kind, h in THIRD:
        out.send(kind, h, lambda r: g_ref[kind[1], r])
    lane = lax.broadcasted_iota(jnp.int32, (1, L), 1)
    row = jnp.zeros((1, L), F32)
    for i, term in enumerate(sums):
        total = jnp.sum(jnp.sum(term, axis=0, keepdims=True), axis=1, keepdims=True)
        row = row + jnp.where(lane == i, total, 0.0)
    sums_ref[...] = jnp.broadcast_to(row, sums_ref.shape)


def second_image_kernel(parity_ref, *refs):
    tile, sides, m_ref = Tile(*refs[:6]), Sides(parity_ref, *refs[6:8], FIRST), refs[8]
    q_ref, g_ref = refs[9:11]
    more = Sides(parity_ref, *refs[11:13], THIRD)
    u_ref = refs[13]
    field = Field(INNER, STEPS, *refs[14:18], m_ref)
    field.fill_diffusion(tile, sides, STEPS)
    forcing = lambda t, r: g_ref[t, r] if own(r) else more.taken(("g", t), r)
    for r in range(-STEPS, ROWS + STEPS):
        field.put(r, forcing(STEPS - 1, r))
    field.adjoint(0, forcing, lambda r: inside(tile.std(r)))
    for r in range(ROWS):
        u_ref[r] = q_ref[r] + field.get(r)[EDGE : EDGE + COLS]


def levels(lat, lon):
    quarter = lat // 4
    near = [[i * quarter + k for k in range(quarter)] for i in range(4)]
    far = [[(i * quarter + k) * lon + j for i in range(4) for j in range(lon)] for k in range(quarter)]
    return near, far


def add_kernel(parts_ref, out_ref):
    out_ref[...] = jnp.broadcast_to(0.25 * jnp.sum(parts_ref[...], axis=0, keepdims=True), out_ref.shape)


def finish_kernel(parts_ref, b_ref, q_ref, u_ref, solution_ref, residual_ref):
    total = jnp.sum(parts_ref[...], axis=0, keepdims=True)
    bb, bq, qq, qu = (total[:, i : i + 1] for i in range(4))
    first = bb / bq
    norm = first * first * qq - bb
    gain = 1.0 + norm / bb
    curve = gain * gain * bq - 2.0 * first * gain * qq + first * first * qu
    second = norm / curve
    along_b = first + second * gain
    along_q = first * second
    for r in range(ROWS):
        b, q = b_ref[r, MIDDLE], q_ref[r]
        solution_ref[r] = along_b * b - along_q * q
        residual_ref[r] = b - along_b * q + along_q * u_ref[r]


def exchange(to_before, to_after):
    size = lax.axis_size("lon")
    up = [(i, (i + 1) % size) for i in range(size)]
    down = [(j, i) for i, j in up]
    return lax.ppermute(to_after, "lon", up), lax.ppermute(to_before, "lon", down)


def swap(core, chip):
    size = lax.axis_size("lat")
    pairs = [[(i, i + 1) for i in range(first, size - 1, 2)] for first in (0, 1)]
    both = [p + [(j, i) for i, j in p] for p in pairs]
    return lax.ppermute(core, "lat", both[0]), lax.ppermute(chip, "lat", both[1])


def shards(
    departures, obs_weight, obs_columns, obs_owner, obs_counts, background_std, diffusion, level_factor, model_mixing
):
    parity = (lax.axis_index("lon") % 2).astype(jnp.int32).reshape(1)
    side_of = (lax.axis_index("lat") % 2).astype(jnp.int32).reshape(1)
    slots = pltpu.VMEM((SLOTS, L), F32)
    buckets = call(
        bucket_kernel,
        "bucket",
        shape(8, BUCKET, L),
        [slots, slots, pltpu.SemaphoreType.DMA((2,))],
        smem=(4, 5),
        hbm=(0, 1),
        vmem=60,
    )(departures, obs_weight, obs_columns.reshape(1, SLOTS), obs_owner.reshape(1, SLOTS), obs_counts, parity)
    received = lax.all_to_all(buckets, "lon", 0, 0)
    mats = call(matrices_kernel, "matrices", shape(4, 2 * L, 2 * L, dtype=BF16))(level_factor, model_mixing)
    fixed = call(fixed_kernel, "fixed", shape(CELLS + COLS, L))(background_std.reshape(CELLS, L), diffusion)
    fixed_left, fixed_right = exchange(fixed, fixed)
    beside = shape(PACKED + ROWS, L)
    tile, to_left, to_right = call(tile_kernel, "tile", (shape(2 * SIZE, L), beside, beside))(
        received, fixed_left, fixed_right
    )
    left, right = exchange(to_left, to_right)
    refs = (left, tile, right, fixed_left, fixed, fixed_right)
    side = shape(FIRST_ROWS, L)
    below, above = swap(*call(sides_kernel, "sides", (side, side), smem=(0,))(side_of, *refs))
    side = shape(WEIGHTS_ROWS, L)
    weights = swap(*call(weights_kernel, "weights", (side, side), smem=(0,))(side_of, *refs))
    refs = (*refs, below, above, mats)
    field, side = shape(ROWS, WIDE, L), shape(SECOND_ROWS, L)
    b, y, low, high = call(right_side_kernel, "right_side", (field, field, side, side), scratch(WIDE, STEPS + 1), smem=(0,))(
        side_of, *refs
    )
    south, north = swap(low, high)
    lat, lon = lax.axis_size("lat"), lax.axis_size("lon")
    near, far = levels(lat, lon)
    small, side = shape(ROWS, COLS, L), shape(THIRD_ROWS, L)
    space = scratch(WIDE, REACH)
    q, g, low, high, sums = call(
        first_image_kernel,
        "first_image",
        (small, shape(STEPS, ROWS, INNER, L), side, side, shape(lat, L)),
        space + [space[0]] * 2,
        smem=(0,),
    )(side_of, *refs, b, y, south, north, *weights)
    sums = lax.all_to_all(sums, "lat", 0, 0, axis_index_groups=near, tiled=True)
    south, north = swap(low, high)
    u = call(second_image_kernel, "second_image", small, scratch(INNER, STEPS), smem=(0,))(
        side_of, *refs, q, g, south, north
    )
    sums = call(add_kernel, "add", shape(4 * lon, L))(sums)
    sums = lax.all_to_all(sums, ("lat", "lon"), 0, 0, axis_index_groups=far, tiled=True)
    return call(finish_kernel, "finish", (small, small))(sums, b, q, u)


def solution(mesh):
    placed = (
        P(("lat", "lon"), None),
        P(("lat", "lon"), None),
        P(("lat", "lon")),
        P(("lat", "lon"), None),
        P(("lat", "lon")),
        P("lat", "lon", None),
        P("lat", "lon"),
        P(),
        P(),
    )
    return jax.shard_map(
        shards,
        mesh=mesh,
        in_specs=placed,
        out_specs=(P("lat", "lon", None), P("lat", "lon", None)),
        check_vma=False,
    )
```

```python
import jax
import jax.numpy as jnp
from jax import lax
from jax.experimental import pallas as pl
from jax.experimental.pallas import tpu as pltpu
from jax.sharding import PartitionSpec as P

F32 = jnp.float32
BF16 = jnp.bfloat16
L = 128
ROWS = 8
COLS = 16
CELLS = ROWS * COLS
STEPS = 3
SLOTS = 256
CAP = 64
WIDE = 3 * COLS
INNER = 2 * COLS
EDGE = COLS // 2
BUCKET = 2 * CAP + 8
REACH = 3 * STEPS

MIB = 1024 * 1024


def call(kernel, name, outs, scratch=(), smem=(), hbm=(), vmem=40):
    def run(*args):
        spaces = [pltpu.SMEM if i in smem else pltpu.HBM if i in hbm else pltpu.VMEM for i in range(len(args))]
        specs = [pl.BlockSpec(memory_space=space) for space in spaces]
        return pl.pallas_call(
            kernel,
            name=name,
            out_shape=outs,
            in_specs=specs,
            out_specs=jax.tree.map(lambda _: pl.BlockSpec(memory_space=pltpu.VMEM), outs),
            scratch_shapes=scratch,
            compiler_params=pltpu.CompilerParams(vmem_limit_bytes=vmem * MIB),
        )(*args)

    return run


def shape(*dims, dtype=F32):
    return jax.ShapeDtypeStruct(dims, dtype)


def halves(x):
    high = x.astype(BF16)
    return high, (x - high.astype(F32)).astype(BF16)


def dot(a, b):
    return jnp.dot(a, b, preferred_element_type=F32)


def matrices_kernel(factor_ref, mixing_ref, out_ref):
    for i, ref in enumerate((mixing_ref, factor_ref)):
        for j in range(2):
            m = 0.5 * ref[...]
            high, low = halves(m.T if j else m)
            row = jnp.concatenate([high, low], axis=1)
            out_ref[2 * i + j] = jnp.concatenate([row, row], axis=0)


MIX, MIX_T, FACTOR, FACTOR_T = range(4)


def bucket_kernel(
    departures_hbm, weight_hbm, columns_ref, owner_ref, counts_ref, parity_ref, out_ref, departures_ref, weight_ref, sems
):
    copies = [
        pltpu.make_async_copy(departures_hbm, departures_ref, sems.at[0]),
        pltpu.make_async_copy(weight_hbm, weight_ref, sems.at[1]),
    ]
    for copy in copies:
        copy.start()
    sub = lax.broadcasted_iota(jnp.int32, (SLOTS, SLOTS), 0)
    lane = lax.broadcasted_iota(jnp.int32, (SLOTS, SLOTS), 1)
    owner_row = owner_ref[...].astype(F32)
    owner_col = jnp.sum(jnp.where(sub == lane, owner_row, 0.0), axis=1, keepdims=True)
    same = owner_row == owner_col
    rank_row = jnp.sum(jnp.where(same & (sub < lane), 1.0, 0.0), axis=0, keepdims=True)
    rank_col = jnp.sum(jnp.where(same & (lane < sub), 1.0, 0.0), axis=1, keepdims=True)
    place = (owner_row * CAP + rank_row).astype(jnp.int32)
    pick = lax.broadcasted_iota(jnp.int32, (8 * CAP, SLOTS), 0) == place
    pick = jnp.where(pick, 1.0, 0.0).astype(BF16)
    slot = lax.broadcasted_iota(jnp.int32, (SLOTS, L), 0)
    for copy in copies:
        copy.wait()
    weights = jnp.where(slot < counts_ref[0], weight_ref[...], 0.0)
    parts = halves(weights * departures_ref[...]) + halves(weights)
    moved = dot(pick, jnp.concatenate(parts, axis=1))
    forcing = moved[:, :L] + moved[:, L : 2 * L]
    weights = moved[:, 2 * L : 3 * L] + moved[:, 3 * L :]
    number = lax.broadcasted_iota(jnp.int32, (1, SLOTS), 1)
    time = (number - STEPS * ((number * 171) >> 9)).astype(F32)
    tile = lax.broadcasted_iota(jnp.int32, (8, SLOTS), 0).astype(F32)
    here = tile == owner_row
    marks = jnp.concatenate(
        [jnp.where(here, time, 0.0), jnp.where(here, columns_ref[...].astype(F32), 0.0)], axis=0
    )
    target = rank_col + (CAP * parity_ref[0]).astype(F32)
    spread = jnp.where(lax.broadcasted_iota(jnp.int32, (SLOTS, L), 1).astype(F32) == target, 1.0, 0.0)
    codes = dot(marks.astype(BF16), spread.astype(BF16))
    codes = CELLS * codes[:8] + codes[8:]
    for d in range(8):
        out_ref[d, :CAP] = forcing[d * CAP : (d + 1) * CAP]
        out_ref[d, CAP : 2 * CAP] = weights[d * CAP : (d + 1) * CAP]
        out_ref[d, 2 * CAP :] = jnp.broadcast_to(codes[d : d + 1], (8, L))


def fixed_kernel(std_ref, diffusion_ref, out_ref):
    out_ref[:CELLS] = std_ref[...]
    sub = lax.broadcasted_iota(jnp.int32, (COLS, COLS), 0)
    lane = lax.broadcasted_iota(jnp.int32, (COLS, COLS), 1)
    place = lax.broadcasted_iota(jnp.int32, (COLS, L), 1)
    turned = jnp.zeros((COLS, L), F32)
    for r in range(ROWS):
        row = diffusion_ref[r : r + 1]
        column = jnp.sum(jnp.where(sub == lane, row, 0.0), axis=1, keepdims=True)
        turned = turned + jnp.where(place == r, column, 0.0)
    out_ref[CELLS:] = turned


SIZE = STEPS * CELLS
PACKED = SIZE + STEPS * ROWS * EDGE


def tile_kernel(received_ref, fixed_left_ref, fixed_right_ref, own_ref, to_left_ref, to_right_ref):
    ones, data = [], []
    cell = lax.broadcasted_iota(jnp.int32, (SIZE, L), 0)
    for j in range(4):
        pair = (2 * j, 2 * j + 1)
        codes = sum(received_ref[s, 2 * CAP : 2 * CAP + 1] for s in pair).astype(jnp.int32)
        ones.append(jnp.where(cell == codes, 1.0, 0.0).astype(BF16))
        for s in pair:
            parts = halves(received_ref[s, :CAP]) + halves(received_ref[s, CAP : 2 * CAP])
            data.append(jnp.concatenate(parts, axis=1))
    total = dot(jnp.concatenate(ones, axis=1), jnp.concatenate(data, axis=0))
    forcing = total[:, :L] + total[:, L : 2 * L]
    weights = total[:, 2 * L : 3 * L] + total[:, 3 * L :]
    for ref in (own_ref, to_left_ref, to_right_ref):
        ref[:SIZE] = forcing
    own_ref[SIZE:] = weights
    for k in range(STEPS * ROWS):
        to = pl.ds(SIZE + k * EDGE, EDGE)
        to_left_ref[to] = weights[k * COLS : k * COLS + EDGE]
        to_right_ref[to] = weights[k * COLS + EDGE : (k + 1) * COLS]
    for r in range(ROWS):
        first = (STEPS - 1) * CELLS + r * COLS
        to_left_ref[PACKED + r : PACKED + r + 1] = weights[first + EDGE : first + EDGE + 1]
        to_right_ref[PACKED + r : PACKED + r + 1] = weights[first + EDGE - 1 : first + EDGE]


def wide(refs, start):
    return jnp.concatenate([ref[start : start + COLS] for ref in refs], axis=0)


class Tile:
    def __init__(self, left_ref, own_ref, right_ref, fixed_left_ref, fixed_ref, fixed_right_ref):
        self.left, self.own, self.right = left_ref, own_ref, right_ref
        self.fixed = (fixed_left_ref, fixed_ref, fixed_right_ref)

    def forcing(self, t, r):
        return wide((self.left, self.own, self.right), t * CELLS + r * COLS)

    def inner_weights(self, t, r):
        start = SIZE + t * CELLS + r * COLS
        packed = pl.ds(SIZE + (t * ROWS + r) * EDGE, EDGE)
        return [self.left[packed], self.own[start : start + COLS], self.right[packed]]

    def weights(self, t, r):
        inner = self.inner_weights(t, r)
        if t < STEPS - 1:
            edges = [jnp.zeros((EDGE, L), F32)] * 2
        else:
            edges = [jnp.broadcast_to(ref[PACKED + r : PACKED + r + 1], (EDGE, L)) for ref in (self.left, self.right)]
        return jnp.concatenate([edges[0], *inner, edges[1]], axis=0)

    def std(self, r):
        return wide(self.fixed, r * COLS)

    def turned(self):
        return wide(self.fixed, CELLS)


def inside(row):
    return row[EDGE : EDGE + INNER]


def padded(row):
    if row.shape[0] == WIDE:
        return row
    edge = jnp.zeros((EDGE, L), F32)
    return jnp.concatenate([edge, row, edge], axis=0)


def places(rows):
    found, total = {}, 0
    for kind, h, width in rows:
        found[kind, h] = (total, width)
        total += width
    return found, total


FIRST, FIRST_ROWS = places(
    [(("f", t), h, WIDE if h < t + 2 else INNER) for t in range(STEPS) for h in range(1, t + 3)]
    + [("std", h, INNER) for h in range(1, STEPS + 1)]
    + [("diffusion", 1, WIDE)]
)
SECOND, SECOND_ROWS = places(
    [("state", h, WIDE if h <= STEPS else INNER) for h in range(1, REACH + 1)]
    + [("b", h, INNER) for h in range(1, STEPS + 1)]
)
WEIGHTS, WEIGHTS_ROWS = places([(("w", t), h, INNER) for t in range(STEPS) for h in range(1, t + 5)])
THIRD, THIRD_ROWS = places([(("g", t), h, INNER) for t in range(STEPS) for h in range(1, t + 2)])


class Sides:
    def __init__(self, parity_ref, chip_ref, core_ref, found):
        self.even = parity_ref[0] == 0
        self.core_ref, self.chip_ref, self.found = core_ref, chip_ref, found

    def send(self, kind, h, row):
        start, width = self.found[kind, h]
        values = [row(r) for r in (h - 1, ROWS - h)]
        low, high = [inside(v) if width < v.shape[0] else v for v in values]
        self.core_ref[start : start + width] = jnp.where(self.even, high, low)
        self.chip_ref[start : start + width] = jnp.where(self.even, low, high)

    def taken(self, kind, r):
        start, width = self.found[kind, -r if r < 0 else r - ROWS + 1]
        core, chip = self.core_ref[start : start + width], self.chip_ref[start : start + width]
        return jnp.where(self.even, chip, core) if r < 0 else jnp.where(self.even, core, chip)


def sides_kernel(*refs):
    tile, sides = Tile(*refs[1:7]), Sides(refs[0], *refs[7:], FIRST)
    for kind, h in FIRST:
        if kind == "std":
            row = tile.std
        elif kind == "diffusion":
            row = lambda r: tile.turned()
        else:
            row = lambda r: tile.forcing(kind[1], r)
        sides.send(kind, h, row)


def weights_kernel(*refs):
    tile, sides = Tile(*refs[1:7]), Sides(refs[0], *refs[7:], WEIGHTS)
    for kind, h in WEIGHTS:
        sides.send(kind, h, lambda r: jnp.concatenate(tile.inner_weights(kind[1], r), axis=0))


def own(r):
    return 0 <= r < ROWS


class Field:
    def __init__(self, width, reach, v_ref, x_ref, y_ref, d_ref, m_ref):
        self.width, self.reach = width, reach
        self.v_ref, self.x_ref, self.y_ref, self.d_ref, self.m_ref = v_ref, x_ref, y_ref, d_ref, m_ref

    def at(self, r):
        return pl.ds((r + self.reach) * self.width, self.width)

    def put(self, r, value):
        self.v_ref[self.at(r)] = value
        high, low = halves(value)
        self.x_ref[self.at(r), :L] = high
        self.x_ref[self.at(r), L:] = low

    def mix(self, first, stop, which):
        rows = pl.ds((first + self.reach) * self.width, (stop - first) * self.width)
        self.y_ref[rows] = dot(self.x_ref[rows], self.m_ref[which])

    def get(self, r):
        return self.v_ref[self.at(r)] + self.y_ref[self.at(r), :L] + self.y_ref[self.at(r), L:]

    def fill_diffusion(self, tile, sides, reach):
        values = {0: tile.turned(), -1: sides.taken("diffusion", -1), 1: sides.taken("diffusion", ROWS)}
        skip = (WIDE - self.width) // 2
        for r in range(-reach, ROWS + reach):
            column = values[r // ROWS][skip : skip + self.width, r % ROWS : r % ROWS + 1]
            self.d_ref[self.at(r)] = jnp.broadcast_to(column, (self.width, L))

    def smooth(self, first, stop, get, put, scaled=False):
        held = []
        for r in range(first, stop):
            value = get(r)
            if scaled and r in (first, stop - 1):
                held.append((value, None, value))
            else:
                d = self.d_ref[self.at(r)]
                held.append((value, d, d * value))
            if len(held) == 3:
                value, d, u = held[1]
                around = held[0][2] + held[2][2] + pltpu.roll(u, 1, 0) + pltpu.roll(u, self.width - 1, 0)
                put(r - 1, value + d * (around - 4.0 * u))
                held.pop(0)

    def forward(self, h, start, seen, scaled=False):
        self.smooth(-h, ROWS + h, start, self.put, scaled)
        for t in range(STEPS):
            first, stop = -h + t + 1, ROWS + h - t - 1
            self.mix(first, stop, MIX)

            def get(r, t=t):
                value = self.get(r)
                seen(t, r, value)
                return value

            if t < STEPS - 1:
                self.smooth(first, stop, get, self.put)
            else:
                for r in range(first, stop):
                    get(r)

    def adjoint(self, h, forcing, std):
        for t in range(STEPS - 1, -1, -1):
            first, stop = -h - t - 1, ROWS + h + t + 1
            self.mix(first, stop, MIX_T)
            if t > 0:
                put = lambda r, value, t=t: self.put(r, value + forcing(t - 1, r))
            else:
                put = lambda r, value: self.put(r, std(r) * value)
            self.smooth(first, stop, self.get, put)
        self.mix(-h, ROWS + h, FACTOR_T)


def scratch(width, reach):
    tall = (ROWS + 2 * reach) * width
    return [
        pltpu.VMEM((tall, L), F32),
        pltpu.VMEM((tall, 2 * L), BF16),
        pltpu.VMEM((tall, 2 * L), F32),
        pltpu.VMEM((tall, L), F32),
    ]


def std_rows(tile, sides):
    return lambda r: tile.std(r) if own(r) else padded(sides.taken("std", r))


def right_side_kernel(parity_ref, *refs):
    tile, sides, m_ref = Tile(*refs[:6]), Sides(parity_ref, *refs[6:8], FIRST), refs[8]
    b_ref, y_ref = refs[9:11]
    out = Sides(parity_ref, *refs[11:13], SECOND)
    field = Field(WIDE, STEPS + 1, *refs[13:17], m_ref)
    field.fill_diffusion(tile, sides, STEPS + 1)
    forcing = lambda t, r: tile.forcing(t, r) if own(r) else padded(sides.taken(("f", t), r))
    std = std_rows(tile, sides)
    for r in range(-STEPS - 1, ROWS + STEPS + 1):
        field.put(r, forcing(STEPS - 1, r))
    field.adjoint(1, forcing, std)
    for r in range(-1, ROWS + 1):
        value = field.get(r)
        field.put(r, value)
        if own(r):
            b_ref[r] = value
    field.mix(-1, ROWS + 1, FACTOR)
    beyond = {}
    for r in range(-1, ROWS + 1):
        state = std(r) * field.get(r)
        if own(r):
            y_ref[r] = state
        else:
            beyond[r] = field.d_ref[field.at(r)] * state
    for kind, h in SECOND:
        out.send(kind, h, lambda r: b_ref[r] if kind == "b" else y_ref[r] if own(r) else beyond[r])


MIDDLE = slice(COLS, 2 * COLS)


def first_image_kernel(parity_ref, *refs):
    tile, sides, m_ref = Tile(*refs[:6]), Sides(parity_ref, *refs[6:8], FIRST), refs[8]
    b_ref, y_ref = refs[9:11]
    more, forced = Sides(parity_ref, *refs[11:13], SECOND), Sides(parity_ref, *refs[13:15], WEIGHTS)
    q_ref, g_ref = refs[15:17]
    out, sums_ref = Sides(parity_ref, *refs[17:19], THIRD), refs[19]
    field = Field(WIDE, REACH, *refs[20:24], m_ref)
    tops = refs[24:26]
    field.fill_diffusion(tile, sides, REACH - 1)
    std = std_rows(tile, sides)

    def weights(t, r):
        return tile.weights(t, r) if own(r) else padded(forced.taken(("w", t), r))

    def start(r):
        if own(r):
            return y_ref[r]
        return padded(more.taken("state", r))

    def force(t, r, value):
        if -t - 4 <= r < ROWS + t + 4:
            if t < STEPS - 1:
                tops[t][field.at(r)] = weights(t, r) * value
            else:
                field.put(r, weights(t, r) * value)

    field.forward(REACH, start, force, scaled=True)
    field.adjoint(STEPS, lambda t, r: tops[t][field.at(r)], std)
    sums = [jnp.zeros((COLS, L), F32) for _ in range(4)]
    for r in range(-STEPS, ROWS + STEPS):
        b = b_ref[r] if own(r) else padded(more.taken("b", r))
        q = b + field.get(r)
        field.put(r, q)
        if own(r):
            b, q = b[MIDDLE], q[MIDDLE]
            q_ref[r] = q
            for i, term in enumerate((b * b, b * q, q * q, q * q)):
                sums[i] = sums[i] + term
    field.mix(-STEPS, ROWS + STEPS, FACTOR)

    def keep(t, r, value):
        if own(r):
            forcing = tile.weights(t, r) * value
            sums[3] = sums[3] + forcing[MIDDLE] * value[MIDDLE]
            g_ref[t, r] = inside(forcing)

    field.forward(STEPS, lambda r: std(r) * field.get(r), keep)
    for kind, h in THIRD:
        out.send(kind, h, lambda r: g_ref[kind[1], r])
    lane = lax.broadcasted_iota(jnp.int32, (1, L), 1)
    row = jnp.zeros((1, L), F32)
    for i, term in enumerate(sums):
        total = jnp.sum(jnp.sum(term, axis=0, keepdims=True), axis=1, keepdims=True)
        row = row + jnp.where(lane == i, total, 0.0)
    sums_ref[...] = jnp.broadcast_to(row, sums_ref.shape)


def second_image_kernel(parity_ref, *refs):
    tile, sides, m_ref = Tile(*refs[:6]), Sides(parity_ref, *refs[6:8], FIRST), refs[8]
    q_ref, g_ref = refs[9:11]
    more = Sides(parity_ref, *refs[11:13], THIRD)
    u_ref = refs[13]
    field = Field(INNER, STEPS, *refs[14:18], m_ref)
    field.fill_diffusion(tile, sides, STEPS)
    forcing = lambda t, r: g_ref[t, r] if own(r) else more.taken(("g", t), r)
    for r in range(-STEPS, ROWS + STEPS):
        field.put(r, forcing(STEPS - 1, r))
    field.adjoint(0, forcing, lambda r: inside(tile.std(r)))
    for r in range(ROWS):
        u_ref[r] = q_ref[r] + field.get(r)[EDGE : EDGE + COLS]


def levels(lat, lon):
    quarter = lat // 4
    near = [[i * quarter + k for k in range(quarter)] for i in range(4)]
    far = [[(i * quarter + k) * lon + j for i in range(4) for j in range(lon)] for k in range(quarter)]
    return near, far


def add_kernel(parts_ref, out_ref):
    out_ref[...] = jnp.broadcast_to(0.25 * jnp.sum(parts_ref[...], axis=0, keepdims=True), out_ref.shape)


def finish_kernel(parts_ref, b_ref, q_ref, u_ref, solution_ref, residual_ref):
    total = jnp.sum(parts_ref[...], axis=0, keepdims=True)
    bb, bq, qq, qu = (total[:, i : i + 1] for i in range(4))
    first = bb / bq
    norm = first * first * qq - bb
    gain = 1.0 + norm / bb
    curve = gain * gain * bq - 2.0 * first * gain * qq + first * first * qu
    second = norm / curve
    along_b = first + second * gain
    along_q = first * second
    for r in range(ROWS):
        b, q = b_ref[r, MIDDLE], q_ref[r]
        solution_ref[r] = along_b * b - along_q * q
        residual_ref[r] = b - along_b * q + along_q * u_ref[r]


def exchange(to_before, to_after):
    size = lax.axis_size("lon")
    up = [(i, (i + 1) % size) for i in range(size)]
    down = [(j, i) for i, j in up]
    return lax.ppermute(to_after, "lon", up), lax.ppermute(to_before, "lon", down)


def swap(chip, core):
    size = lax.axis_size("lat")
    pairs = [[(i, i + 1) for i in range(first, size - 1, 2)] for first in (0, 1)]
    both = [p + [(j, i) for i, j in p] for p in pairs]
    return lax.ppermute(chip, "lat", both[1]), lax.ppermute(core, "lat", both[0])


def shards(
    departures, obs_weight, obs_columns, obs_owner, obs_counts, background_std, diffusion, level_factor, model_mixing
):
    parity = (lax.axis_index("lon") % 2).astype(jnp.int32).reshape(1)
    side_of = (lax.axis_index("lat") % 2).astype(jnp.int32).reshape(1)
    slots = pltpu.VMEM((SLOTS, L), F32)
    buckets = call(
        bucket_kernel,
        "bucket",
        shape(8, BUCKET, L),
        [slots, slots, pltpu.SemaphoreType.DMA((2,))],
        smem=(4, 5),
        hbm=(0, 1),
        vmem=60,
    )(departures, obs_weight, obs_columns.reshape(1, SLOTS), obs_owner.reshape(1, SLOTS), obs_counts, parity)
    received = lax.all_to_all(buckets, "lon", 0, 0)
    mats = call(matrices_kernel, "matrices", shape(4, 2 * L, 2 * L, dtype=BF16))(level_factor, model_mixing)
    fixed = call(fixed_kernel, "fixed", shape(CELLS + COLS, L))(background_std.reshape(CELLS, L), diffusion)
    fixed_left, fixed_right = exchange(fixed, fixed)
    beside = shape(PACKED + ROWS, L)
    tile, to_left, to_right = call(tile_kernel, "tile", (shape(2 * SIZE, L), beside, beside))(
        received, fixed_left, fixed_right
    )
    left, right = exchange(to_left, to_right)
    refs = (left, tile, right, fixed_left, fixed, fixed_right)
    side = shape(FIRST_ROWS, L)
    below, above = swap(*call(sides_kernel, "sides", (side, side), smem=(0,))(side_of, *refs))
    side = shape(WEIGHTS_ROWS, L)
    weights = swap(*call(weights_kernel, "weights", (side, side), smem=(0,))(side_of, *refs))
    refs = (*refs, below, above, mats)
    field, side = shape(ROWS, WIDE, L), shape(SECOND_ROWS, L)
    b, y, low, high = call(right_side_kernel, "right_side", (field, field, side, side), scratch(WIDE, STEPS + 1), smem=(0,))(
        side_of, *refs
    )
    south, north = swap(low, high)
    lat, lon = lax.axis_size("lat"), lax.axis_size("lon")
    near, far = levels(lat, lon)
    small, side = shape(ROWS, COLS, L), shape(THIRD_ROWS, L)
    space = scratch(WIDE, REACH)
    q, g, low, high, sums = call(
        first_image_kernel,
        "first_image",
        (small, shape(STEPS, ROWS, INNER, L), side, side, shape(lat, L)),
        space + [space[0]] * 2,
        smem=(0,),
    )(side_of, *refs, b, y, south, north, *weights)
    sums = lax.all_to_all(sums, "lat", 0, 0, axis_index_groups=near, tiled=True)
    south, north = swap(low, high)
    u = call(second_image_kernel, "second_image", small, scratch(INNER, STEPS), smem=(0,))(
        side_of, *refs, q, g, south, north
    )
    sums = call(add_kernel, "add", shape(4 * lon, L))(sums)
    sums = lax.all_to_all(sums, ("lat", "lon"), 0, 0, axis_index_groups=far, tiled=True)
    return call(finish_kernel, "finish", (small, small))(sums, b, q, u)


def solution(mesh):
    placed = (
        P(("lat", "lon"), None),
        P(("lat", "lon"), None),
        P(("lat", "lon")),
        P(("lat", "lon"), None),
        P(("lat", "lon")),
        P("lat", "lon", None),
        P("lat", "lon"),
        P(),
        P(),
    )
    return jax.shard_map(
        shards,
        mesh=mesh,
        in_specs=placed,
        out_specs=(P("lat", "lon", None), P("lat", "lon", None)),
        check_vma=False,
    )
```

```python
import jax
import jax.numpy as jnp
from jax import lax
from jax.experimental import pallas as pl
from jax.experimental.pallas import tpu as pltpu
from jax.sharding import PartitionSpec as P

F32 = jnp.float32
BF16 = jnp.bfloat16
L = 128
ROWS = 8
COLS = 16
CELLS = ROWS * COLS
STEPS = 3
SLOTS = 256
CAP = 64
WIDE = 3 * COLS
INNER = 2 * COLS
EDGE = COLS // 2
BUCKET = 2 * CAP + 8
REACH = 3 * STEPS

MIB = 1024 * 1024


def call(kernel, name, outs, scratch=(), smem=(), hbm=(), vmem=40):
    def run(*args):
        spaces = [pltpu.SMEM if i in smem else pltpu.HBM if i in hbm else pltpu.VMEM for i in range(len(args))]
        specs = [pl.BlockSpec(memory_space=space) for space in spaces]
        return pl.pallas_call(
            kernel,
            name=name,
            out_shape=outs,
            in_specs=specs,
            out_specs=jax.tree.map(lambda _: pl.BlockSpec(memory_space=pltpu.VMEM), outs),
            scratch_shapes=scratch,
            compiler_params=pltpu.CompilerParams(vmem_limit_bytes=vmem * MIB),
        )(*args)

    return run


def shape(*dims, dtype=F32):
    return jax.ShapeDtypeStruct(dims, dtype)


def halves(x):
    high = x.astype(BF16)
    return high, (x - high.astype(F32)).astype(BF16)


def dot(a, b):
    return jnp.dot(a, b, preferred_element_type=F32)


def matrices_kernel(factor_ref, mixing_ref, out_ref):
    for i, ref in enumerate((mixing_ref, factor_ref)):
        for j in range(2):
            m = 0.5 * ref[...]
            high, low = halves(m.T if j else m)
            row = jnp.concatenate([high, low], axis=1)
            out_ref[2 * i + j] = jnp.concatenate([row, row], axis=0)


MIX, MIX_T, FACTOR, FACTOR_T = range(4)


def bucket_kernel(
    departures_hbm, weight_hbm, columns_ref, owner_ref, counts_ref, parity_ref, out_ref, departures_ref, weight_ref, sems
):
    copies = [
        pltpu.make_async_copy(departures_hbm, departures_ref, sems.at[0]),
        pltpu.make_async_copy(weight_hbm, weight_ref, sems.at[1]),
    ]
    for copy in copies:
        copy.start()
    sub = lax.broadcasted_iota(jnp.int32, (SLOTS, SLOTS), 0)
    lane = lax.broadcasted_iota(jnp.int32, (SLOTS, SLOTS), 1)
    owner_row = owner_ref[...].astype(F32)
    owner_col = jnp.sum(jnp.where(sub == lane, owner_row, 0.0), axis=1, keepdims=True)
    same = owner_row == owner_col
    rank_row = jnp.sum(jnp.where(same & (sub < lane), 1.0, 0.0), axis=0, keepdims=True)
    rank_col = jnp.sum(jnp.where(same & (lane < sub), 1.0, 0.0), axis=1, keepdims=True)
    place = (owner_row * CAP + rank_row).astype(jnp.int32)
    pick = lax.broadcasted_iota(jnp.int32, (8 * CAP, SLOTS), 0) == place
    pick = jnp.where(pick, 1.0, 0.0).astype(BF16)
    slot = lax.broadcasted_iota(jnp.int32, (SLOTS, L), 0)
    for copy in copies:
        copy.wait()
    weights = jnp.where(slot < counts_ref[0], weight_ref[...], 0.0)
    parts = halves(weights * departures_ref[...]) + halves(weights)
    moved = dot(pick, jnp.concatenate(parts, axis=1))
    forcing = moved[:, :L] + moved[:, L : 2 * L]
    weights = moved[:, 2 * L : 3 * L] + moved[:, 3 * L :]
    number = lax.broadcasted_iota(jnp.int32, (1, SLOTS), 1)
    time = (number - STEPS * ((number * 171) >> 9)).astype(F32)
    tile = lax.broadcasted_iota(jnp.int32, (8, SLOTS), 0).astype(F32)
    here = tile == owner_row
    marks = jnp.concatenate(
        [jnp.where(here, time, 0.0), jnp.where(here, columns_ref[...].astype(F32), 0.0)], axis=0
    )
    target = rank_col + (CAP * (parity_ref[0] >> 1)).astype(F32)
    spread = jnp.where(lax.broadcasted_iota(jnp.int32, (SLOTS, L), 1).astype(F32) == target, 1.0, 0.0)
    codes = dot(marks.astype(BF16), spread.astype(BF16))
    codes = CELLS * codes[:8] + codes[8:]
    for d in range(8):
        out_ref[d, :CAP] = forcing[d * CAP : (d + 1) * CAP]
        out_ref[d, CAP : 2 * CAP] = weights[d * CAP : (d + 1) * CAP]
        out_ref[d, 2 * CAP :] = jnp.broadcast_to(codes[d : d + 1], (8, L))


def fixed_kernel(std_ref, diffusion_ref, out_ref):
    out_ref[:CELLS] = std_ref[...]
    sub = lax.broadcasted_iota(jnp.int32, (COLS, COLS), 0)
    lane = lax.broadcasted_iota(jnp.int32, (COLS, COLS), 1)
    place = lax.broadcasted_iota(jnp.int32, (COLS, L), 1)
    turned = jnp.zeros((COLS, L), F32)
    for r in range(ROWS):
        row = diffusion_ref[r : r + 1]
        column = jnp.sum(jnp.where(sub == lane, row, 0.0), axis=1, keepdims=True)
        turned = turned + jnp.where(place == r, column, 0.0)
    out_ref[CELLS:] = turned


SIZE = STEPS * CELLS
PACKED = SIZE + STEPS * ROWS * EDGE


def tile_kernel(received_ref, fixed_first_ref, fixed_second_ref, parity_ref, own_ref, first_ref, second_ref):
    ones, data = [], []
    cell = lax.broadcasted_iota(jnp.int32, (SIZE, L), 0)
    for j in range(4):
        pair = (2 * j, 2 * j + 1)
        codes = sum(received_ref[s, 2 * CAP : 2 * CAP + 1] for s in pair).astype(jnp.int32)
        ones.append(jnp.where(cell == codes, 1.0, 0.0).astype(BF16))
        for s in pair:
            parts = halves(received_ref[s, :CAP]) + halves(received_ref[s, CAP : 2 * CAP])
            data.append(jnp.concatenate(parts, axis=1))
    total = dot(jnp.concatenate(ones, axis=1), jnp.concatenate(data, axis=0))
    forcing = total[:, :L] + total[:, L : 2 * L]
    weights = total[:, 2 * L : 3 * L] + total[:, 3 * L :]
    for ref in (own_ref, first_ref, second_ref):
        ref[:SIZE] = forcing
    own_ref[SIZE:] = weights
    even = (parity_ref[0] >> 1) == 0
    for k in range(STEPS * ROWS):
        to = pl.ds(SIZE + k * EDGE, EDGE)
        left, right = weights[k * COLS : k * COLS + EDGE], weights[k * COLS + EDGE : (k + 1) * COLS]
        first_ref[to] = jnp.where(even, right, left)
        second_ref[to] = jnp.where(even, left, right)
    for r in range(ROWS):
        start = (STEPS - 1) * CELLS + r * COLS + EDGE
        left, right = weights[start : start + 1], weights[start - 1 : start]
        first_ref[PACKED + r : PACKED + r + 1] = jnp.where(even, right, left)
        second_ref[PACKED + r : PACKED + r + 1] = jnp.where(even, left, right)


class Tile:
    def __init__(self, parity_ref, first_ref, own_ref, second_ref, fixed_first_ref, fixed_ref, fixed_second_ref):
        self.even = (parity_ref[0] >> 1) == 0
        self.refs = (first_ref, own_ref, second_ref)
        self.fixed = (fixed_first_ref, fixed_ref, fixed_second_ref)

    def beside(self, refs, rows):
        first, second = refs[0][rows], refs[2][rows]
        return jnp.where(self.even, second, first), jnp.where(self.even, first, second)

    def wide(self, refs, start):
        rows = pl.ds(start, COLS)
        left, right = self.beside(refs, rows)
        return jnp.concatenate([left, refs[1][rows], right], axis=0)

    def forcing(self, t, r):
        return self.wide(self.refs, t * CELLS + r * COLS)

    def inner_weights(self, t, r):
        start = SIZE + t * CELLS + r * COLS
        left, right = self.beside(self.refs, pl.ds(SIZE + (t * ROWS + r) * EDGE, EDGE))
        return [left, self.refs[1][start : start + COLS], right]

    def weights(self, t, r):
        inner = self.inner_weights(t, r)
        if t < STEPS - 1:
            edges = [jnp.zeros((EDGE, L), F32)] * 2
        else:
            edges = [jnp.broadcast_to(row, (EDGE, L)) for row in self.beside(self.refs, pl.ds(PACKED + r, 1))]
        return jnp.concatenate([edges[0], *inner, edges[1]], axis=0)

    def std(self, r):
        return self.wide(self.fixed, r * COLS)

    def turned(self):
        return self.wide(self.fixed, CELLS)


def inside(row):
    return row[EDGE : EDGE + INNER]


def padded(row):
    if row.shape[0] == WIDE:
        return row
    edge = jnp.zeros((EDGE, L), F32)
    return jnp.concatenate([edge, row, edge], axis=0)


def places(rows):
    found, total = {}, 0
    for kind, h, width in rows:
        found[kind, h] = (total, width)
        total += width
    return found, total


FIRST, FIRST_ROWS = places(
    [(("f", t), h, WIDE if h < t + 2 else INNER) for t in range(STEPS) for h in range(1, t + 3)]
    + [("std", h, INNER) for h in range(1, STEPS + 1)]
    + [("diffusion", 1, WIDE)]
)
SECOND, SECOND_ROWS = places(
    [("state", h, WIDE if h <= STEPS else INNER) for h in range(1, REACH + 1)]
    + [("b", h, INNER) for h in range(1, STEPS + 1)]
)
WEIGHTS, WEIGHTS_ROWS = places([(("w", t), h, INNER) for t in range(STEPS) for h in range(1, t + 5)])
THIRD, THIRD_ROWS = places([(("g", t), h, INNER) for t in range(STEPS) for h in range(1, t + 2)])


class Sides:
    def __init__(self, parity_ref, chip_ref, core_ref, found):
        self.even = (parity_ref[0] & 1) == 0
        self.core_ref, self.chip_ref, self.found = core_ref, chip_ref, found

    def send(self, kind, h, row):
        start, width = self.found[kind, h]
        values = [row(r) for r in (h - 1, ROWS - h)]
        low, high = [inside(v) if width < v.shape[0] else v for v in values]
        self.core_ref[start : start + width] = jnp.where(self.even, high, low)
        self.chip_ref[start : start + width] = jnp.where(self.even, low, high)

    def taken(self, kind, r):
        start, width = self.found[kind, -r if r < 0 else r - ROWS + 1]
        core, chip = self.core_ref[start : start + width], self.chip_ref[start : start + width]
        return jnp.where(self.even, chip, core) if r < 0 else jnp.where(self.even, core, chip)


def sides_kernel(*refs):
    tile, sides = Tile(*refs[:7]), Sides(refs[0], *refs[7:], FIRST)
    for kind, h in FIRST:
        if kind == "std":
            row = tile.std
        elif kind == "diffusion":
            row = lambda r: tile.turned()
        else:
            row = lambda r: tile.forcing(kind[1], r)
        sides.send(kind, h, row)


def weights_kernel(*refs):
    tile, sides = Tile(*refs[:7]), Sides(refs[0], *refs[7:], WEIGHTS)
    for kind, h in WEIGHTS:
        sides.send(kind, h, lambda r: jnp.concatenate(tile.inner_weights(kind[1], r), axis=0))


def own(r):
    return 0 <= r < ROWS


class Field:
    def __init__(self, width, reach, v_ref, x_ref, y_ref, d_ref, m_ref):
        self.width, self.reach = width, reach
        self.v_ref, self.x_ref, self.y_ref, self.d_ref, self.m_ref = v_ref, x_ref, y_ref, d_ref, m_ref

    def at(self, r):
        return pl.ds((r + self.reach) * self.width, self.width)

    def put(self, r, value):
        self.v_ref[self.at(r)] = value
        high, low = halves(value)
        self.x_ref[self.at(r), :L] = high
        self.x_ref[self.at(r), L:] = low

    def mix(self, first, stop, which):
        rows = pl.ds((first + self.reach) * self.width, (stop - first) * self.width)
        self.y_ref[rows] = dot(self.x_ref[rows], self.m_ref[which])

    def get(self, r):
        return self.v_ref[self.at(r)] + self.y_ref[self.at(r), :L] + self.y_ref[self.at(r), L:]

    def fill_diffusion(self, tile, sides, reach):
        values = {0: tile.turned(), -1: sides.taken("diffusion", -1), 1: sides.taken("diffusion", ROWS)}
        skip = (WIDE - self.width) // 2
        for r in range(-reach, ROWS + reach):
            column = values[r // ROWS][skip : skip + self.width, r % ROWS : r % ROWS + 1]
            self.d_ref[self.at(r)] = jnp.broadcast_to(column, (self.width, L))

    def smooth(self, first, stop, get, put, scaled=False):
        held = []
        for r in range(first, stop):
            value = get(r)
            if scaled and r in (first, stop - 1):
                held.append((value, None, value))
            else:
                d = self.d_ref[self.at(r)]
                held.append((value, d, d * value))
            if len(held) == 3:
                value, d, u = held[1]
                around = held[0][2] + held[2][2] + pltpu.roll(u, 1, 0) + pltpu.roll(u, self.width - 1, 0)
                put(r - 1, value + d * (around - 4.0 * u))
                held.pop(0)

    def forward(self, h, start, seen, scaled=False):
        self.smooth(-h, ROWS + h, start, self.put, scaled)
        for t in range(STEPS):
            first, stop = -h + t + 1, ROWS + h - t - 1
            self.mix(first, stop, MIX)

            def get(r, t=t):
                value = self.get(r)
                seen(t, r, value)
                return value

            if t < STEPS - 1:
                self.smooth(first, stop, get, self.put)
            else:
                for r in range(first, stop):
                    get(r)

    def adjoint(self, h, forcing, std):
        for t in range(STEPS - 1, -1, -1):
            first, stop = -h - t - 1, ROWS + h + t + 1
            self.mix(first, stop, MIX_T)
            if t > 0:
                put = lambda r, value, t=t: self.put(r, value + forcing(t - 1, r))
            else:
                put = lambda r, value: self.put(r, std(r) * value)
            self.smooth(first, stop, self.get, put)
        self.mix(-h, ROWS + h, FACTOR_T)


def scratch(width, reach):
    tall = (ROWS + 2 * reach) * width
    return [
        pltpu.VMEM((tall, L), F32),
        pltpu.VMEM((tall, 2 * L), BF16),
        pltpu.VMEM((tall, 2 * L), F32),
        pltpu.VMEM((tall, L), F32),
    ]


def std_rows(tile, sides):
    return lambda r: tile.std(r) if own(r) else padded(sides.taken("std", r))


def right_side_kernel(parity_ref, *refs):
    tile, sides, m_ref = Tile(parity_ref, *refs[:6]), Sides(parity_ref, *refs[6:8], FIRST), refs[8]
    b_ref, y_ref = refs[9:11]
    out = Sides(parity_ref, *refs[11:13], SECOND)
    field = Field(WIDE, STEPS + 1, *refs[13:17], m_ref)
    field.fill_diffusion(tile, sides, STEPS + 1)
    forcing = lambda t, r: tile.forcing(t, r) if own(r) else padded(sides.taken(("f", t), r))
    std = std_rows(tile, sides)
    for r in range(-STEPS - 1, ROWS + STEPS + 1):
        field.put(r, forcing(STEPS - 1, r))
    field.adjoint(1, forcing, std)
    for r in range(-1, ROWS + 1):
        value = field.get(r)
        field.put(r, value)
        if own(r):
            b_ref[r] = value
    field.mix(-1, ROWS + 1, FACTOR)
    beyond = {}
    for r in range(-1, ROWS + 1):
        state = std(r) * field.get(r)
        if own(r):
            y_ref[r] = state
        else:
            beyond[r] = field.d_ref[field.at(r)] * state
    for kind, h in SECOND:
        out.send(kind, h, lambda r: b_ref[r] if kind == "b" else y_ref[r] if own(r) else beyond[r])


MIDDLE = slice(COLS, 2 * COLS)


def first_image_kernel(parity_ref, *refs):
    tile, sides, m_ref = Tile(parity_ref, *refs[:6]), Sides(parity_ref, *refs[6:8], FIRST), refs[8]
    b_ref, y_ref = refs[9:11]
    more, forced = Sides(parity_ref, *refs[11:13], SECOND), Sides(parity_ref, *refs[13:15], WEIGHTS)
    q_ref, g_ref = refs[15:17]
    out, sums_ref = Sides(parity_ref, *refs[17:19], THIRD), refs[19]
    field = Field(WIDE, REACH, *refs[20:24], m_ref)
    tops = refs[24:26]
    field.fill_diffusion(tile, sides, REACH - 1)
    std = std_rows(tile, sides)

    def weights(t, r):
        return tile.weights(t, r) if own(r) else padded(forced.taken(("w", t), r))

    def start(r):
        if own(r):
            return y_ref[r]
        return padded(more.taken("state", r))

    def force(t, r, value):
        if -t - 4 <= r < ROWS + t + 4:
            if t < STEPS - 1:
                tops[t][field.at(r)] = weights(t, r) * value
            else:
                field.put(r, weights(t, r) * value)

    field.forward(REACH, start, force, scaled=True)
    field.adjoint(STEPS, lambda t, r: tops[t][field.at(r)], std)
    sums = [jnp.zeros((COLS, L), F32) for _ in range(4)]
    for r in range(-STEPS, ROWS + STEPS):
        b = b_ref[r] if own(r) else padded(more.taken("b", r))
        q = b + field.get(r)
        field.put(r, q)
        if own(r):
            b, q = b[MIDDLE], q[MIDDLE]
            q_ref[r] = q
            for i, term in enumerate((b * b, b * q, q * q, q * q)):
                sums[i] = sums[i] + term
    field.mix(-STEPS, ROWS + STEPS, FACTOR)

    def keep(t, r, value):
        if own(r):
            forcing = tile.weights(t, r) * value
            sums[3] = sums[3] + forcing[MIDDLE] * value[MIDDLE]
            g_ref[t, r] = inside(forcing)

    field.forward(STEPS, lambda r: std(r) * field.get(r), keep)
    for kind, h in THIRD:
        out.send(kind, h, lambda r: g_ref[kind[1], r])
    lane = lax.broadcasted_iota(jnp.int32, (1, L), 1)
    row = jnp.zeros((1, L), F32)
    for i, term in enumerate(sums):
        total = jnp.sum(jnp.sum(term, axis=0, keepdims=True), axis=1, keepdims=True)
        row = row + jnp.where(lane == i, total, 0.0)
    sums_ref[...] = jnp.broadcast_to(row, sums_ref.shape)


def second_image_kernel(parity_ref, *refs):
    tile, sides, m_ref = Tile(parity_ref, *refs[:6]), Sides(parity_ref, *refs[6:8], FIRST), refs[8]
    q_ref, g_ref = refs[9:11]
    more = Sides(parity_ref, *refs[11:13], THIRD)
    u_ref = refs[13]
    field = Field(INNER, STEPS, *refs[14:18], m_ref)
    field.fill_diffusion(tile, sides, STEPS)
    forcing = lambda t, r: g_ref[t, r] if own(r) else more.taken(("g", t), r)
    for r in range(-STEPS, ROWS + STEPS):
        field.put(r, forcing(STEPS - 1, r))
    field.adjoint(0, forcing, lambda r: inside(tile.std(r)))
    for r in range(ROWS):
        u_ref[r] = q_ref[r] + field.get(r)[EDGE : EDGE + COLS]


def levels(lat, lon):
    quarter = lat // 4
    near = [[i * quarter + k for k in range(quarter)] for i in range(4)]
    far = [[(i * quarter + k) * lon + j for i in range(4) for j in range(lon)] for k in range(quarter)]
    return near, far


def add_kernel(parts_ref, out_ref):
    out_ref[...] = jnp.broadcast_to(0.25 * jnp.sum(parts_ref[...], axis=0, keepdims=True), out_ref.shape)


def finish_kernel(parts_ref, b_ref, q_ref, u_ref, solution_ref, residual_ref):
    total = jnp.sum(parts_ref[...], axis=0, keepdims=True)
    bb, bq, qq, qu = (total[:, i : i + 1] for i in range(4))
    first = bb / bq
    norm = first * first * qq - bb
    gain = 1.0 + norm / bb
    curve = gain * gain * bq - 2.0 * first * gain * qq + first * first * qu
    second = norm / curve
    along_b = first + second * gain
    along_q = first * second
    for r in range(ROWS):
        b, q = b_ref[r, MIDDLE], q_ref[r]
        solution_ref[r] = along_b * b - along_q * q
        residual_ref[r] = b - along_b * q + along_q * u_ref[r]


def beside(first, second):
    size = lax.axis_size("lon")
    pairs = [[(i, (i + 1) % size) for i in range(start, size, 2)] for start in (0, 1)]
    both = [p + [(j, i) for i, j in p] for p in pairs]
    return lax.ppermute(first, "lon", both[0]), lax.ppermute(second, "lon", both[1])


def swap(chip, core):
    size = lax.axis_size("lat")
    pairs = [[(i, i + 1) for i in range(first, size - 1, 2)] for first in (0, 1)]
    both = [p + [(j, i) for i, j in p] for p in pairs]
    return lax.ppermute(chip, "lat", both[1]), lax.ppermute(core, "lat", both[0])


def shards(
    departures, obs_weight, obs_columns, obs_owner, obs_counts, background_std, diffusion, level_factor, model_mixing
):
    side_of = (lax.axis_index("lat") % 2 + 2 * (lax.axis_index("lon") % 2)).astype(jnp.int32).reshape(1)
    slots = pltpu.VMEM((SLOTS, L), F32)
    buckets = call(
        bucket_kernel,
        "bucket",
        shape(8, BUCKET, L),
        [slots, slots, pltpu.SemaphoreType.DMA((2,))],
        smem=(4, 5),
        hbm=(0, 1),
        vmem=60,
    )(departures, obs_weight, obs_columns.reshape(1, SLOTS), obs_owner.reshape(1, SLOTS), obs_counts, side_of)
    received = lax.all_to_all(buckets, "lon", 0, 0)
    mats = call(matrices_kernel, "matrices", shape(4, 2 * L, 2 * L, dtype=BF16))(level_factor, model_mixing)
    fixed = call(fixed_kernel, "fixed", shape(CELLS + COLS, L))(background_std.reshape(CELLS, L), diffusion)
    fixed_first, fixed_second = beside(fixed, fixed)
    edge = shape(PACKED + ROWS, L)
    tile, first, second = call(tile_kernel, "tile", (shape(2 * SIZE, L), edge, edge), smem=(3,))(
        received, fixed_first, fixed_second, side_of
    )
    first, second = beside(first, second)
    refs = (first, tile, second, fixed_first, fixed, fixed_second)
    side = shape(FIRST_ROWS, L)
    below, above = swap(*call(sides_kernel, "sides", (side, side), smem=(0,))(side_of, *refs))
    side = shape(WEIGHTS_ROWS, L)
    weights = swap(*call(weights_kernel, "weights", (side, side), smem=(0,))(side_of, *refs))
    refs = (*refs, below, above, mats)
    field, side = shape(ROWS, WIDE, L), shape(SECOND_ROWS, L)
    b, y, low, high = call(right_side_kernel, "right_side", (field, field, side, side), scratch(WIDE, STEPS + 1), smem=(0,))(
        side_of, *refs
    )
    south, north = swap(low, high)
    lat, lon = lax.axis_size("lat"), lax.axis_size("lon")
    near, far = levels(lat, lon)
    small, side = shape(ROWS, COLS, L), shape(THIRD_ROWS, L)
    space = scratch(WIDE, REACH)
    q, g, low, high, sums = call(
        first_image_kernel,
        "first_image",
        (small, shape(STEPS, ROWS, INNER, L), side, side, shape(lat, L)),
        space + [space[0]] * 2,
        smem=(0,),
    )(side_of, *refs, b, y, south, north, *weights)
    sums = lax.all_to_all(sums, "lat", 0, 0, axis_index_groups=near, tiled=True)
    south, north = swap(low, high)
    u = call(second_image_kernel, "second_image", small, scratch(INNER, STEPS), smem=(0,))(
        side_of, *refs, q, g, south, north
    )
    sums = call(add_kernel, "add", shape(4 * lon, L))(sums)
    sums = lax.all_to_all(sums, ("lat", "lon"), 0, 0, axis_index_groups=far, tiled=True)
    return call(finish_kernel, "finish", (small, small))(sums, b, q, u)


def solution(mesh):
    placed = (
        P(("lat", "lon"), None),
        P(("lat", "lon"), None),
        P(("lat", "lon")),
        P(("lat", "lon"), None),
        P(("lat", "lon")),
        P("lat", "lon", None),
        P("lat", "lon"),
        P(),
        P(),
    )
    return jax.shard_map(
        shards,
        mesh=mesh,
        in_specs=placed,
        out_specs=(P("lat", "lon", None), P("lat", "lon", None)),
        check_vma=False,
    )
```

```python
import jax
import jax.numpy as jnp
from jax import lax
from jax.experimental import pallas as pl
from jax.experimental.pallas import tpu as pltpu
from jax.sharding import PartitionSpec as P

F32 = jnp.float32
BF16 = jnp.bfloat16
L = 128
ROWS = 8
COLS = 16
CELLS = ROWS * COLS
STEPS = 3
SLOTS = 256
CAP = 64
WIDE = 3 * COLS
INNER = 2 * COLS
EDGE = COLS // 2
BUCKET = 2 * CAP + 8
REACH = 3 * STEPS

MIB = 1024 * 1024


def call(kernel, name, outs, scratch=(), smem=(), hbm=(), vmem=40, out_space=pltpu.VMEM):
    def run(*args):
        spaces = [pltpu.SMEM if i in smem else pltpu.HBM if i in hbm else pltpu.VMEM for i in range(len(args))]
        specs = [pl.BlockSpec(memory_space=space) for space in spaces]
        return pl.pallas_call(
            kernel,
            name=name,
            out_shape=outs,
            in_specs=specs,
            out_specs=jax.tree.map(lambda _: pl.BlockSpec(memory_space=out_space), outs),
            scratch_shapes=scratch,
            compiler_params=pltpu.CompilerParams(vmem_limit_bytes=vmem * MIB),
        )(*args)

    return run


def shape(*dims, dtype=F32):
    return jax.ShapeDtypeStruct(dims, dtype)


def halves(x):
    high = x.astype(BF16)
    return high, (x - high.astype(F32)).astype(BF16)


def dot(a, b):
    return jnp.dot(a, b, preferred_element_type=F32)


def matrices_kernel(factor_ref, mixing_ref, out_ref):
    for i, ref in enumerate((mixing_ref, factor_ref)):
        for j in range(2):
            m = 0.5 * ref[...]
            high, low = halves(m.T if j else m)
            row = jnp.concatenate([high, low], axis=1)
            out_ref[2 * i + j] = jnp.concatenate([row, row], axis=0)


MIX, MIX_T, FACTOR, FACTOR_T = range(4)


def bucket_kernel(
    departures_hbm, weight_hbm, columns_ref, owner_ref, counts_ref, parity_ref, out_hbm,
    departures_ref, weight_ref, out_ref, sems,
):
    copies = [
        pltpu.make_async_copy(departures_hbm, departures_ref, sems.at[0]),
        pltpu.make_async_copy(weight_hbm, weight_ref, sems.at[1]),
    ]
    for copy in copies:
        copy.start()
    sub = lax.broadcasted_iota(jnp.int32, (SLOTS, SLOTS), 0)
    lane = lax.broadcasted_iota(jnp.int32, (SLOTS, SLOTS), 1)
    owner_row = owner_ref[...].astype(F32)
    owner_col = jnp.sum(jnp.where(sub == lane, owner_row, 0.0), axis=1, keepdims=True)
    same = owner_row == owner_col
    rank_row = jnp.sum(jnp.where(same & (sub < lane), 1.0, 0.0), axis=0, keepdims=True)
    rank_col = jnp.sum(jnp.where(same & (lane < sub), 1.0, 0.0), axis=1, keepdims=True)
    place = (owner_row * CAP + rank_row).astype(jnp.int32)
    pick = lax.broadcasted_iota(jnp.int32, (8 * CAP, SLOTS), 0) == place
    pick = jnp.where(pick, 1.0, 0.0).astype(BF16)
    slot = lax.broadcasted_iota(jnp.int32, (SLOTS, L), 0)
    for copy in copies:
        copy.wait()
    weights = jnp.where(slot < counts_ref[0], weight_ref[...], 0.0)
    parts = halves(weights * departures_ref[...]) + halves(weights)
    data = jnp.concatenate(parts, axis=1)
    number = lax.broadcasted_iota(jnp.int32, (1, SLOTS), 1)
    time = (number - STEPS * ((number * 171) >> 9)).astype(F32)
    tile = lax.broadcasted_iota(jnp.int32, (8, SLOTS), 0).astype(F32)
    here = tile == owner_row
    marks = jnp.concatenate(
        [jnp.where(here, time, 0.0), jnp.where(here, columns_ref[...].astype(F32), 0.0)], axis=0
    )
    target = rank_col + (CAP * parity_ref[0]).astype(F32)
    spread = jnp.where(lax.broadcasted_iota(jnp.int32, (SLOTS, L), 1).astype(F32) == target, 1.0, 0.0)
    codes = dot(marks.astype(BF16), spread.astype(BF16))
    codes = CELLS * codes[:8] + codes[8:]
    sends = []
    for j in range(4):
        moved = dot(pick[2 * j * CAP : 2 * (j + 1) * CAP], data)
        forcing = moved[:, :L] + moved[:, L : 2 * L]
        weights = moved[:, 2 * L : 3 * L] + moved[:, 3 * L :]
        for k in range(2):
            d, rows = 2 * j + k, slice(k * CAP, (k + 1) * CAP)
            out_ref[d, :CAP] = forcing[rows]
            out_ref[d, CAP : 2 * CAP] = weights[rows]
            out_ref[d, 2 * CAP :] = jnp.broadcast_to(codes[d : d + 1], (8, L))
            sends.append(pltpu.make_async_copy(out_ref.at[d], out_hbm.at[d], sems.at[2 + d]))
            sends[-1].start()
    for copy in sends:
        copy.wait()


def fixed_kernel(std_ref, diffusion_ref, out_ref):
    out_ref[:CELLS] = std_ref[...]
    sub = lax.broadcasted_iota(jnp.int32, (COLS, COLS), 0)
    lane = lax.broadcasted_iota(jnp.int32, (COLS, COLS), 1)
    place = lax.broadcasted_iota(jnp.int32, (COLS, L), 1)
    turned = jnp.zeros((COLS, L), F32)
    for r in range(ROWS):
        row = diffusion_ref[r : r + 1]
        column = jnp.sum(jnp.where(sub == lane, row, 0.0), axis=1, keepdims=True)
        turned = turned + jnp.where(place == r, column, 0.0)
    out_ref[CELLS:] = turned


SIZE = STEPS * CELLS
PACKED = SIZE + STEPS * ROWS * EDGE


def tile_kernel(received_ref, fixed_left_ref, fixed_right_ref, m_ref, own_ref, to_left_ref, to_right_ref):
    ones, data = [], []
    cell = lax.broadcasted_iota(jnp.int32, (SIZE, L), 0)
    for j in range(4):
        pair = (2 * j, 2 * j + 1)
        codes = sum(received_ref[s, 2 * CAP : 2 * CAP + 1] for s in pair).astype(jnp.int32)
        ones.append(jnp.where(cell == codes, 1.0, 0.0).astype(BF16))
        for s in pair:
            parts = halves(received_ref[s, :CAP]) + halves(received_ref[s, CAP : 2 * CAP])
            data.append(jnp.concatenate(parts, axis=1))
    total = dot(jnp.concatenate(ones, axis=1), jnp.concatenate(data, axis=0))
    forcing = total[:, :L] + total[:, L : 2 * L]
    weights = total[:, 2 * L : 3 * L] + total[:, 3 * L :]
    for ref in (own_ref, to_left_ref, to_right_ref):
        ref[:SIZE] = forcing
    own_ref[SIZE:] = weights
    for k in range(STEPS * ROWS):
        to = pl.ds(SIZE + k * EDGE, EDGE)
        to_left_ref[to] = weights[k * COLS : k * COLS + EDGE]
        to_right_ref[to] = weights[k * COLS + EDGE : (k + 1) * COLS]
    for r in range(ROWS):
        first = (STEPS - 1) * CELLS + r * COLS
        to_left_ref[PACKED + r : PACKED + r + 1] = weights[first + EDGE : first + EDGE + 1]
        to_right_ref[PACKED + r : PACKED + r + 1] = weights[first + EDGE - 1 : first + EDGE]


def wide(refs, start):
    return jnp.concatenate([ref[start : start + COLS] for ref in refs], axis=0)


class Tile:
    def __init__(self, left_ref, own_ref, right_ref, fixed_left_ref, fixed_ref, fixed_right_ref):
        self.left, self.own, self.right = left_ref, own_ref, right_ref
        self.fixed = (fixed_left_ref, fixed_ref, fixed_right_ref)

    def forcing(self, t, r):
        return wide((self.left, self.own, self.right), t * CELLS + r * COLS)

    def inner_weights(self, t, r):
        start = SIZE + t * CELLS + r * COLS
        packed = pl.ds(SIZE + (t * ROWS + r) * EDGE, EDGE)
        return [self.left[packed], self.own[start : start + COLS], self.right[packed]]

    def weights(self, t, r):
        inner = self.inner_weights(t, r)
        if t < STEPS - 1:
            edges = [jnp.zeros((EDGE, L), F32)] * 2
        else:
            edges = [jnp.broadcast_to(ref[PACKED + r : PACKED + r + 1], (EDGE, L)) for ref in (self.left, self.right)]
        return jnp.concatenate([edges[0], *inner, edges[1]], axis=0)

    def std(self, r):
        return wide(self.fixed, r * COLS)

    def turned(self):
        return wide(self.fixed, CELLS)


def inside(row):
    return row[EDGE : EDGE + INNER]


def padded(row):
    if row.shape[0] == WIDE:
        return row
    edge = jnp.zeros((EDGE, L), F32)
    return jnp.concatenate([edge, row, edge], axis=0)


def places(rows):
    found, total = {}, 0
    for kind, h, width in rows:
        found[kind, h] = (total, width)
        total += width
    return found, total


FIRST, FIRST_ROWS = places(
    [(("f", t), h, WIDE if h < t + 2 else INNER) for t in range(STEPS) for h in range(1, t + 3)]
    + [("std", h, INNER) for h in range(1, STEPS + 1)]
    + [("diffusion", 1, WIDE)]
)
SECOND, SECOND_ROWS = places(
    [("state", h, WIDE if h <= STEPS else INNER) for h in range(1, REACH + 1)]
    + [("b", h, INNER) for h in range(1, STEPS + 1)]
)
WEIGHTS, WEIGHTS_ROWS = places([(("w", t), h, INNER) for t in range(STEPS) for h in range(1, t + 5)])
THIRD, THIRD_ROWS = places([(("g", t), h, INNER) for t in range(STEPS) for h in range(1, t + 2)])


class Sides:
    def __init__(self, parity_ref, chip_ref, core_ref, found):
        self.even = parity_ref[0] == 0
        self.core_ref, self.chip_ref, self.found = core_ref, chip_ref, found

    def send(self, kind, h, row):
        start, width = self.found[kind, h]
        values = [row(r) for r in (h - 1, ROWS - h)]
        low, high = [inside(v) if width < v.shape[0] else v for v in values]
        self.core_ref[start : start + width] = jnp.where(self.even, high, low)
        self.chip_ref[start : start + width] = jnp.where(self.even, low, high)

    def taken(self, kind, r):
        start, width = self.found[kind, -r if r < 0 else r - ROWS + 1]
        core, chip = self.core_ref[start : start + width], self.chip_ref[start : start + width]
        return jnp.where(self.even, chip, core) if r < 0 else jnp.where(self.even, core, chip)


def sides_kernel(*refs):
    tile, sides = Tile(*refs[1:7]), Sides(refs[0], *refs[7:], FIRST)
    for kind, h in FIRST:
        if kind == "std":
            row = tile.std
        elif kind == "diffusion":
            row = lambda r: tile.turned()
        else:
            row = lambda r: tile.forcing(kind[1], r)
        sides.send(kind, h, row)


def weights_kernel(*refs):
    tile, sides = Tile(*refs[1:7]), Sides(refs[0], *refs[7:], WEIGHTS)
    for kind, h in WEIGHTS:
        sides.send(kind, h, lambda r: jnp.concatenate(tile.inner_weights(kind[1], r), axis=0))


def own(r):
    return 0 <= r < ROWS


class Field:
    def __init__(self, width, reach, v_ref, x_ref, y_ref, d_ref, m_ref):
        self.width, self.reach = width, reach
        self.v_ref, self.x_ref, self.y_ref, self.d_ref, self.m_ref = v_ref, x_ref, y_ref, d_ref, m_ref

    def at(self, r):
        return pl.ds((r + self.reach) * self.width, self.width)

    def put(self, r, value):
        self.v_ref[self.at(r)] = value
        high, low = halves(value)
        self.x_ref[self.at(r), :L] = high
        self.x_ref[self.at(r), L:] = low

    def mix(self, first, stop, which):
        rows = pl.ds((first + self.reach) * self.width, (stop - first) * self.width)
        self.y_ref[rows] = dot(self.x_ref[rows], self.m_ref[which])

    def get(self, r):
        return self.v_ref[self.at(r)] + self.y_ref[self.at(r), :L] + self.y_ref[self.at(r), L:]

    def fill_diffusion(self, tile, sides, reach):
        values = {0: tile.turned(), -1: sides.taken("diffusion", -1), 1: sides.taken("diffusion", ROWS)}
        skip = (WIDE - self.width) // 2
        for r in range(-reach, ROWS + reach):
            column = values[r // ROWS][skip : skip + self.width, r % ROWS : r % ROWS + 1]
            self.d_ref[self.at(r)] = jnp.broadcast_to(column, (self.width, L))

    def smooth(self, first, stop, get, put, scaled=False):
        held = []
        for r in range(first, stop):
            value = get(r)
            if scaled and r in (first, stop - 1):
                held.append((value, None, value))
            else:
                d = self.d_ref[self.at(r)]
                held.append((value, d, d * value))
            if len(held) == 3:
                value, d, u = held[1]
                around = held[0][2] + held[2][2] + pltpu.roll(u, 1, 0) + pltpu.roll(u, self.width - 1, 0)
                put(r - 1, value + d * (around - 4.0 * u))
                held.pop(0)

    def forward(self, h, start, seen, scaled=False):
        self.smooth(-h, ROWS + h, start, self.put, scaled)
        for t in range(STEPS):
            first, stop = -h + t + 1, ROWS + h - t - 1
            self.mix(first, stop, MIX)

            def get(r, t=t):
                value = self.get(r)
                seen(t, r, value)
                return value

            if t < STEPS - 1:
                self.smooth(first, stop, get, self.put)
            else:
                for r in range(first, stop):
                    get(r)

    def adjoint(self, h, forcing, std):
        for t in range(STEPS - 1, -1, -1):
            first, stop = -h - t - 1, ROWS + h + t + 1
            self.mix(first, stop, MIX_T)
            if t > 0:
                put = lambda r, value, t=t: self.put(r, value + forcing(t - 1, r))
            else:
                put = lambda r, value: self.put(r, std(r) * value)
            self.smooth(first, stop, self.get, put)
        self.mix(-h, ROWS + h, FACTOR_T)


def scratch(width, reach):
    tall = (ROWS + 2 * reach) * width
    return [
        pltpu.VMEM((tall, L), F32),
        pltpu.VMEM((tall, 2 * L), BF16),
        pltpu.VMEM((tall, 2 * L), F32),
        pltpu.VMEM((tall, L), F32),
    ]


def std_rows(tile, sides):
    return lambda r: tile.std(r) if own(r) else padded(sides.taken("std", r))


def right_side_kernel(parity_ref, *refs):
    tile, sides, m_ref = Tile(*refs[:6]), Sides(parity_ref, *refs[6:8], FIRST), refs[8]
    b_ref, y_ref = refs[9:11]
    out = Sides(parity_ref, *refs[11:13], SECOND)
    field = Field(WIDE, STEPS + 1, *refs[13:17], m_ref)
    field.fill_diffusion(tile, sides, STEPS + 1)
    forcing = lambda t, r: tile.forcing(t, r) if own(r) else padded(sides.taken(("f", t), r))
    std = std_rows(tile, sides)
    for r in range(-STEPS - 1, ROWS + STEPS + 1):
        field.put(r, forcing(STEPS - 1, r))
    field.adjoint(1, forcing, std)
    for r in range(-1, ROWS + 1):
        value = field.get(r)
        field.put(r, value)
        if own(r):
            b_ref[r] = value
    field.mix(-1, ROWS + 1, FACTOR)
    beyond = {}
    for r in range(-1, ROWS + 1):
        state = std(r) * field.get(r)
        if own(r):
            y_ref[r] = state
        else:
            beyond[r] = field.d_ref[field.at(r)] * state
    for kind, h in SECOND:
        out.send(kind, h, lambda r: b_ref[r] if kind == "b" else y_ref[r] if own(r) else beyond[r])


MIDDLE = slice(COLS, 2 * COLS)


def first_image_kernel(parity_ref, *refs):
    tile, sides, m_ref = Tile(*refs[:6]), Sides(parity_ref, *refs[6:8], FIRST), refs[8]
    b_ref, y_ref = refs[9:11]
    more, forced = Sides(parity_ref, *refs[11:13], SECOND), Sides(parity_ref, *refs[13:15], WEIGHTS)
    q_ref, g_ref = refs[15:17]
    out, sums_ref = Sides(parity_ref, *refs[17:19], THIRD), refs[19]
    field = Field(WIDE, REACH, *refs[20:24], m_ref)
    tops = refs[24:26]
    field.fill_diffusion(tile, sides, REACH - 1)
    std = std_rows(tile, sides)

    def weights(t, r):
        return tile.weights(t, r) if own(r) else padded(forced.taken(("w", t), r))

    def start(r):
        if own(r):
            return y_ref[r]
        return padded(more.taken("state", r))

    def force(t, r, value):
        if -t - 4 <= r < ROWS + t + 4:
            if t < STEPS - 1:
                tops[t][field.at(r)] = weights(t, r) * value
            else:
                field.put(r, weights(t, r) * value)

    field.forward(REACH, start, force, scaled=True)
    field.adjoint(STEPS, lambda t, r: tops[t][field.at(r)], std)
    sums = [jnp.zeros((COLS, L), F32) for _ in range(4)]
    for r in range(-STEPS, ROWS + STEPS):
        b = b_ref[r] if own(r) else padded(more.taken("b", r))
        q = b + field.get(r)
        field.put(r, q)
        if own(r):
            b, q = b[MIDDLE], q[MIDDLE]
            q_ref[r] = q
            for i, term in enumerate((b * b, b * q, q * q, q * q)):
                sums[i] = sums[i] + term
    field.mix(-STEPS, ROWS + STEPS, FACTOR)

    def keep(t, r, value):
        if own(r):
            forcing = tile.weights(t, r) * value
            sums[3] = sums[3] + forcing[MIDDLE] * value[MIDDLE]
            g_ref[t, r] = inside(forcing)

    field.forward(STEPS, lambda r: std(r) * field.get(r), keep)
    for kind, h in THIRD:
        out.send(kind, h, lambda r: g_ref[kind[1], r])
    lane = lax.broadcasted_iota(jnp.int32, (1, L), 1)
    row = jnp.zeros((1, L), F32)
    for i, term in enumerate(sums):
        total = jnp.sum(jnp.sum(term, axis=0, keepdims=True), axis=1, keepdims=True)
        row = row + jnp.where(lane == i, total, 0.0)
    sums_ref[...] = jnp.broadcast_to(row, sums_ref.shape)


def second_image_kernel(parity_ref, *refs):
    tile, sides, m_ref = Tile(*refs[:6]), Sides(parity_ref, *refs[6:8], FIRST), refs[8]
    q_ref, g_ref = refs[9:11]
    more = Sides(parity_ref, *refs[11:13], THIRD)
    u_ref = refs[13]
    field = Field(INNER, STEPS, *refs[14:18], m_ref)
    field.fill_diffusion(tile, sides, STEPS)
    forcing = lambda t, r: g_ref[t, r] if own(r) else more.taken(("g", t), r)
    for r in range(-STEPS, ROWS + STEPS):
        field.put(r, forcing(STEPS - 1, r))
    field.adjoint(0, forcing, lambda r: inside(tile.std(r)))
    for r in range(ROWS):
        u_ref[r] = q_ref[r] + field.get(r)[EDGE : EDGE + COLS]


def levels(lat, lon):
    quarter = lat // 4
    near = [[i * quarter + k for k in range(quarter)] for i in range(4)]
    far = [[(i * quarter + k) * lon + j for i in range(4) for j in range(lon)] for k in range(quarter)]
    return near, far


def add_kernel(parts_ref, out_ref):
    out_ref[...] = jnp.broadcast_to(0.25 * jnp.sum(parts_ref[...], axis=0, keepdims=True), out_ref.shape)


def finish_kernel(parts_ref, b_ref, q_ref, u_ref, solution_ref, residual_ref):
    total = jnp.sum(parts_ref[...], axis=0, keepdims=True)
    bb, bq, qq, qu = (total[:, i : i + 1] for i in range(4))
    first = bb / bq
    norm = first * first * qq - bb
    gain = 1.0 + norm / bb
    curve = gain * gain * bq - 2.0 * first * gain * qq + first * first * qu
    second = norm / curve
    along_b = first + second * gain
    along_q = first * second
    for r in range(ROWS):
        b, q = b_ref[r, MIDDLE], q_ref[r]
        solution_ref[r] = along_b * b - along_q * q
        residual_ref[r] = b - along_b * q + along_q * u_ref[r]


def exchange(to_before, to_after):
    size = lax.axis_size("lon")
    up = [(i, (i + 1) % size) for i in range(size)]
    down = [(j, i) for i, j in up]
    return lax.ppermute(to_after, "lon", up), lax.ppermute(to_before, "lon", down)


def swap(chip, core):
    size = lax.axis_size("lat")
    pairs = [[(i, i + 1) for i in range(first, size - 1, 2)] for first in (0, 1)]
    both = [p + [(j, i) for i, j in p] for p in pairs]
    return lax.ppermute(chip, "lat", both[1]), lax.ppermute(core, "lat", both[0])


def shards(
    departures, obs_weight, obs_columns, obs_owner, obs_counts, background_std, diffusion, level_factor, model_mixing
):
    parity = (lax.axis_index("lon") % 2).astype(jnp.int32).reshape(1)
    side_of = (lax.axis_index("lat") % 2).astype(jnp.int32).reshape(1)
    slots = pltpu.VMEM((SLOTS, L), F32)
    buckets = call(
        bucket_kernel,
        "bucket",
        shape(8, BUCKET, L),
        [slots, slots, pltpu.VMEM((8, BUCKET, L), F32), pltpu.SemaphoreType.DMA((10,))],
        smem=(4, 5),
        hbm=(0, 1),
        vmem=60,
        out_space=pltpu.HBM,
    )(departures, obs_weight, obs_columns.reshape(1, SLOTS), obs_owner.reshape(1, SLOTS), obs_counts, parity)
    received = lax.all_to_all(buckets, "lon", 0, 0)
    mats = call(matrices_kernel, "matrices", shape(4, 2 * L, 2 * L, dtype=BF16))(level_factor, model_mixing)
    fixed = call(fixed_kernel, "fixed", shape(CELLS + COLS, L))(background_std.reshape(CELLS, L), diffusion)
    fixed_left, fixed_right = exchange(fixed, fixed)
    beside = shape(PACKED + ROWS, L)
    tile, to_left, to_right = call(tile_kernel, "tile", (shape(2 * SIZE, L), beside, beside))(
        received, fixed_left, fixed_right, mats
    )
    left, right = exchange(to_left, to_right)
    refs = (left, tile, right, fixed_left, fixed, fixed_right)
    side = shape(FIRST_ROWS, L)
    below, above = swap(*call(sides_kernel, "sides", (side, side), smem=(0,))(side_of, *refs))
    side = shape(WEIGHTS_ROWS, L)
    weights = swap(*call(weights_kernel, "weights", (side, side), smem=(0,))(side_of, *refs))
    refs = (*refs, below, above, mats)
    field, side = shape(ROWS, WIDE, L), shape(SECOND_ROWS, L)
    b, y, low, high = call(right_side_kernel, "right_side", (field, field, side, side), scratch(WIDE, STEPS + 1), smem=(0,))(
        side_of, *refs
    )
    south, north = swap(low, high)
    lat, lon = lax.axis_size("lat"), lax.axis_size("lon")
    near, far = levels(lat, lon)
    small, side = shape(ROWS, COLS, L), shape(THIRD_ROWS, L)
    space = scratch(WIDE, REACH)
    q, g, low, high, sums = call(
        first_image_kernel,
        "first_image",
        (small, shape(STEPS, ROWS, INNER, L), side, side, shape(lat, L)),
        space + [space[0]] * 2,
        smem=(0,),
    )(side_of, *refs, b, y, south, north, *weights)
    sums = lax.all_to_all(sums, "lat", 0, 0, axis_index_groups=near, tiled=True)
    south, north = swap(low, high)
    u = call(second_image_kernel, "second_image", small, scratch(INNER, STEPS), smem=(0,))(
        side_of, *refs, q, g, south, north
    )
    sums = call(add_kernel, "add", shape(4 * lon, L))(sums)
    sums = lax.all_to_all(sums, ("lat", "lon"), 0, 0, axis_index_groups=far, tiled=True)
    return call(finish_kernel, "finish", (small, small))(sums, b, q, u)


def solution(mesh):
    placed = (
        P(("lat", "lon"), None),
        P(("lat", "lon"), None),
        P(("lat", "lon")),
        P(("lat", "lon"), None),
        P(("lat", "lon")),
        P("lat", "lon", None),
        P("lat", "lon"),
        P(),
        P(),
    )
    return jax.shard_map(
        shards,
        mesh=mesh,
        in_specs=placed,
        out_specs=(P("lat", "lon", None), P("lat", "lon", None)),
        check_vma=False,
    )
```

```python
import jax
import jax.numpy as jnp
from jax import lax
from jax.experimental import pallas as pl
from jax.experimental.pallas import tpu as pltpu
from jax.sharding import PartitionSpec as P

F32 = jnp.float32
BF16 = jnp.bfloat16
L = 128
ROWS = 8
COLS = 16
CELLS = ROWS * COLS
STEPS = 3
SLOTS = 256
CAP = 64
WIDE = 3 * COLS
INNER = 2 * COLS
EDGE = COLS // 2
BUCKET = 2 * CAP + 8
REACH = 3 * STEPS

MIB = 1024 * 1024


def call(kernel, name, outs, scratch=(), smem=(), hbm=(), vmem=40, out_space=pltpu.VMEM):
    def run(*args):
        spaces = [pltpu.SMEM if i in smem else pltpu.HBM if i in hbm else pltpu.VMEM for i in range(len(args))]
        specs = [pl.BlockSpec(memory_space=space) for space in spaces]
        return pl.pallas_call(
            kernel,
            name=name,
            out_shape=outs,
            in_specs=specs,
            out_specs=jax.tree.map(lambda _: pl.BlockSpec(memory_space=out_space), outs),
            scratch_shapes=scratch,
            compiler_params=pltpu.CompilerParams(vmem_limit_bytes=vmem * MIB),
        )(*args)

    return run


def shape(*dims, dtype=F32):
    return jax.ShapeDtypeStruct(dims, dtype)


def halves(x):
    high = x.astype(BF16)
    return high, (x - high.astype(F32)).astype(BF16)


def dot(a, b):
    return jnp.dot(a, b, preferred_element_type=F32)


def matrices_kernel(factor_ref, mixing_ref, out_ref):
    for i, ref in enumerate((mixing_ref, factor_ref)):
        for j in range(2):
            m = 0.5 * ref[...]
            high, low = halves(m.T if j else m)
            row = jnp.concatenate([high, low], axis=1)
            out_ref[2 * i + j] = jnp.concatenate([row, row], axis=0)


MIX, MIX_T, FACTOR, FACTOR_T = range(4)


def bucket_kernel(
    departures_hbm, weight_hbm, columns_ref, owner_ref, counts_ref, parity_ref, out_hbm,
    departures_ref, weight_ref, out_ref, sems,
):
    copies = [
        pltpu.make_async_copy(departures_hbm, departures_ref, sems.at[0]),
        pltpu.make_async_copy(weight_hbm, weight_ref, sems.at[1]),
    ]
    for copy in copies:
        copy.start()
    sub = lax.broadcasted_iota(jnp.int32, (SLOTS, SLOTS), 0)
    lane = lax.broadcasted_iota(jnp.int32, (SLOTS, SLOTS), 1)
    owner_row = owner_ref[...].astype(F32)
    owner_col = jnp.sum(jnp.where(sub == lane, owner_row, 0.0), axis=1, keepdims=True)
    same = owner_row == owner_col
    rank_row = jnp.sum(jnp.where(same & (sub < lane), 1.0, 0.0), axis=0, keepdims=True)
    rank_col = jnp.sum(jnp.where(same & (lane < sub), 1.0, 0.0), axis=1, keepdims=True)
    place = (owner_row * CAP + rank_row).astype(jnp.int32)
    pick = lax.broadcasted_iota(jnp.int32, (8 * CAP, SLOTS), 0) == place
    pick = jnp.where(pick, 1.0, 0.0).astype(BF16)
    slot = lax.broadcasted_iota(jnp.int32, (SLOTS, L), 0)
    for copy in copies:
        copy.wait()
    weights = jnp.where(slot < counts_ref[0], weight_ref[...], 0.0)
    parts = halves(weights * departures_ref[...]) + halves(weights)
    data = jnp.concatenate(parts, axis=1)
    number = lax.broadcasted_iota(jnp.int32, (1, SLOTS), 1)
    time = (number - STEPS * ((number * 171) >> 9)).astype(F32)
    tile = lax.broadcasted_iota(jnp.int32, (8, SLOTS), 0).astype(F32)
    here = tile == owner_row
    marks = jnp.concatenate(
        [jnp.where(here, time, 0.0), jnp.where(here, columns_ref[...].astype(F32), 0.0)], axis=0
    )
    target = rank_col + (CAP * parity_ref[0]).astype(F32)
    spread = jnp.where(lax.broadcasted_iota(jnp.int32, (SLOTS, L), 1).astype(F32) == target, 1.0, 0.0)
    codes = dot(marks.astype(BF16), spread.astype(BF16))
    codes = CELLS * codes[:8] + codes[8:]
    sends = []
    for j in range(4):
        moved = dot(pick[2 * j * CAP : 2 * (j + 1) * CAP], data)
        forcing = moved[:, :L] + moved[:, L : 2 * L]
        weights = moved[:, 2 * L : 3 * L] + moved[:, 3 * L :]
        for k in range(2):
            d, rows = 2 * j + k, slice(k * CAP, (k + 1) * CAP)
            out_ref[d, :CAP] = forcing[rows]
            out_ref[d, CAP : 2 * CAP] = weights[rows]
            out_ref[d, 2 * CAP :] = jnp.broadcast_to(codes[d : d + 1], (8, L))
            sends.append(pltpu.make_async_copy(out_ref.at[d], out_hbm.at[d], sems.at[2 + d]))
            sends[-1].start()
    for copy in sends:
        copy.wait()


def fixed_kernel(std_ref, diffusion_ref, out_ref):
    out_ref[:CELLS] = std_ref[...]
    sub = lax.broadcasted_iota(jnp.int32, (COLS, COLS), 0)
    lane = lax.broadcasted_iota(jnp.int32, (COLS, COLS), 1)
    place = lax.broadcasted_iota(jnp.int32, (COLS, L), 1)
    turned = jnp.zeros((COLS, L), F32)
    for r in range(ROWS):
        row = diffusion_ref[r : r + 1]
        column = jnp.sum(jnp.where(sub == lane, row, 0.0), axis=1, keepdims=True)
        turned = turned + jnp.where(place == r, column, 0.0)
    out_ref[CELLS:] = turned


SIZE = STEPS * CELLS
PACKED = SIZE + STEPS * ROWS * EDGE


def tile_kernel(received_ref, fixed_left_ref, fixed_right_ref, m_ref, own_ref, to_left_ref, to_right_ref):
    ones, data = [], []
    cell = lax.broadcasted_iota(jnp.int32, (SIZE, L), 0)
    for j in range(4):
        pair = (2 * j, 2 * j + 1)
        codes = sum(received_ref[s, 2 * CAP : 2 * CAP + 1] for s in pair).astype(jnp.int32)
        ones.append(jnp.where(cell == codes, 1.0, 0.0).astype(BF16))
        for s in pair:
            parts = halves(received_ref[s, :CAP]) + halves(received_ref[s, CAP : 2 * CAP])
            data.append(jnp.concatenate(parts, axis=1))
    total = dot(jnp.concatenate(ones, axis=1), jnp.concatenate(data, axis=0))
    forcing = total[:, :L] + total[:, L : 2 * L]
    weights = total[:, 2 * L : 3 * L] + total[:, 3 * L :]
    for ref in (own_ref, to_left_ref, to_right_ref):
        ref[:SIZE] = forcing
    own_ref[SIZE:] = weights
    for k in range(STEPS * ROWS):
        to = pl.ds(SIZE + k * EDGE, EDGE)
        to_left_ref[to] = weights[k * COLS : k * COLS + EDGE]
        to_right_ref[to] = weights[k * COLS + EDGE : (k + 1) * COLS]
    for r in range(ROWS):
        first = (STEPS - 1) * CELLS + r * COLS
        to_left_ref[PACKED + r : PACKED + r + 1] = weights[first + EDGE : first + EDGE + 1]
        to_right_ref[PACKED + r : PACKED + r + 1] = weights[first + EDGE - 1 : first + EDGE]


def wide(refs, start):
    return jnp.concatenate([ref[start : start + COLS] for ref in refs], axis=0)


class Tile:
    def __init__(self, left_ref, own_ref, right_ref, fixed_left_ref, fixed_ref, fixed_right_ref):
        self.left, self.own, self.right = left_ref, own_ref, right_ref
        self.fixed = (fixed_left_ref, fixed_ref, fixed_right_ref)

    def forcing(self, t, r):
        return wide((self.left, self.own, self.right), t * CELLS + r * COLS)

    def inner_weights(self, t, r):
        start = SIZE + t * CELLS + r * COLS
        packed = pl.ds(SIZE + (t * ROWS + r) * EDGE, EDGE)
        return [self.left[packed], self.own[start : start + COLS], self.right[packed]]

    def weights(self, t, r):
        inner = self.inner_weights(t, r)
        if t < STEPS - 1:
            edges = [jnp.zeros((EDGE, L), F32)] * 2
        else:
            edges = [jnp.broadcast_to(ref[PACKED + r : PACKED + r + 1], (EDGE, L)) for ref in (self.left, self.right)]
        return jnp.concatenate([edges[0], *inner, edges[1]], axis=0)

    def std(self, r):
        return wide(self.fixed, r * COLS)

    def turned(self):
        return wide(self.fixed, CELLS)


def inside(row):
    return row[EDGE : EDGE + INNER]


def padded(row):
    if row.shape[0] == WIDE:
        return row
    edge = jnp.zeros((EDGE, L), F32)
    return jnp.concatenate([edge, row, edge], axis=0)


def places(rows):
    found, total = {}, 0
    for kind, h, width in rows:
        found[kind, h] = (total, width)
        total += width
    return found, total


FIRST, FIRST_ROWS = places(
    [(("f", t), h, WIDE if h < t + 2 else INNER) for t in range(STEPS) for h in range(1, t + 3)]
    + [("std", h, INNER) for h in range(1, STEPS + 1)]
    + [("diffusion", 1, WIDE)]
)
SECOND, SECOND_ROWS = places(
    [("state", h, WIDE if h <= STEPS else INNER) for h in range(1, REACH + 1)]
    + [("b", h, INNER) for h in range(1, STEPS + 1)]
)
WEIGHTS, WEIGHTS_ROWS = places([(("w", t), h, INNER) for t in range(STEPS) for h in range(1, t + 5)])
THIRD, THIRD_ROWS = places([(("g", t), h, INNER) for t in range(STEPS) for h in range(1, t + 2)])


class Sides:
    def __init__(self, parity_ref, chip_ref, core_ref, found):
        self.even = parity_ref[0] == 0
        self.core_ref, self.chip_ref, self.found = core_ref, chip_ref, found

    def send(self, kind, h, row):
        start, width = self.found[kind, h]
        values = [row(r) for r in (h - 1, ROWS - h)]
        low, high = [inside(v) if width < v.shape[0] else v for v in values]
        self.core_ref[start : start + width] = jnp.where(self.even, high, low)
        self.chip_ref[start : start + width] = jnp.where(self.even, low, high)

    def taken(self, kind, r):
        start, width = self.found[kind, -r if r < 0 else r - ROWS + 1]
        core, chip = self.core_ref[start : start + width], self.chip_ref[start : start + width]
        return jnp.where(self.even, chip, core) if r < 0 else jnp.where(self.even, core, chip)


def sides_kernel(*refs):
    tile, sides = Tile(*refs[1:7]), Sides(refs[0], *refs[7:], FIRST)
    for kind, h in FIRST:
        if kind == "std":
            row = tile.std
        elif kind == "diffusion":
            row = lambda r: tile.turned()
        else:
            row = lambda r: tile.forcing(kind[1], r)
        sides.send(kind, h, row)


def weights_kernel(*refs):
    tile, sides = Tile(*refs[1:7]), Sides(refs[0], *refs[7:], WEIGHTS)
    for kind, h in WEIGHTS:
        sides.send(kind, h, lambda r: jnp.concatenate(tile.inner_weights(kind[1], r), axis=0))


def own(r):
    return 0 <= r < ROWS


class Field:
    def __init__(self, width, reach, v_ref, x_ref, y_ref, d_ref, m_ref):
        self.width, self.reach = width, reach
        self.v_ref, self.x_ref, self.y_ref, self.d_ref, self.m_ref = v_ref, x_ref, y_ref, d_ref, m_ref

    def at(self, r):
        return pl.ds((r + self.reach) * self.width, self.width)

    def put(self, r, value):
        self.v_ref[self.at(r)] = value
        high, low = halves(value)
        self.x_ref[self.at(r), :L] = high
        self.x_ref[self.at(r), L:] = low

    def mix(self, first, stop, which):
        rows = pl.ds((first + self.reach) * self.width, (stop - first) * self.width)
        self.y_ref[rows] = dot(self.x_ref[rows], self.m_ref[which])

    def get(self, r):
        return self.v_ref[self.at(r)] + self.y_ref[self.at(r), :L] + self.y_ref[self.at(r), L:]

    def fill_diffusion(self, tile, sides, reach):
        values = {0: tile.turned(), -1: sides.taken("diffusion", -1), 1: sides.taken("diffusion", ROWS)}
        skip = (WIDE - self.width) // 2
        for r in range(-reach, ROWS + reach):
            column = values[r // ROWS][skip : skip + self.width, r % ROWS : r % ROWS + 1]
            self.d_ref[self.at(r)] = jnp.broadcast_to(column, (self.width, L))

    def smooth(self, first, stop, get, put, scaled=False):
        held = []
        for r in range(first, stop):
            value = get(r)
            if scaled and r in (first, stop - 1):
                held.append((value, None, value))
            else:
                d = self.d_ref[self.at(r)]
                held.append((value, d, d * value))
            if len(held) == 3:
                value, d, u = held[1]
                around = held[0][2] + held[2][2] + pltpu.roll(u, 1, 0) + pltpu.roll(u, self.width - 1, 0)
                put(r - 1, value + d * (around - 4.0 * u))
                held.pop(0)

    def forward(self, h, start, seen, scaled=False):
        self.smooth(-h, ROWS + h, start, self.put, scaled)
        for t in range(STEPS):
            first, stop = -h + t + 1, ROWS + h - t - 1
            self.mix(first, stop, MIX)

            def get(r, t=t):
                value = self.get(r)
                seen(t, r, value)
                return value

            if t < STEPS - 1:
                self.smooth(first, stop, get, self.put)
            else:
                for r in range(first, stop):
                    get(r)

    def adjoint(self, h, forcing, std):
        for t in range(STEPS - 1, -1, -1):
            first, stop = -h - t - 1, ROWS + h + t + 1
            self.mix(first, stop, MIX_T)
            if t > 0:
                put = lambda r, value, t=t: self.put(r, value + forcing(t - 1, r))
            else:
                put = lambda r, value: self.put(r, std(r) * value)
            self.smooth(first, stop, self.get, put)
        self.mix(-h, ROWS + h, FACTOR_T)


def scratch(width, reach):
    tall = (ROWS + 2 * reach) * width
    return [
        pltpu.VMEM((tall, L), F32),
        pltpu.VMEM((tall, 2 * L), BF16),
        pltpu.VMEM((tall, 2 * L), F32),
        pltpu.VMEM((tall, L), F32),
    ]


def std_rows(tile, sides):
    return lambda r: tile.std(r) if own(r) else padded(sides.taken("std", r))


def right_side_kernel(parity_ref, *refs):
    tile, sides, m_ref = Tile(*refs[:6]), Sides(parity_ref, *refs[6:8], FIRST), refs[8]
    b_ref, y_ref = refs[9:11]
    out = Sides(parity_ref, *refs[11:13], SECOND)
    field = Field(WIDE, STEPS + 1, *refs[13:17], m_ref)
    field.fill_diffusion(tile, sides, STEPS + 1)
    forcing = lambda t, r: tile.forcing(t, r) if own(r) else padded(sides.taken(("f", t), r))
    std = std_rows(tile, sides)
    for r in range(-STEPS - 1, ROWS + STEPS + 1):
        field.put(r, forcing(STEPS - 1, r))
    field.adjoint(1, forcing, std)
    for r in range(-1, ROWS + 1):
        value = field.get(r)
        field.put(r, value)
        if own(r):
            b_ref[r] = value
    field.mix(-1, ROWS + 1, FACTOR)
    beyond = {}
    for r in range(-1, ROWS + 1):
        state = std(r) * field.get(r)
        if own(r):
            y_ref[r] = state
        else:
            beyond[r] = field.d_ref[field.at(r)] * state
    for kind, h in SECOND:
        out.send(kind, h, lambda r: b_ref[r] if kind == "b" else y_ref[r] if own(r) else beyond[r])


MIDDLE = slice(COLS, 2 * COLS)


def first_image_kernel(parity_ref, *refs):
    tile, sides, m_ref = Tile(*refs[:6]), Sides(parity_ref, *refs[6:8], FIRST), refs[8]
    b_ref, y_ref = refs[9:11]
    more, forced = Sides(parity_ref, *refs[11:13], SECOND), Sides(parity_ref, *refs[13:15], WEIGHTS)
    q_ref, g_ref = refs[15:17]
    out, sums_ref = Sides(parity_ref, *refs[17:19], THIRD), refs[19]
    field = Field(WIDE, REACH, *refs[20:24], m_ref)
    tops = refs[24:26]
    field.fill_diffusion(tile, sides, REACH - 1)
    std = std_rows(tile, sides)

    def weights(t, r):
        return tile.weights(t, r) if own(r) else padded(forced.taken(("w", t), r))

    def start(r):
        if own(r):
            return y_ref[r]
        return padded(more.taken("state", r))

    def force(t, r, value):
        if -t - 4 <= r < ROWS + t + 4:
            if t < STEPS - 1:
                tops[t][field.at(r)] = weights(t, r) * value
            else:
                field.put(r, weights(t, r) * value)

    field.forward(REACH, start, force, scaled=True)
    field.adjoint(STEPS, lambda t, r: tops[t][field.at(r)], std)
    sums = [jnp.zeros((COLS, L), F32) for _ in range(4)]
    for r in range(-STEPS, ROWS + STEPS):
        b = b_ref[r] if own(r) else padded(more.taken("b", r))
        q = b + field.get(r)
        field.put(r, q)
        if own(r):
            b, q = b[MIDDLE], q[MIDDLE]
            q_ref[r] = q
            for i, term in enumerate((b * b, b * q, q * q, q * q)):
                sums[i] = sums[i] + term
    field.mix(-STEPS, ROWS + STEPS, FACTOR)

    def keep(t, r, value):
        if own(r):
            forcing = tile.weights(t, r) * value
            sums[3] = sums[3] + forcing[MIDDLE] * value[MIDDLE]
            g_ref[t, r] = inside(forcing)

    field.forward(STEPS, lambda r: std(r) * field.get(r), keep)
    for kind, h in THIRD:
        out.send(kind, h, lambda r: g_ref[kind[1], r])
    lane = lax.broadcasted_iota(jnp.int32, (1, L), 1)
    row = jnp.zeros((1, L), F32)
    for i, term in enumerate(sums):
        total = jnp.sum(jnp.sum(term, axis=0, keepdims=True), axis=1, keepdims=True)
        row = row + jnp.where(lane == i, total, 0.0)
    sums_ref[...] = jnp.broadcast_to(row, sums_ref.shape)


def second_image_kernel(parity_ref, *refs):
    tile, sides, m_ref = Tile(*refs[:6]), Sides(parity_ref, *refs[6:8], FIRST), refs[8]
    q_ref, g_ref = refs[9:11]
    more = Sides(parity_ref, *refs[11:13], THIRD)
    u_ref = refs[13]
    field = Field(INNER, STEPS, *refs[14:18], m_ref)
    field.fill_diffusion(tile, sides, STEPS)
    forcing = lambda t, r: g_ref[t, r] if own(r) else more.taken(("g", t), r)
    for r in range(-STEPS, ROWS + STEPS):
        field.put(r, forcing(STEPS - 1, r))
    field.adjoint(0, forcing, lambda r: inside(tile.std(r)))
    for r in range(ROWS):
        u_ref[r] = q_ref[r] + field.get(r)[EDGE : EDGE + COLS]


def levels(lat, lon):
    row = 2 * lon
    first = [[2 * i + core for i in range(lat // 2)] for core in range(2)]
    second = [[i * row + k for k in range(row)] for i in range(lat // 2)]
    return first, second


def add_kernel(parts_ref, out_ref):
    out_ref[...] = jnp.broadcast_to(0.5 * jnp.sum(parts_ref[...], axis=0, keepdims=True), out_ref.shape)


def finish_kernel(parts_ref, b_ref, q_ref, u_ref, solution_ref, residual_ref):
    total = jnp.sum(parts_ref[...], axis=0, keepdims=True)
    bb, bq, qq, qu = (total[:, i : i + 1] for i in range(4))
    first = bb / bq
    norm = first * first * qq - bb
    gain = 1.0 + norm / bb
    curve = gain * gain * bq - 2.0 * first * gain * qq + first * first * qu
    second = norm / curve
    along_b = first + second * gain
    along_q = first * second
    for r in range(ROWS):
        b, q = b_ref[r, MIDDLE], q_ref[r]
        solution_ref[r] = along_b * b - along_q * q
        residual_ref[r] = b - along_b * q + along_q * u_ref[r]


def exchange(to_before, to_after):
    size = lax.axis_size("lon")
    up = [(i, (i + 1) % size) for i in range(size)]
    down = [(j, i) for i, j in up]
    return lax.ppermute(to_after, "lon", up), lax.ppermute(to_before, "lon", down)


def swap(chip, core):
    size = lax.axis_size("lat")
    pairs = [[(i, i + 1) for i in range(first, size - 1, 2)] for first in (0, 1)]
    both = [p + [(j, i) for i, j in p] for p in pairs]
    return lax.ppermute(chip, "lat", both[1]), lax.ppermute(core, "lat", both[0])


def shards(
    departures, obs_weight, obs_columns, obs_owner, obs_counts, background_std, diffusion, level_factor, model_mixing
):
    parity = (lax.axis_index("lon") % 2).astype(jnp.int32).reshape(1)
    side_of = (lax.axis_index("lat") % 2).astype(jnp.int32).reshape(1)
    slots = pltpu.VMEM((SLOTS, L), F32)
    buckets = call(
        bucket_kernel,
        "bucket",
        shape(8, BUCKET, L),
        [slots, slots, pltpu.VMEM((8, BUCKET, L), F32), pltpu.SemaphoreType.DMA((10,))],
        smem=(4, 5),
        hbm=(0, 1),
        vmem=60,
        out_space=pltpu.HBM,
    )(departures, obs_weight, obs_columns.reshape(1, SLOTS), obs_owner.reshape(1, SLOTS), obs_counts, parity)
    received = lax.all_to_all(buckets, "lon", 0, 0)
    mats = call(matrices_kernel, "matrices", shape(4, 2 * L, 2 * L, dtype=BF16))(level_factor, model_mixing)
    fixed = call(fixed_kernel, "fixed", shape(CELLS + COLS, L))(background_std.reshape(CELLS, L), diffusion)
    fixed_left, fixed_right = exchange(fixed, fixed)
    beside = shape(PACKED + ROWS, L)
    tile, to_left, to_right = call(tile_kernel, "tile", (shape(2 * SIZE, L), beside, beside))(
        received, fixed_left, fixed_right, mats
    )
    left, right = exchange(to_left, to_right)
    refs = (left, tile, right, fixed_left, fixed, fixed_right)
    side = shape(FIRST_ROWS, L)
    below, above = swap(*call(sides_kernel, "sides", (side, side), smem=(0,))(side_of, *refs))
    side = shape(WEIGHTS_ROWS, L)
    weights = swap(*call(weights_kernel, "weights", (side, side), smem=(0,))(side_of, *refs))
    refs = (*refs, below, above, mats)
    field, side = shape(ROWS, WIDE, L), shape(SECOND_ROWS, L)
    b, y, low, high = call(right_side_kernel, "right_side", (field, field, side, side), scratch(WIDE, STEPS + 1), smem=(0,))(
        side_of, *refs
    )
    south, north = swap(low, high)
    lat, lon = lax.axis_size("lat"), lax.axis_size("lon")
    alike, row = levels(lat, lon)
    small, side = shape(ROWS, COLS, L), shape(THIRD_ROWS, L)
    space = scratch(WIDE, REACH)
    q, g, low, high, sums = call(
        first_image_kernel,
        "first_image",
        (small, shape(STEPS, ROWS, INNER, L), side, side, shape(lat, L)),
        space + [space[0]] * 2,
        smem=(0,),
    )(side_of, *refs, b, y, south, north, *weights)
    sums = lax.all_to_all(sums, "lat", 0, 0, axis_index_groups=alike, tiled=True)
    south, north = swap(low, high)
    u = call(second_image_kernel, "second_image", small, scratch(INNER, STEPS), smem=(0,))(
        side_of, *refs, q, g, south, north
    )
    sums = call(add_kernel, "add", shape(2 * lon, L))(sums)
    sums = lax.all_to_all(sums, ("lat", "lon"), 0, 0, axis_index_groups=row, tiled=True)
    return call(finish_kernel, "finish", (small, small))(sums, b, q, u)


def solution(mesh):
    placed = (
        P(("lat", "lon"), None),
        P(("lat", "lon"), None),
        P(("lat", "lon")),
        P(("lat", "lon"), None),
        P(("lat", "lon")),
        P("lat", "lon", None),
        P("lat", "lon"),
        P(),
        P(),
    )
    return jax.shard_map(
        shards,
        mesh=mesh,
        in_specs=placed,
        out_specs=(P("lat", "lon", None), P("lat", "lon", None)),
        check_vma=False,
    )
```

```python
import jax
import jax.numpy as jnp
from jax import lax
from jax.experimental import pallas as pl
from jax.experimental.pallas import tpu as pltpu
from jax.sharding import PartitionSpec as P

F32 = jnp.float32
BF16 = jnp.bfloat16
L = 128
ROWS = 8
COLS = 16
CELLS = ROWS * COLS
STEPS = 3
SLOTS = 256
CAP = 64
WIDE = 3 * COLS
INNER = 2 * COLS
EDGE = COLS // 2
BUCKET = 2 * CAP + 8
REACH = 3 * STEPS

MIB = 1024 * 1024


def call(kernel, name, outs, scratch=(), smem=(), hbm=(), vmem=40, out_space=pltpu.VMEM):
    def run(*args):
        spaces = [pltpu.SMEM if i in smem else pltpu.HBM if i in hbm else pltpu.VMEM for i in range(len(args))]
        specs = [pl.BlockSpec(memory_space=space) for space in spaces]
        return pl.pallas_call(
            kernel,
            name=name,
            out_shape=outs,
            in_specs=specs,
            out_specs=jax.tree.map(lambda _: pl.BlockSpec(memory_space=out_space), outs),
            scratch_shapes=scratch,
            compiler_params=pltpu.CompilerParams(vmem_limit_bytes=vmem * MIB),
        )(*args)

    return run


def shape(*dims, dtype=F32):
    return jax.ShapeDtypeStruct(dims, dtype)


def halves(x):
    high = x.astype(BF16)
    return high, (x - high.astype(F32)).astype(BF16)


def dot(a, b):
    return jnp.dot(a, b, preferred_element_type=F32)


def matrices_kernel(factor_ref, mixing_ref, out_ref):
    for i, ref in enumerate((mixing_ref, factor_ref)):
        for j in range(2):
            m = 0.5 * ref[...]
            high, low = halves(m.T if j else m)
            row = jnp.concatenate([high, low], axis=1)
            out_ref[2 * i + j] = jnp.concatenate([row, row], axis=0)


MIX, MIX_T, FACTOR, FACTOR_T = range(4)


def bucket_kernel(
    departures_hbm, weight_hbm, columns_ref, owner_ref, counts_ref, parity_ref, out_hbm,
    departures_ref, weight_ref, out_ref, sems,
):
    copies = [
        pltpu.make_async_copy(departures_hbm, departures_ref, sems.at[0]),
        pltpu.make_async_copy(weight_hbm, weight_ref, sems.at[1]),
    ]
    for copy in copies:
        copy.start()
    sub = lax.broadcasted_iota(jnp.int32, (SLOTS, SLOTS), 0)
    lane = lax.broadcasted_iota(jnp.int32, (SLOTS, SLOTS), 1)
    owner_row = owner_ref[...].astype(F32)
    owner_col = jnp.sum(jnp.where(sub == lane, owner_row, 0.0), axis=1, keepdims=True)
    same = owner_row == owner_col
    rank_row = jnp.sum(jnp.where(same & (sub < lane), 1.0, 0.0), axis=0, keepdims=True)
    rank_col = jnp.sum(jnp.where(same & (lane < sub), 1.0, 0.0), axis=1, keepdims=True)
    place = (owner_row * CAP + rank_row).astype(jnp.int32)
    pick = lax.broadcasted_iota(jnp.int32, (8 * CAP, SLOTS), 0) == place
    pick = jnp.where(pick, 1.0, 0.0).astype(BF16)
    slot = lax.broadcasted_iota(jnp.int32, (SLOTS, L), 0)
    for copy in copies:
        copy.wait()
    weights = jnp.where(slot < counts_ref[0], weight_ref[...], 0.0)
    parts = halves(weights * departures_ref[...]) + halves(weights)
    data = jnp.concatenate(parts, axis=1)
    number = lax.broadcasted_iota(jnp.int32, (1, SLOTS), 1)
    time = (number - STEPS * ((number * 171) >> 9)).astype(F32)
    tile = lax.broadcasted_iota(jnp.int32, (8, SLOTS), 0).astype(F32)
    here = tile == owner_row
    marks = jnp.concatenate(
        [jnp.where(here, time, 0.0), jnp.where(here, columns_ref[...].astype(F32), 0.0)], axis=0
    )
    target = rank_col + (CAP * parity_ref[0]).astype(F32)
    spread = jnp.where(lax.broadcasted_iota(jnp.int32, (SLOTS, L), 1).astype(F32) == target, 1.0, 0.0)
    codes = dot(marks.astype(BF16), spread.astype(BF16))
    codes = CELLS * codes[:8] + codes[8:]
    sends = []
    for j in range(4):
        moved = dot(pick[2 * j * CAP : 2 * (j + 1) * CAP], data)
        forcing = moved[:, :L] + moved[:, L : 2 * L]
        weights = moved[:, 2 * L : 3 * L] + moved[:, 3 * L :]
        for k in range(2):
            d, rows = 2 * j + k, slice(k * CAP, (k + 1) * CAP)
            out_ref[d, :CAP] = forcing[rows]
            out_ref[d, CAP : 2 * CAP] = weights[rows]
            out_ref[d, 2 * CAP :] = jnp.broadcast_to(codes[d : d + 1], (8, L))
            sends.append(pltpu.make_async_copy(out_ref.at[d], out_hbm.at[d], sems.at[2 + d]))
            sends[-1].start()
    for copy in sends:
        copy.wait()


def fixed_kernel(std_ref, diffusion_ref, out_ref):
    out_ref[:CELLS] = std_ref[...]
    sub = lax.broadcasted_iota(jnp.int32, (COLS, COLS), 0)
    lane = lax.broadcasted_iota(jnp.int32, (COLS, COLS), 1)
    place = lax.broadcasted_iota(jnp.int32, (COLS, L), 1)
    turned = jnp.zeros((COLS, L), F32)
    for r in range(ROWS):
        row = diffusion_ref[r : r + 1]
        column = jnp.sum(jnp.where(sub == lane, row, 0.0), axis=1, keepdims=True)
        turned = turned + jnp.where(place == r, column, 0.0)
    out_ref[CELLS:] = turned


SIZE = STEPS * CELLS
PACKED = SIZE + STEPS * ROWS * EDGE


def tile_kernel(received_ref, fixed_left_ref, fixed_right_ref, m_ref, own_ref, to_left_ref, to_right_ref):
    ones, data = [], []
    cell = lax.broadcasted_iota(jnp.int32, (SIZE, L), 0)
    for j in range(4):
        pair = (2 * j, 2 * j + 1)
        codes = sum(received_ref[s, 2 * CAP : 2 * CAP + 1] for s in pair).astype(jnp.int32)
        ones.append(jnp.where(cell == codes, 1.0, 0.0).astype(BF16))
        for s in pair:
            parts = halves(received_ref[s, :CAP]) + halves(received_ref[s, CAP : 2 * CAP])
            data.append(jnp.concatenate(parts, axis=1))
    total = dot(jnp.concatenate(ones, axis=1), jnp.concatenate(data, axis=0))
    forcing = total[:, :L] + total[:, L : 2 * L]
    weights = total[:, 2 * L : 3 * L] + total[:, 3 * L :]
    for ref in (own_ref, to_left_ref, to_right_ref):
        ref[:SIZE] = forcing
    own_ref[SIZE:] = weights
    for k in range(STEPS * ROWS):
        to = pl.ds(SIZE + k * EDGE, EDGE)
        to_left_ref[to] = weights[k * COLS : k * COLS + EDGE]
        to_right_ref[to] = weights[k * COLS + EDGE : (k + 1) * COLS]
    for r in range(ROWS):
        first = (STEPS - 1) * CELLS + r * COLS
        to_left_ref[PACKED + r : PACKED + r + 1] = weights[first + EDGE : first + EDGE + 1]
        to_right_ref[PACKED + r : PACKED + r + 1] = weights[first + EDGE - 1 : first + EDGE]


def wide(refs, start):
    return jnp.concatenate([ref[start : start + COLS] for ref in refs], axis=0)


class Tile:
    def __init__(self, left_ref, own_ref, right_ref, fixed_left_ref, fixed_ref, fixed_right_ref):
        self.left, self.own, self.right = left_ref, own_ref, right_ref
        self.fixed = (fixed_left_ref, fixed_ref, fixed_right_ref)

    def forcing(self, t, r):
        return wide((self.left, self.own, self.right), t * CELLS + r * COLS)

    def inner_weights(self, t, r):
        start = SIZE + t * CELLS + r * COLS
        packed = pl.ds(SIZE + (t * ROWS + r) * EDGE, EDGE)
        return [self.left[packed], self.own[start : start + COLS], self.right[packed]]

    def weights(self, t, r):
        inner = self.inner_weights(t, r)
        if t < STEPS - 1:
            edges = [jnp.zeros((EDGE, L), F32)] * 2
        else:
            edges = [jnp.broadcast_to(ref[PACKED + r : PACKED + r + 1], (EDGE, L)) for ref in (self.left, self.right)]
        return jnp.concatenate([edges[0], *inner, edges[1]], axis=0)

    def std(self, r):
        return wide(self.fixed, r * COLS)

    def turned(self):
        return wide(self.fixed, CELLS)


def inside(row):
    return row[EDGE : EDGE + INNER]


def padded(row):
    if row.shape[0] == WIDE:
        return row
    edge = jnp.zeros((EDGE, L), F32)
    return jnp.concatenate([edge, row, edge], axis=0)


def places(rows):
    found, total = {}, 0
    for kind, h, width in rows:
        found[kind, h] = (total, width)
        total += width
    return found, total


FIRST, FIRST_ROWS = places(
    [(("f", t), h, WIDE if h < t + 2 else INNER) for t in range(STEPS) for h in range(1, t + 3)]
    + [("std", h, INNER) for h in range(1, STEPS + 1)]
    + [("diffusion", 1, WIDE)]
)
SECOND, SECOND_ROWS = places(
    [("state", h, WIDE if h <= STEPS else INNER) for h in range(1, REACH + 1)]
    + [("b", h, INNER) for h in range(1, STEPS + 1)]
)
WEIGHTS, WEIGHTS_ROWS = places([(("w", t), h, INNER) for t in range(STEPS) for h in range(1, t + 5)])
THIRD, THIRD_ROWS = places([(("g", t), h, INNER) for t in range(STEPS) for h in range(1, t + 2)])


class Sides:
    def __init__(self, parity_ref, chip_ref, core_ref, found):
        self.even = parity_ref[0] == 0
        self.core_ref, self.chip_ref, self.found = core_ref, chip_ref, found

    def send(self, kind, h, row):
        start, width = self.found[kind, h]
        values = [row(r) for r in (h - 1, ROWS - h)]
        low, high = [inside(v) if width < v.shape[0] else v for v in values]
        self.core_ref[start : start + width] = jnp.where(self.even, high, low)
        self.chip_ref[start : start + width] = jnp.where(self.even, low, high)

    def taken(self, kind, r):
        start, width = self.found[kind, -r if r < 0 else r - ROWS + 1]
        core, chip = self.core_ref[start : start + width], self.chip_ref[start : start + width]
        return jnp.where(self.even, chip, core) if r < 0 else jnp.where(self.even, core, chip)


def sides_kernel(*refs):
    tile, sides = Tile(*refs[1:7]), Sides(refs[0], *refs[7:], FIRST)
    for kind, h in FIRST:
        if kind == "std":
            row = tile.std
        elif kind == "diffusion":
            row = lambda r: tile.turned()
        else:
            row = lambda r: tile.forcing(kind[1], r)
        sides.send(kind, h, row)


def weights_kernel(*refs):
    tile, sides = Tile(*refs[1:7]), Sides(refs[0], *refs[7:], WEIGHTS)
    for kind, h in WEIGHTS:
        sides.send(kind, h, lambda r: jnp.concatenate(tile.inner_weights(kind[1], r), axis=0))


def own(r):
    return 0 <= r < ROWS


class Field:
    def __init__(self, width, reach, v_ref, x_ref, y_ref, d_ref, m_ref):
        self.width, self.reach = width, reach
        self.v_ref, self.x_ref, self.y_ref, self.d_ref, self.m_ref = v_ref, x_ref, y_ref, d_ref, m_ref

    def at(self, r):
        return pl.ds((r + self.reach) * self.width, self.width)

    def put(self, r, value):
        self.v_ref[self.at(r)] = value
        high, low = halves(value)
        self.x_ref[self.at(r), :L] = high
        self.x_ref[self.at(r), L:] = low

    def mix(self, first, stop, which):
        rows = pl.ds((first + self.reach) * self.width, (stop - first) * self.width)
        self.y_ref[rows] = dot(self.x_ref[rows], self.m_ref[which])

    def get(self, r):
        return self.v_ref[self.at(r)] + self.y_ref[self.at(r), :L] + self.y_ref[self.at(r), L:]

    def fill_diffusion(self, tile, sides, reach):
        values = {0: tile.turned(), -1: sides.taken("diffusion", -1), 1: sides.taken("diffusion", ROWS)}
        skip = (WIDE - self.width) // 2
        for r in range(-reach, ROWS + reach):
            column = values[r // ROWS][skip : skip + self.width, r % ROWS : r % ROWS + 1]
            self.d_ref[self.at(r)] = jnp.broadcast_to(column, (self.width, L))

    def smooth(self, first, stop, get, put, scaled=False):
        held = []
        for r in range(first, stop):
            value = get(r)
            if scaled and r in (first, stop - 1):
                held.append((value, None, value))
            else:
                d = self.d_ref[self.at(r)]
                held.append((value, d, d * value))
            if len(held) == 3:
                value, d, u = held[1]
                around = held[0][2] + held[2][2] + pltpu.roll(u, 1, 0) + pltpu.roll(u, self.width - 1, 0)
                put(r - 1, value + d * (around - 4.0 * u))
                held.pop(0)

    def forward(self, h, start, seen, scaled=False):
        self.smooth(-h, ROWS + h, start, self.put, scaled)
        for t in range(STEPS):
            first, stop = -h + t + 1, ROWS + h - t - 1
            self.mix(first, stop, MIX)

            def get(r, t=t):
                value = self.get(r)
                seen(t, r, value)
                return value

            if t < STEPS - 1:
                self.smooth(first, stop, get, self.put)
            else:
                for r in range(first, stop):
                    get(r)

    def adjoint(self, h, forcing, std, last=None):
        for t in range(STEPS - 1, -1, -1):
            first, stop = -h - t - 1, ROWS + h + t + 1
            self.mix(first, stop, MIX_T)
            if t > 0:
                put = lambda r, value, t=t: self.put(r, value + forcing(t - 1, r))
            elif last is None:
                put = lambda r, value: self.put(r, std(r) * value)
            else:
                put = lambda r, value: last.put(r, std(r) * inside(value))
            self.smooth(first, stop, self.get, put)
        (last or self).mix(-h, ROWS + h, FACTOR_T)


def scratch(width, reach):
    tall = (ROWS + 2 * reach) * width
    return [
        pltpu.VMEM((tall, L), F32),
        pltpu.VMEM((tall, 2 * L), BF16),
        pltpu.VMEM((tall, 2 * L), F32),
        pltpu.VMEM((tall, L), F32),
    ]


def std_rows(tile, sides):
    return lambda r: tile.std(r) if own(r) else padded(sides.taken("std", r))


def right_side_kernel(parity_ref, *refs):
    tile, sides, m_ref = Tile(*refs[:6]), Sides(parity_ref, *refs[6:8], FIRST), refs[8]
    b_ref, y_ref = refs[9:11]
    out = Sides(parity_ref, *refs[11:13], SECOND)
    field = Field(WIDE, STEPS + 1, *refs[13:17], m_ref)
    field.fill_diffusion(tile, sides, STEPS + 1)
    forcing = lambda t, r: tile.forcing(t, r) if own(r) else padded(sides.taken(("f", t), r))
    std = std_rows(tile, sides)
    for r in range(-STEPS - 1, ROWS + STEPS + 1):
        field.put(r, forcing(STEPS - 1, r))
    field.adjoint(1, forcing, std)
    for r in range(-1, ROWS + 1):
        value = field.get(r)
        field.put(r, value)
        if own(r):
            b_ref[r] = value
    field.mix(-1, ROWS + 1, FACTOR)
    beyond = {}
    for r in range(-1, ROWS + 1):
        state = std(r) * field.get(r)
        if own(r):
            y_ref[r] = state
        else:
            beyond[r] = field.d_ref[field.at(r)] * state
    for kind, h in SECOND:
        out.send(kind, h, lambda r: b_ref[r] if kind == "b" else y_ref[r] if own(r) else beyond[r])


MIDDLE = slice(COLS, 2 * COLS)


def first_image_kernel(parity_ref, *refs):
    tile, sides, m_ref = Tile(*refs[:6]), Sides(parity_ref, *refs[6:8], FIRST), refs[8]
    b_ref, y_ref = refs[9:11]
    more, forced = Sides(parity_ref, *refs[11:13], SECOND), Sides(parity_ref, *refs[13:15], WEIGHTS)
    q_ref, g_ref = refs[15:17]
    out, sums_ref = Sides(parity_ref, *refs[17:19], THIRD), refs[19]
    field = Field(WIDE, REACH, *refs[20:24], m_ref)
    tops = refs[24:26]
    inner = Field(INNER, STEPS, *refs[26:30], m_ref)
    field.fill_diffusion(tile, sides, REACH - 1)
    for r in range(-STEPS, ROWS + STEPS):
        inner.d_ref[inner.at(r)] = inside(field.d_ref[field.at(r)])
    wide_std = std_rows(tile, sides)
    std = lambda r: inside(wide_std(r))

    def weights(t, r):
        return tile.weights(t, r) if own(r) else padded(forced.taken(("w", t), r))

    def start(r):
        if own(r):
            return y_ref[r]
        return padded(more.taken("state", r))

    def force(t, r, value):
        if -t - 4 <= r < ROWS + t + 4:
            if t < STEPS - 1:
                tops[t][field.at(r)] = weights(t, r) * value
            else:
                field.put(r, weights(t, r) * value)

    field.forward(REACH, start, force, scaled=True)
    field.adjoint(STEPS, lambda t, r: tops[t][field.at(r)], std, inner)
    sums = [jnp.zeros((COLS, L), F32) for _ in range(4)]
    for r in range(-STEPS, ROWS + STEPS):
        b = inside(b_ref[r]) if own(r) else more.taken("b", r)
        q = b + inner.get(r)
        inner.put(r, q)
        if own(r):
            b, q = b[EDGE : EDGE + COLS], q[EDGE : EDGE + COLS]
            q_ref[r] = q
            for i, term in enumerate((b * b, b * q, q * q, q * q)):
                sums[i] = sums[i] + term
    inner.mix(-STEPS, ROWS + STEPS, FACTOR)

    def keep(t, r, value):
        if own(r):
            forcing = jnp.concatenate(tile.inner_weights(t, r), axis=0) * value
            sums[3] = sums[3] + forcing[EDGE : EDGE + COLS] * value[EDGE : EDGE + COLS]
            g_ref[t, r] = forcing

    inner.forward(STEPS, lambda r: std(r) * inner.get(r), keep)
    for kind, h in THIRD:
        out.send(kind, h, lambda r: g_ref[kind[1], r])
    lane = lax.broadcasted_iota(jnp.int32, (1, L), 1)
    row = jnp.zeros((1, L), F32)
    for i, term in enumerate(sums):
        total = jnp.sum(jnp.sum(term, axis=0, keepdims=True), axis=1, keepdims=True)
        row = row + jnp.where(lane == i, total, 0.0)
    sums_ref[...] = jnp.broadcast_to(row, sums_ref.shape)


def second_image_kernel(parity_ref, *refs):
    tile, sides, m_ref = Tile(*refs[:6]), Sides(parity_ref, *refs[6:8], FIRST), refs[8]
    q_ref, g_ref = refs[9:11]
    more = Sides(parity_ref, *refs[11:13], THIRD)
    u_ref = refs[13]
    field = Field(INNER, STEPS, *refs[14:18], m_ref)
    field.fill_diffusion(tile, sides, STEPS)
    forcing = lambda t, r: g_ref[t, r] if own(r) else more.taken(("g", t), r)
    for r in range(-STEPS, ROWS + STEPS):
        field.put(r, forcing(STEPS - 1, r))
    field.adjoint(0, forcing, lambda r: inside(tile.std(r)))
    for r in range(ROWS):
        u_ref[r] = q_ref[r] + field.get(r)[EDGE : EDGE + COLS]


def levels(lat, lon):
    quarter = lat // 4
    near = [[i * quarter + k for k in range(quarter)] for i in range(4)]
    far = [[(i * quarter + k) * lon + j for i in range(4) for j in range(lon)] for k in range(quarter)]
    return near, far


def add_kernel(parts_ref, out_ref):
    out_ref[...] = jnp.broadcast_to(0.25 * jnp.sum(parts_ref[...], axis=0, keepdims=True), out_ref.shape)


def finish_kernel(parts_ref, b_ref, q_ref, u_ref, solution_ref, residual_ref):
    total = jnp.sum(parts_ref[...], axis=0, keepdims=True)
    bb, bq, qq, qu = (total[:, i : i + 1] for i in range(4))
    first = bb / bq
    norm = first * first * qq - bb
    gain = 1.0 + norm / bb
    curve = gain * gain * bq - 2.0 * first * gain * qq + first * first * qu
    second = norm / curve
    along_b = first + second * gain
    along_q = first * second
    for r in range(ROWS):
        b, q = b_ref[r, MIDDLE], q_ref[r]
        solution_ref[r] = along_b * b - along_q * q
        residual_ref[r] = b - along_b * q + along_q * u_ref[r]


def exchange(to_before, to_after):
    size = lax.axis_size("lon")
    up = [(i, (i + 1) % size) for i in range(size)]
    down = [(j, i) for i, j in up]
    return lax.ppermute(to_after, "lon", up), lax.ppermute(to_before, "lon", down)


def swap(chip, core):
    size = lax.axis_size("lat")
    pairs = [[(i, i + 1) for i in range(first, size - 1, 2)] for first in (0, 1)]
    both = [p + [(j, i) for i, j in p] for p in pairs]
    return lax.ppermute(chip, "lat", both[1]), lax.ppermute(core, "lat", both[0])


def shards(
    departures, obs_weight, obs_columns, obs_owner, obs_counts, background_std, diffusion, level_factor, model_mixing
):
    parity = (lax.axis_index("lon") % 2).astype(jnp.int32).reshape(1)
    side_of = (lax.axis_index("lat") % 2).astype(jnp.int32).reshape(1)
    slots = pltpu.VMEM((SLOTS, L), F32)
    buckets = call(
        bucket_kernel,
        "bucket",
        shape(8, BUCKET, L),
        [slots, slots, pltpu.VMEM((8, BUCKET, L), F32), pltpu.SemaphoreType.DMA((10,))],
        smem=(4, 5),
        hbm=(0, 1),
        vmem=60,
        out_space=pltpu.HBM,
    )(departures, obs_weight, obs_columns.reshape(1, SLOTS), obs_owner.reshape(1, SLOTS), obs_counts, parity)
    received = lax.all_to_all(buckets, "lon", 0, 0)
    mats = call(matrices_kernel, "matrices", shape(4, 2 * L, 2 * L, dtype=BF16))(level_factor, model_mixing)
    fixed = call(fixed_kernel, "fixed", shape(CELLS + COLS, L))(background_std.reshape(CELLS, L), diffusion)
    fixed_left, fixed_right = exchange(fixed, fixed)
    beside = shape(PACKED + ROWS, L)
    tile, to_left, to_right = call(tile_kernel, "tile", (shape(2 * SIZE, L), beside, beside))(
        received, fixed_left, fixed_right, mats
    )
    left, right = exchange(to_left, to_right)
    refs = (left, tile, right, fixed_left, fixed, fixed_right)
    side = shape(FIRST_ROWS, L)
    below, above = swap(*call(sides_kernel, "sides", (side, side), smem=(0,))(side_of, *refs))
    side = shape(WEIGHTS_ROWS, L)
    weights = swap(*call(weights_kernel, "weights", (side, side), smem=(0,))(side_of, *refs))
    refs = (*refs, below, above, mats)
    field, side = shape(ROWS, WIDE, L), shape(SECOND_ROWS, L)
    b, y, low, high = call(right_side_kernel, "right_side", (field, field, side, side), scratch(WIDE, STEPS + 1), smem=(0,))(
        side_of, *refs
    )
    south, north = swap(low, high)
    lat, lon = lax.axis_size("lat"), lax.axis_size("lon")
    near, far = levels(lat, lon)
    small, side = shape(ROWS, COLS, L), shape(THIRD_ROWS, L)
    space = scratch(WIDE, REACH)
    q, g, low, high, sums = call(
        first_image_kernel,
        "first_image",
        (small, shape(STEPS, ROWS, INNER, L), side, side, shape(lat, L)),
        space + [space[0]] * 2 + scratch(INNER, STEPS),
        smem=(0,),
    )(side_of, *refs, b, y, south, north, *weights)
    sums = lax.all_to_all(sums, "lat", 0, 0, axis_index_groups=near, tiled=True)
    south, north = swap(low, high)
    u = call(second_image_kernel, "second_image", small, scratch(INNER, STEPS), smem=(0,))(
        side_of, *refs, q, g, south, north
    )
    sums = call(add_kernel, "add", shape(4 * lon, L))(sums)
    sums = lax.all_to_all(sums, ("lat", "lon"), 0, 0, axis_index_groups=far, tiled=True)
    return call(finish_kernel, "finish", (small, small))(sums, b, q, u)


def solution(mesh):
    placed = (
        P(("lat", "lon"), None),
        P(("lat", "lon"), None),
        P(("lat", "lon")),
        P(("lat", "lon"), None),
        P(("lat", "lon")),
        P("lat", "lon", None),
        P("lat", "lon"),
        P(),
        P(),
    )
    return jax.shard_map(
        shards,
        mesh=mesh,
        in_specs=placed,
        out_specs=(P("lat", "lon", None), P("lat", "lon", None)),
        check_vma=False,
    )
```

```python
import jax
import jax.numpy as jnp
from jax import lax
from jax.experimental import pallas as pl
from jax.experimental.pallas import tpu as pltpu
from jax.sharding import PartitionSpec as P

F32 = jnp.float32
BF16 = jnp.bfloat16
L = 128
ROWS = 8
COLS = 16
CELLS = ROWS * COLS
STEPS = 3
SLOTS = 256
CAP = 64
WIDE = 3 * COLS
INNER = 2 * COLS
EDGE = COLS // 2
BUCKET = 2 * CAP + 8
REACH = 3 * STEPS

MIB = 1024 * 1024


def call(kernel, name, outs, scratch=(), smem=(), hbm=(), vmem=40, out_space=pltpu.VMEM):
    def run(*args):
        spaces = [pltpu.SMEM if i in smem else pltpu.HBM if i in hbm else pltpu.VMEM for i in range(len(args))]
        specs = [pl.BlockSpec(memory_space=space) for space in spaces]
        return pl.pallas_call(
            kernel,
            name=name,
            out_shape=outs,
            in_specs=specs,
            out_specs=jax.tree.map(lambda _: pl.BlockSpec(memory_space=out_space), outs),
            scratch_shapes=scratch,
            compiler_params=pltpu.CompilerParams(vmem_limit_bytes=vmem * MIB),
        )(*args)

    return run


def shape(*dims, dtype=F32):
    return jax.ShapeDtypeStruct(dims, dtype)


def halves(x):
    high = x.astype(BF16)
    return high, (x - high.astype(F32)).astype(BF16)


def dot(a, b):
    return jnp.dot(a, b, preferred_element_type=F32)


def matrices_kernel(factor_ref, mixing_ref, out_ref):
    for i, ref in enumerate((mixing_ref, factor_ref)):
        for j in range(2):
            m = 0.5 * ref[...]
            high, low = halves(m.T if j else m)
            row = jnp.concatenate([high, low], axis=1)
            out_ref[2 * i + j] = jnp.concatenate([row, row], axis=0)


MIX, MIX_T, FACTOR, FACTOR_T = range(4)


def bucket_kernel(
    departures_hbm, weight_hbm, columns_ref, owner_ref, counts_ref, parity_ref, out_hbm,
    departures_ref, weight_ref, out_ref, sems,
):
    copies = [
        pltpu.make_async_copy(departures_hbm, departures_ref, sems.at[0]),
        pltpu.make_async_copy(weight_hbm, weight_ref, sems.at[1]),
    ]
    for copy in copies:
        copy.start()
    sub = lax.broadcasted_iota(jnp.int32, (SLOTS, SLOTS), 0)
    lane = lax.broadcasted_iota(jnp.int32, (SLOTS, SLOTS), 1)
    owner_row = owner_ref[...].astype(F32)
    owner_col = jnp.sum(jnp.where(sub == lane, owner_row, 0.0), axis=1, keepdims=True)
    same = owner_row == owner_col
    rank_row = jnp.sum(jnp.where(same & (sub < lane), 1.0, 0.0), axis=0, keepdims=True)
    rank_col = jnp.sum(jnp.where(same & (lane < sub), 1.0, 0.0), axis=1, keepdims=True)
    place = (owner_row * CAP + rank_row).astype(jnp.int32)
    pick = lax.broadcasted_iota(jnp.int32, (8 * CAP, SLOTS), 0) == place
    pick = jnp.where(pick, 1.0, 0.0).astype(BF16)
    slot = lax.broadcasted_iota(jnp.int32, (SLOTS, L), 0)
    for copy in copies:
        copy.wait()
    weights = jnp.where(slot < counts_ref[0], weight_ref[...], 0.0)
    parts = halves(weights * departures_ref[...]) + halves(weights)
    data = jnp.concatenate(parts, axis=1)
    number = lax.broadcasted_iota(jnp.int32, (1, SLOTS), 1)
    time = (number - STEPS * ((number * 171) >> 9)).astype(F32)
    tile = lax.broadcasted_iota(jnp.int32, (8, SLOTS), 0).astype(F32)
    here = tile == owner_row
    marks = jnp.concatenate(
        [jnp.where(here, time, 0.0), jnp.where(here, columns_ref[...].astype(F32), 0.0)], axis=0
    )
    target = rank_col + (CAP * parity_ref[0]).astype(F32)
    spread = jnp.where(lax.broadcasted_iota(jnp.int32, (SLOTS, L), 1).astype(F32) == target, 1.0, 0.0)
    codes = dot(marks.astype(BF16), spread.astype(BF16))
    codes = CELLS * codes[:8] + codes[8:]
    sends = []
    for j in range(4):
        moved = dot(pick[2 * j * CAP : 2 * (j + 1) * CAP], data)
        forcing = moved[:, :L] + moved[:, L : 2 * L]
        weights = moved[:, 2 * L : 3 * L] + moved[:, 3 * L :]
        for k in range(2):
            d, rows = 2 * j + k, slice(k * CAP, (k + 1) * CAP)
            out_ref[d, :CAP] = forcing[rows]
            out_ref[d, CAP : 2 * CAP] = weights[rows]
            out_ref[d, 2 * CAP :] = jnp.broadcast_to(codes[d : d + 1], (8, L))
            sends.append(pltpu.make_async_copy(out_ref.at[d], out_hbm.at[d], sems.at[2 + d]))
            sends[-1].start()
    for copy in sends:
        copy.wait()


def fixed_kernel(std_ref, diffusion_ref, out_ref):
    out_ref[:CELLS] = std_ref[...]
    sub = lax.broadcasted_iota(jnp.int32, (COLS, COLS), 0)
    lane = lax.broadcasted_iota(jnp.int32, (COLS, COLS), 1)
    place = lax.broadcasted_iota(jnp.int32, (COLS, L), 1)
    turned = jnp.zeros((COLS, L), F32)
    for r in range(ROWS):
        row = diffusion_ref[r : r + 1]
        column = jnp.sum(jnp.where(sub == lane, row, 0.0), axis=1, keepdims=True)
        turned = turned + jnp.where(place == r, column, 0.0)
    out_ref[CELLS:] = turned


SIZE = STEPS * CELLS
PACKED = SIZE + STEPS * ROWS * EDGE


def tile_kernel(received_ref, fixed_ref, m_ref, own_ref, to_left_ref, to_right_ref):
    ones, data = [], []
    cell = lax.broadcasted_iota(jnp.int32, (SIZE, L), 0)
    for j in range(4):
        pair = (2 * j, 2 * j + 1)
        codes = sum(received_ref[s, 2 * CAP : 2 * CAP + 1] for s in pair).astype(jnp.int32)
        ones.append(jnp.where(cell == codes, 1.0, 0.0).astype(BF16))
        for s in pair:
            parts = halves(received_ref[s, :CAP]) + halves(received_ref[s, CAP : 2 * CAP])
            data.append(jnp.concatenate(parts, axis=1))
    total = dot(jnp.concatenate(ones, axis=1), jnp.concatenate(data, axis=0))
    forcing = total[:, :L] + total[:, L : 2 * L]
    weights = total[:, 2 * L : 3 * L] + total[:, 3 * L :]
    for ref in (own_ref, to_left_ref, to_right_ref):
        ref[:SIZE] = forcing
    own_ref[SIZE:] = weights
    for k in range(STEPS * ROWS):
        to = pl.ds(SIZE + k * EDGE, EDGE)
        to_left_ref[to] = weights[k * COLS : k * COLS + EDGE]
        to_right_ref[to] = weights[k * COLS + EDGE : (k + 1) * COLS]
    for r in range(ROWS):
        first = (STEPS - 1) * CELLS + r * COLS
        to_left_ref[PACKED + r : PACKED + r + 1] = weights[first + EDGE : first + EDGE + 1]
        to_right_ref[PACKED + r : PACKED + r + 1] = weights[first + EDGE - 1 : first + EDGE]


def wide(refs, start):
    return jnp.concatenate([ref[start : start + COLS] for ref in refs], axis=0)


class Tile:
    def __init__(self, left_ref, own_ref, right_ref, fixed_left_ref, fixed_ref, fixed_right_ref):
        self.left, self.own, self.right = left_ref, own_ref, right_ref
        self.fixed = (fixed_left_ref, fixed_ref, fixed_right_ref)

    def forcing(self, t, r):
        return wide((self.left, self.own, self.right), t * CELLS + r * COLS)

    def inner_weights(self, t, r):
        start = SIZE + t * CELLS + r * COLS
        packed = pl.ds(SIZE + (t * ROWS + r) * EDGE, EDGE)
        return [self.left[packed], self.own[start : start + COLS], self.right[packed]]

    def weights(self, t, r):
        inner = self.inner_weights(t, r)
        if t < STEPS - 1:
            edges = [jnp.zeros((EDGE, L), F32)] * 2
        else:
            edges = [jnp.broadcast_to(ref[PACKED + r : PACKED + r + 1], (EDGE, L)) for ref in (self.left, self.right)]
        return jnp.concatenate([edges[0], *inner, edges[1]], axis=0)

    def std(self, r):
        return wide(self.fixed, r * COLS)

    def turned(self):
        return wide(self.fixed, CELLS)


def inside(row):
    return row[EDGE : EDGE + INNER]


def padded(row):
    if row.shape[0] == WIDE:
        return row
    edge = jnp.zeros((EDGE, L), F32)
    return jnp.concatenate([edge, row, edge], axis=0)


def places(rows):
    found, total = {}, 0
    for kind, h, width in rows:
        found[kind, h] = (total, width)
        total += width
    return found, total


FIRST, FIRST_ROWS = places(
    [(("f", t), h, WIDE if h < t + 2 else INNER) for t in range(STEPS) for h in range(1, t + 3)]
    + [("std", h, INNER) for h in range(1, STEPS + 1)]
    + [("diffusion", 1, WIDE)]
)
SECOND, SECOND_ROWS = places(
    [("state", h, WIDE if h <= STEPS else INNER) for h in range(1, REACH + 1)]
    + [("b", h, INNER) for h in range(1, STEPS + 1)]
)
WEIGHTS, WEIGHTS_ROWS = places([(("w", t), h, INNER) for t in range(STEPS) for h in range(1, t + 5)])
THIRD, THIRD_ROWS = places([(("g", t), h, INNER) for t in range(STEPS) for h in range(1, t + 2)])


class Sides:
    def __init__(self, parity_ref, chip_ref, core_ref, found):
        self.even = parity_ref[0] == 0
        self.core_ref, self.chip_ref, self.found = core_ref, chip_ref, found

    def send(self, kind, h, row):
        start, width = self.found[kind, h]
        values = [row(r) for r in (h - 1, ROWS - h)]
        low, high = [inside(v) if width < v.shape[0] else v for v in values]
        self.core_ref[start : start + width] = jnp.where(self.even, high, low)
        self.chip_ref[start : start + width] = jnp.where(self.even, low, high)

    def taken(self, kind, r):
        start, width = self.found[kind, -r if r < 0 else r - ROWS + 1]
        core, chip = self.core_ref[start : start + width], self.chip_ref[start : start + width]
        return jnp.where(self.even, chip, core) if r < 0 else jnp.where(self.even, core, chip)


def sides_kernel(*refs):
    tile, sides = Tile(*refs[1:7]), Sides(refs[0], *refs[7:], FIRST)
    for kind, h in FIRST:
        if kind == "std":
            row = tile.std
        elif kind == "diffusion":
            row = lambda r: tile.turned()
        else:
            row = lambda r: tile.forcing(kind[1], r)
        sides.send(kind, h, row)


def weights_kernel(*refs):
    tile, sides = Tile(*refs[1:7]), Sides(refs[0], *refs[7:], WEIGHTS)
    for kind, h in WEIGHTS:
        sides.send(kind, h, lambda r: jnp.concatenate(tile.inner_weights(kind[1], r), axis=0))


def own(r):
    return 0 <= r < ROWS


class Field:
    def __init__(self, width, reach, v_ref, x_ref, y_ref, d_ref, m_ref):
        self.width, self.reach = width, reach
        self.v_ref, self.x_ref, self.y_ref, self.d_ref, self.m_ref = v_ref, x_ref, y_ref, d_ref, m_ref

    def at(self, r):
        return pl.ds((r + self.reach) * self.width, self.width)

    def put(self, r, value):
        self.v_ref[self.at(r)] = value
        high, low = halves(value)
        self.x_ref[self.at(r), :L] = high
        self.x_ref[self.at(r), L:] = low

    def mix(self, first, stop, which):
        rows = pl.ds((first + self.reach) * self.width, (stop - first) * self.width)
        self.y_ref[rows] = dot(self.x_ref[rows], self.m_ref[which])

    def get(self, r):
        return self.v_ref[self.at(r)] + self.y_ref[self.at(r), :L] + self.y_ref[self.at(r), L:]

    def fill_diffusion(self, tile, sides, reach):
        values = {0: tile.turned(), -1: sides.taken("diffusion", -1), 1: sides.taken("diffusion", ROWS)}
        skip = (WIDE - self.width) // 2
        for r in range(-reach, ROWS + reach):
            column = values[r // ROWS][skip : skip + self.width, r % ROWS : r % ROWS + 1]
            self.d_ref[self.at(r)] = jnp.broadcast_to(column, (self.width, L))

    def smooth(self, first, stop, get, put, scaled=False):
        held = []
        for r in range(first, stop):
            value = get(r)
            if scaled and r in (first, stop - 1):
                held.append((value, None, value))
            else:
                d = self.d_ref[self.at(r)]
                held.append((value, d, d * value))
            if len(held) == 3:
                value, d, u = held[1]
                around = held[0][2] + held[2][2] + pltpu.roll(u, 1, 0) + pltpu.roll(u, self.width - 1, 0)
                put(r - 1, value + d * (around - 4.0 * u))
                held.pop(0)

    def forward(self, h, start, seen, scaled=False):
        self.smooth(-h, ROWS + h, start, self.put, scaled)
        for t in range(STEPS):
            first, stop = -h + t + 1, ROWS + h - t - 1
            self.mix(first, stop, MIX)

            def get(r, t=t):
                value = self.get(r)
                seen(t, r, value)
                return value

            if t < STEPS - 1:
                self.smooth(first, stop, get, self.put)
            else:
                for r in range(first, stop):
                    get(r)

    def adjoint(self, h, forcing, std, last=None):
        for t in range(STEPS - 1, -1, -1):
            first, stop = -h - t - 1, ROWS + h + t + 1
            self.mix(first, stop, MIX_T)
            if t > 0:
                put = lambda r, value, t=t: self.put(r, value + forcing(t - 1, r))
            elif last is None:
                put = lambda r, value: self.put(r, std(r) * value)
            else:
                put = lambda r, value: last.put(r, std(r) * inside(value))
            self.smooth(first, stop, self.get, put)
        (last or self).mix(-h, ROWS + h, FACTOR_T)


def scratch(width, reach):
    tall = (ROWS + 2 * reach) * width
    return [
        pltpu.VMEM((tall, L), F32),
        pltpu.VMEM((tall, 2 * L), BF16),
        pltpu.VMEM((tall, 2 * L), F32),
        pltpu.VMEM((tall, L), F32),
    ]


def std_rows(tile, sides):
    return lambda r: tile.std(r) if own(r) else padded(sides.taken("std", r))


def right_side_kernel(parity_ref, *refs):
    tile, sides, m_ref = Tile(*refs[:6]), Sides(parity_ref, *refs[6:8], FIRST), refs[8]
    b_ref, y_ref = refs[9:11]
    out = Sides(parity_ref, *refs[11:13], SECOND)
    field = Field(WIDE, STEPS + 1, *refs[13:17], m_ref)
    field.fill_diffusion(tile, sides, STEPS + 1)
    forcing = lambda t, r: tile.forcing(t, r) if own(r) else padded(sides.taken(("f", t), r))
    std = std_rows(tile, sides)
    for r in range(-STEPS - 1, ROWS + STEPS + 1):
        field.put(r, forcing(STEPS - 1, r))
    field.adjoint(1, forcing, std)
    for r in range(-1, ROWS + 1):
        value = field.get(r)
        field.put(r, value)
        if own(r):
            b_ref[r] = value
    field.mix(-1, ROWS + 1, FACTOR)
    beyond = {}
    for r in range(-1, ROWS + 1):
        state = std(r) * field.get(r)
        if own(r):
            y_ref[r] = state
        else:
            beyond[r] = field.d_ref[field.at(r)] * state
    for kind, h in SECOND:
        out.send(kind, h, lambda r: b_ref[r] if kind == "b" else y_ref[r] if own(r) else beyond[r])


MIDDLE = slice(COLS, 2 * COLS)


def first_image_kernel(parity_ref, *refs):
    tile, sides, m_ref = Tile(*refs[:6]), Sides(parity_ref, *refs[6:8], FIRST), refs[8]
    b_ref, y_ref = refs[9:11]
    more, forced = Sides(parity_ref, *refs[11:13], SECOND), Sides(parity_ref, *refs[13:15], WEIGHTS)
    q_ref, g_ref = refs[15:17]
    out, sums_ref = Sides(parity_ref, *refs[17:19], THIRD), refs[19]
    field = Field(WIDE, REACH, *refs[20:24], m_ref)
    tops = refs[24:26]
    inner = Field(INNER, STEPS, *refs[26:30], m_ref)
    field.fill_diffusion(tile, sides, REACH - 1)
    for r in range(-STEPS, ROWS + STEPS):
        inner.d_ref[inner.at(r)] = inside(field.d_ref[field.at(r)])
    wide_std = std_rows(tile, sides)
    std = lambda r: inside(wide_std(r))

    def weights(t, r):
        return tile.weights(t, r) if own(r) else padded(forced.taken(("w", t), r))

    def start(r):
        if own(r):
            return y_ref[r]
        return padded(more.taken("state", r))

    def force(t, r, value):
        if -t - 4 <= r < ROWS + t + 4:
            if t < STEPS - 1:
                tops[t][field.at(r)] = weights(t, r) * value
            else:
                field.put(r, weights(t, r) * value)

    field.forward(REACH, start, force, scaled=True)
    field.adjoint(STEPS, lambda t, r: tops[t][field.at(r)], std, inner)
    sums = [jnp.zeros((COLS, L), F32) for _ in range(4)]
    for r in range(-STEPS, ROWS + STEPS):
        b = inside(b_ref[r]) if own(r) else more.taken("b", r)
        q = b + inner.get(r)
        inner.put(r, q)
        if own(r):
            b, q = b[EDGE : EDGE + COLS], q[EDGE : EDGE + COLS]
            q_ref[r] = q
            for i, term in enumerate((b * b, b * q, q * q, q * q)):
                sums[i] = sums[i] + term
    inner.mix(-STEPS, ROWS + STEPS, FACTOR)

    def keep(t, r, value):
        if own(r):
            forcing = jnp.concatenate(tile.inner_weights(t, r), axis=0) * value
            sums[3] = sums[3] + forcing[EDGE : EDGE + COLS] * value[EDGE : EDGE + COLS]
            g_ref[t, r] = forcing

    inner.forward(STEPS, lambda r: std(r) * inner.get(r), keep)
    for kind, h in THIRD:
        out.send(kind, h, lambda r: g_ref[kind[1], r])
    lane = lax.broadcasted_iota(jnp.int32, (1, L), 1)
    row = jnp.zeros((1, L), F32)
    for i, term in enumerate(sums):
        total = jnp.sum(jnp.sum(term, axis=0, keepdims=True), axis=1, keepdims=True)
        row = row + jnp.where(lane == i, total, 0.0)
    sums_ref[...] = jnp.broadcast_to(row, sums_ref.shape)


def second_image_kernel(parity_ref, *refs):
    tile, sides, m_ref = Tile(*refs[:6]), Sides(parity_ref, *refs[6:8], FIRST), refs[8]
    q_ref, g_ref = refs[9:11]
    more = Sides(parity_ref, *refs[11:13], THIRD)
    u_ref = refs[13]
    field = Field(INNER, STEPS, *refs[14:18], m_ref)
    field.fill_diffusion(tile, sides, STEPS)
    forcing = lambda t, r: g_ref[t, r] if own(r) else more.taken(("g", t), r)
    for r in range(-STEPS, ROWS + STEPS):
        field.put(r, forcing(STEPS - 1, r))
    field.adjoint(0, forcing, lambda r: inside(tile.std(r)))
    for r in range(ROWS):
        u_ref[r] = q_ref[r] + field.get(r)[EDGE : EDGE + COLS]


def levels(lat, lon):
    quarter = lat // 4
    near = [[i * quarter + k for k in range(quarter)] for i in range(4)]
    far = [[(i * quarter + k) * lon + j for i in range(4) for j in range(lon)] for k in range(quarter)]
    return near, far


def add_kernel(parts_ref, out_ref):
    out_ref[...] = jnp.broadcast_to(0.25 * jnp.sum(parts_ref[...], axis=0, keepdims=True), out_ref.shape)


def finish_kernel(parts_ref, b_ref, q_ref, u_ref, solution_ref, residual_ref):
    total = jnp.sum(parts_ref[...], axis=0, keepdims=True)
    bb, bq, qq, qu = (total[:, i : i + 1] for i in range(4))
    first = bb / bq
    norm = first * first * qq - bb
    gain = 1.0 + norm / bb
    curve = gain * gain * bq - 2.0 * first * gain * qq + first * first * qu
    second = norm / curve
    along_b = first + second * gain
    along_q = first * second
    for r in range(ROWS):
        b, q = b_ref[r, MIDDLE], q_ref[r]
        solution_ref[r] = along_b * b - along_q * q
        residual_ref[r] = b - along_b * q + along_q * u_ref[r]


def exchange(to_before, to_after):
    size = lax.axis_size("lon")
    up = [(i, (i + 1) % size) for i in range(size)]
    down = [(j, i) for i, j in up]
    return lax.ppermute(to_after, "lon", up), lax.ppermute(to_before, "lon", down)


def swap(chip, core):
    size = lax.axis_size("lat")
    pairs = [[(i, i + 1) for i in range(first, size - 1, 2)] for first in (0, 1)]
    both = [p + [(j, i) for i, j in p] for p in pairs]
    return lax.ppermute(chip, "lat", both[1]), lax.ppermute(core, "lat", both[0])


def shards(
    departures, obs_weight, obs_columns, obs_owner, obs_counts, background_std, diffusion, level_factor, model_mixing
):
    parity = (lax.axis_index("lon") % 2).astype(jnp.int32).reshape(1)
    side_of = (lax.axis_index("lat") % 2).astype(jnp.int32).reshape(1)
    slots = pltpu.VMEM((SLOTS, L), F32)
    buckets = call(
        bucket_kernel,
        "bucket",
        shape(8, BUCKET, L),
        [slots, slots, pltpu.VMEM((8, BUCKET, L), F32), pltpu.SemaphoreType.DMA((10,))],
        smem=(4, 5),
        hbm=(0, 1),
        vmem=60,
        out_space=pltpu.HBM,
    )(departures, obs_weight, obs_columns.reshape(1, SLOTS), obs_owner.reshape(1, SLOTS), obs_counts, parity)
    received = lax.all_to_all(buckets, "lon", 0, 0)
    mats = call(matrices_kernel, "matrices", shape(4, 2 * L, 2 * L, dtype=BF16))(level_factor, model_mixing)
    fixed = call(fixed_kernel, "fixed", shape(CELLS + COLS, L))(background_std.reshape(CELLS, L), diffusion)
    fixed_left, fixed_right = exchange(fixed, fixed)
    beside = shape(PACKED + ROWS, L)
    tile, to_left, to_right = call(tile_kernel, "tile", (shape(2 * SIZE, L), beside, beside))(
        received, fixed, mats
    )
    left, right = exchange(to_left, to_right)
    refs = (left, tile, right, fixed_left, fixed, fixed_right)
    side = shape(FIRST_ROWS, L)
    below, above = swap(*call(sides_kernel, "sides", (side, side), smem=(0,))(side_of, *refs))
    side = shape(WEIGHTS_ROWS, L)
    weights = swap(*call(weights_kernel, "weights", (side, side), smem=(0,))(side_of, *refs))
    refs = (*refs, below, above, mats)
    field, side = shape(ROWS, WIDE, L), shape(SECOND_ROWS, L)
    b, y, low, high = call(right_side_kernel, "right_side", (field, field, side, side), scratch(WIDE, STEPS + 1), smem=(0,))(
        side_of, *refs
    )
    south, north = swap(low, high)
    lat, lon = lax.axis_size("lat"), lax.axis_size("lon")
    near, far = levels(lat, lon)
    small, side = shape(ROWS, COLS, L), shape(THIRD_ROWS, L)
    space = scratch(WIDE, REACH)
    q, g, low, high, sums = call(
        first_image_kernel,
        "first_image",
        (small, shape(STEPS, ROWS, INNER, L), side, side, shape(lat, L)),
        space + [space[0]] * 2 + scratch(INNER, STEPS),
        smem=(0,),
    )(side_of, *refs, b, y, south, north, *weights)
    sums = lax.all_to_all(sums, "lat", 0, 0, axis_index_groups=near, tiled=True)
    south, north = swap(low, high)
    u = call(second_image_kernel, "second_image", small, scratch(INNER, STEPS), smem=(0,))(
        side_of, *refs, q, g, south, north
    )
    sums = call(add_kernel, "add", shape(4 * lon, L))(sums)
    sums = lax.all_to_all(sums, ("lat", "lon"), 0, 0, axis_index_groups=far, tiled=True)
    return call(finish_kernel, "finish", (small, small))(sums, b, q, u)


def solution(mesh):
    placed = (
        P(("lat", "lon"), None),
        P(("lat", "lon"), None),
        P(("lat", "lon")),
        P(("lat", "lon"), None),
        P(("lat", "lon")),
        P("lat", "lon", None),
        P("lat", "lon"),
        P(),
        P(),
    )
    return jax.shard_map(
        shards,
        mesh=mesh,
        in_specs=placed,
        out_specs=(P("lat", "lon", None), P("lat", "lon", None)),
        check_vma=False,
    )
```
